32 devices in a mesh: groups: 2 (over y), dp: 16 (over z, x, core), tensor: 1.
Axes of the slice: x: 2, y: 2, z: 4, core: 2. Of those that a mesh axis runs over, the one named last changes fastest.
Arguments:
- hidden_acts: bfloat16 [16384, 14336], P(('groups', 'dp'), 'tensor'), parts along dimension 0, may hold values from -6 to 6
- output_grads: bfloat16 [16384, 8192], P(('groups', 'dp'), 'tensor'), parts along dimension 0, may hold values from -6 to 6
- query_left: bfloat16 [64, 16, 14336], P('dp', None, 'tensor'), may hold values from -0.005859375 to 0.005859375
- query_right: bfloat16 [64, 16, 8192], P('dp', None, 'tensor'), may hold values from -0.0078125 to 0.0078125
- bucket_ids: int32 [128], P(('groups', 'dp')), parts along dimension 0, may hold values from 0 to 3, as said below
- seq_lengths: int32 [128], P(('groups', 'dp')), parts along dimension 0, may hold values from 0 to 512, as said below
Outputs:
- scores: float32 [64, 128], P('tensor', ('groups', 'dp')), parts along dimension 1
The draws below stay inside these ranges and needn't reach their ends.
There are 2 independent parts, one for each index of `groups`. The reference program is written for one: setup_inputs(seed, part) draws one part's arguments, and reference() takes and returns one part's arrays. A program takes and returns all parts, laid end to end along the dimension named above; an argument that names none is the same for every part. Nothing has to cross between parts.
Inputs may be any that keep to these rules, and one draw needn't show every extreme that they name: `bucket_ids`: each group of 4 slots lists its used buckets first and empty slots (id 3) last; their bucket lengths sum to at most 512. `seq_lengths`: A slot of bucket 0 has length 1 to 128; of bucket 1 or 2, more than half of its bucket length and at most all of it; an empty slot has length 0.
All inputs are finite; a program needn't handle non-finite values.
Results may differ from the reference program's by a relative error of at most 0.0003.
Values may be sent and summed in bfloat16 or wider, within the bound.
No kernel may reach another device: no remote copies, remote signals or barrier semaphores. Data moves between devices by JAX's collectives and lax.ppermute only.
A program may use at most 128 MiB of HBM per device.

```python
import jax
import jax.numpy as jnp
from jax import lax

D = 8192
FFW = 14336
Q = 64
R = 16
BUCKET = 128
S_DEV = 4
TOK_DEV = 512
TOKENS = 8192
SEQS = 64


def bucket_layout(key):
    key = jax.random.fold_in(key, 11)
    layouts = jnp.array([[2, 3, 3, 3], [1, 1, 3, 3], [1, 0, 0, 3], [0, 0, 0, 0], [0, 1, 3, 3]], jnp.int32)
    devices = SEQS // S_DEV
    chosen = jax.random.randint(key, (devices,), 0, 5)
    chosen = chosen.at[0].set(0).at[1].set(3)
    slot_ids = layouts[chosen]
    widths = BUCKET * jnp.where(slot_ids == 0, 1, jnp.where(slot_ids == 1, 2, jnp.where(slot_ids == 2, 4, 0))).astype(jnp.int32)
    lowest = jnp.where(slot_ids == 0, 1, widths // 2 + 1)
    highest = jnp.maximum(widths + 1, lowest + 1)
    lengths = jax.random.randint(jax.random.fold_in(key, 1), slot_ids.shape, lowest, highest)
    lengths = jnp.where(slot_ids == 3, 0, lengths).astype(jnp.int32)
    lengths = lengths.at[0, 0].set(4 * BUCKET)
    return (slot_ids.reshape(-1), lengths.reshape(-1))


def draw_bucket_ids(key, part):
    return bucket_layout(key)[0]


def draw_seq_lengths(key, part):
    return bucket_layout(key)[1]


def block_scale(key, dims, shards, smallest, largest):
    loudness, own = 1.0, jax.random.fold_in(key, 6)
    for position, shards_of in shards:
        steps = jnp.exp(jax.random.uniform(jax.random.fold_in(own, position), (shards_of,), jnp.float32, smallest / len(shards), largest / len(shards)))
        loudness = loudness * jnp.repeat(steps, dims[position] // shards_of).reshape([-1 if axis == position else 1 for axis in range(len(dims))])
    return loudness


def normal_values(key, extent, spread, most, cuts=(), kind=jnp.bfloat16):
    values = jax.random.normal(key, extent, jnp.float32) * spread
    if len(cuts) > 0:
        values = block_scale(key, extent, cuts, -0.22, 0.18) * values
    return jnp.clip(values, min=-most, max=most).astype(kind)


def setup_inputs(seed: int = 0, part: int = 0) -> dict:
    keys = jax.random.split(jax.random.key(seed), 7)
    part_keys = jax.random.split(jax.random.fold_in(keys[6], part), 7)
    hidden_acts = normal_values(part_keys[0], (TOKENS, FFW), 1.0, 6.0, ((0, 16),))
    output_grads = normal_values(part_keys[1], (TOKENS, D), 1.0, 6.0, ((0, 16),))
    query_left = normal_values(keys[2], (Q, R, FFW), (FFW * 64) ** -0.5, 0.005859375, ((0, 16),))
    query_right = normal_values(keys[3], (Q, R, D), (D * 64) ** -0.5, 0.0078125, ((0, 16),))
    bucket_ids = draw_bucket_ids(jax.random.fold_in(jax.random.fold_in(keys[6], part), 71), part)
    seq_lengths = draw_seq_lengths(jax.random.fold_in(jax.random.fold_in(keys[6], part), 71), part)
    return dict(hidden_acts=hidden_acts, output_grads=output_grads, query_left=query_left, query_right=query_right, bucket_ids=bucket_ids, seq_lengths=seq_lengths)


def bucket_lengths(slot_ids):
    return BUCKET * jnp.where(slot_ids == 0, 1, jnp.where(slot_ids == 1, 2, jnp.where(slot_ids == 2, 4, 0))).astype(jnp.int32)


def slot_matrix(slot_ids, lengths, positions):
    widths = bucket_lengths(slot_ids)
    starts = (jnp.cumsum(widths) - widths).astype(jnp.int32)
    place = jnp.arange(positions, dtype=jnp.int32)[:, None]
    inside = (place >= starts[None, :]) & (place < starts[None, :] + lengths[None, :])
    return inside.astype(jnp.float32)


def reference(hidden_acts, output_grads, query_left, query_right, bucket_ids, seq_lengths):
    left_rows = query_left.reshape(Q * R, FFW)
    right_rows = query_right.reshape(Q * R, D)
    devices = hidden_acts.shape[0] // TOK_DEV
    hidden_blocks = hidden_acts.reshape(devices, TOK_DEV, FFW)
    grad_blocks = output_grads.reshape(devices, TOK_DEV, D)
    slot_blocks = bucket_ids.reshape(devices, S_DEV)
    length_blocks = seq_lengths.reshape(devices, S_DEV)

    def score_device(pieces):
        hidden_here, grads_here, slots_here, lengths_here = pieces
        left_proj = jnp.dot(hidden_here, left_rows.T, preferred_element_type=jnp.float32)
        right_proj = jnp.dot(grads_here, right_rows.T, preferred_element_type=jnp.float32)
        token_term = jnp.sum((left_proj * right_proj).reshape(TOK_DEV, Q, R), axis=2)
        slot_mask = slot_matrix(slots_here, lengths_here, TOK_DEV)
        return jnp.dot(token_term.T, slot_mask, precision=lax.Precision.HIGHEST, preferred_element_type=jnp.float32)

    per_device = lax.map(score_device, (hidden_blocks, grad_blocks, slot_blocks, length_blocks))
    return jnp.transpose(per_device, (1, 0, 2)).reshape(Q, devices * S_DEV)
```

```python
import functools

import jax
import jax.numpy as jnp
from jax import lax
from jax.experimental import pallas as pl
from jax.experimental.pallas import tpu as pltpu
from jax.sharding import PartitionSpec as P

BUCKET = 128


def bucket_lengths(slot_ids):
    return BUCKET * jnp.where(
        slot_ids == 0, 1, jnp.where(slot_ids == 1, 2, jnp.where(slot_ids == 2, 4, 0))
    ).astype(jnp.int32)


def slot_matrix(slot_ids, lengths, positions):
    widths = bucket_lengths(slot_ids)
    starts = jnp.cumsum(widths) - widths
    place = jnp.arange(positions, dtype=jnp.int32)[:, None]
    inside = (place >= starts[None, :]) & (place < starts[None, :] + lengths[None, :])
    return inside.astype(jnp.float32)


def project(acts, factors):
    rows = factors.reshape(-1, factors.shape[2])
    return lax.dot_general(acts, rows, (((1,), (1,)), ((), ())), preferred_element_type=jnp.float32)


def gather_whole(hidden_acts, output_grads, query_left, query_right, bucket_ids, seq_lengths):
    tokens_here = hidden_acts.shape[0]
    rank_count = query_left.shape[1]
    left_all, right_all = (
        lax.all_gather(query_left, "dp", axis=0, tiled=True),
        lax.all_gather(query_right, "dp", axis=0, tiled=True),
    )
    left_proj = project(hidden_acts, left_all)
    right_proj = project(output_grads, right_all)
    queries = left_proj.shape[1] // rank_count
    left_terms = left_proj.reshape(tokens_here, queries, rank_count)
    right_terms = right_proj.reshape(tokens_here, queries, rank_count)
    left_terms, right_terms = lax.psum((left_terms, right_terms), "tensor")
    share_size = queries // lax.axis_size("tensor")
    first_query = lax.axis_index("tensor") * share_size
    left_terms = lax.dynamic_slice_in_dim(left_terms, first_query, share_size, 1)
    right_terms = lax.dynamic_slice_in_dim(right_terms, first_query, share_size, 1)
    token_term = jnp.sum(left_terms * right_terms, axis=2)
    slot_mask = slot_matrix(bucket_ids, seq_lengths, tokens_here)
    return jnp.dot(
        token_term.T, slot_mask, precision=lax.Precision.HIGHEST, preferred_element_type=jnp.float32
    )


CORE, COLUMN, NEAR, ACROSS = 1, 2, 4, 12
OPPOSITE = 8
VMEM_LIMIT = 40 * 1024 * 1024


def flip(array, code, count):
    return lax.ppermute(array, "dp", [(i, i ^ code) for i in range(count)])


def swap_groups(array):
    return lax.ppermute(array, "groups", [(0, 1), (1, 0)])


def lines(array, pairs):
    return lax.ppermute(
        array, "dp", [(a * 4 + rest, b * 4 + rest) for a, b in pairs for rest in range(4)]
    )


def proj_kernel(count, first_ref, own_ref, other_ref, *refs):
    del first_ref
    pieces, out_ref = refs[:count], refs[count]
    step = pl.program_id(0)
    rows = own_ref.shape[0]
    factors = jnp.concatenate([p[...] for p in pieces], axis=0)
    dims = (((1,), (1,)), ((), ()))
    top = lax.dot_general(own_ref[...], factors, dims, preferred_element_type=jnp.float32)
    low = lax.dot_general(other_ref[...], factors, dims, preferred_element_type=jnp.float32)

    @pl.when(step == 0)
    def _():
        out_ref[:rows] = top
        out_ref[rows:] = low

    @pl.when(step > 0)
    def _():
        out_ref[:rows] += top
        out_ref[rows:] += low


def proj(own, other, pieces, first, block):
    rows, depth = own.shape[0], pieces[0].shape[1]
    steps = depth // block
    held = sum(p.shape[0] for p in pieces)
    tokens = pl.BlockSpec((rows, block), lambda k, first: (0, first[0] * steps + k))
    return pl.pallas_call(
        functools.partial(proj_kernel, len(pieces)),
        out_shape=jax.ShapeDtypeStruct((2 * rows, held), jnp.float32),
        grid_spec=pltpu.PrefetchScalarGridSpec(
            num_scalar_prefetch=1,
            grid=(steps,),
            in_specs=[tokens, tokens]
            + [pl.BlockSpec((p.shape[0], block), lambda k, first: (0, k)) for p in pieces],
            out_specs=pl.BlockSpec((2 * rows, held), lambda k, first: (0, 0)),
        ),
        compiler_params=pltpu.CompilerParams(vmem_limit_bytes=VMEM_LIMIT),
        cost_estimate=pl.CostEstimate(
            flops=4 * rows * held * depth,
            bytes_accessed=4 * rows * depth + 2 * held * depth + 8 * rows * held,
            transcendentals=0,
        ),
    )(first, own, other, *pieces)


def score_kernel(slots, spans_ref, mine_ref, theirs_ref, right_ref, out_ref):
    rows = mine_ref.shape[0] // 2
    place = lax.broadcasted_iota(jnp.int32, (rows, 1), 0)
    for part in range(2):
        here = slice(part * rows, (part + 1) * rows)
        terms = (mine_ref[here] + theirs_ref[here]) * right_ref[here]
        for j in range(slots):
            k = part * slots + j
            inside = (place >= spans_ref[0, k]) & (place < spans_ref[1, k])
            out_ref[k : k + 1, :] = jnp.sum(
                jnp.where(inside, terms, 0.0), axis=0, keepdims=True
            )


def score(spans, mine, theirs, right):
    slots = spans.shape[1] // 2
    return pl.pallas_call(
        functools.partial(score_kernel, slots),
        out_shape=jax.ShapeDtypeStruct((2 * slots, mine.shape[1]), jnp.float32),
        in_specs=[pl.BlockSpec(memory_space=pltpu.SMEM)]
        + [pl.BlockSpec(memory_space=pltpu.VMEM)] * 3,
        out_specs=pl.BlockSpec(memory_space=pltpu.VMEM),
        compiler_params=pltpu.CompilerParams(vmem_limit_bytes=VMEM_LIMIT),
        cost_estimate=pl.CostEstimate(
            flops=10 * mine.size, bytes_accessed=12 * mine.size, transcendentals=0
        ),
    )(spans, mine, theirs, right)


def spans_of(slot_ids, lengths):
    widths = bucket_lengths(slot_ids)
    starts = jnp.cumsum(widths) - widths
    return jnp.stack([starts, starts + lengths]).astype(jnp.int32)


def relay(hidden_acts, output_grads, query_left, query_right, bucket_ids, seq_lengths):
    count = lax.axis_size("dp")
    me, group = lax.axis_index("dp"), lax.axis_index("groups")
    z = me // 4
    local, ranks = query_left.shape[:2]
    left = query_left.reshape(local * ranks, -1)
    half = left.shape[1] // 2
    send = functools.partial(flip, count=count)

    grads_there = send(output_grads, CORE)
    acts_there = send(hidden_acts, CORE)
    spans_here = spans_of(bucket_ids, seq_lengths)
    spans = jnp.concatenate([spans_here, send(spans_here, CORE)], axis=1)

    a, b, c = {}, {}, {}
    a[0] = lax.dynamic_slice_in_dim(left, group * half, half, 1)
    c[0] = lax.dynamic_slice_in_dim(left, (1 - group) * half, half, 1)
    b[0] = query_right.reshape(local * ranks, -1)

    def along_z(held):
        held[NEAR] = send(held[0], NEAR)
        held[ACROSS] = send(held[0], ACROSS)
        outer = lines(held[ACROSS], [(1, 0), (2, 3)])
        inner = lines(held[NEAR], [(2, 1), (1, 2)])
        held[OPPOSITE] = jnp.where((z == 0) | (z == 3), outer, inner)

    def over_x(held, code):
        held[code | COLUMN] = send(held[code], COLUMN)

    over_x(a, 0)
    along_z(a)
    over_x(b, 0)
    for code in (NEAR, ACROSS, OPPOSITE):
        over_x(a, code)
    along_z(b)
    b[NEAR | COLUMN] = send(b[COLUMN], NEAR)
    for code in (ACROSS, OPPOSITE):
        over_x(b, code)
    order = (COLUMN, NEAR, ACROSS, NEAR | COLUMN, OPPOSITE, ACROSS | COLUMN, OPPOSITE | COLUMN)
    for code in order:
        c[code] = swap_groups(a[code])

    mine = jnp.reshape(group, (1,)).astype(jnp.int32)
    zero = jnp.zeros((1,), jnp.int32)
    groups = (
        (0, COLUMN, NEAR, ACROSS),
        (NEAR | COLUMN, OPPOSITE, ACROSS | COLUMN, OPPOSITE | COLUMN),
    )
    sums = []
    for codes in groups:
        left_mine = proj(hidden_acts, acts_there, [a[k] for k in codes], mine, 1024)
        left_theirs = proj(hidden_acts, acts_there, [c[k] for k in codes], 1 - mine, 1024)
        right = proj(output_grads, grads_there, [b[k] for k in codes], zero, 1024)
        sums.append(score(spans, left_mine, left_theirs, right))

    slots = bucket_ids.shape[0]
    table = jnp.concatenate(sums, axis=1)
    table = jnp.sum(table.reshape(2 * slots, -1, ranks), axis=2).T.reshape(-1, local, 2 * slots)
    ours, others = table[..., :slots], table[..., slots:]
    others = send(others, CORE)
    place = {code: k for k, code in enumerate(groups[0] + groups[1])}
    rows = jnp.stack(
        [others[place[k & ~CORE]] if k & CORE else ours[place[k]] for k in range(count)]
    )
    for bit in (1, 2, 4, 8):
        paired = rows.reshape(-1, 2, bit, local, slots)
        rows = jnp.where((me & bit) != 0, paired[:, ::-1], paired).reshape(rows.shape)
    return rows.reshape(count * local, slots)


def solution(mesh):
    sizes = mesh.shape
    fits = sizes["dp"] == 16 and sizes["groups"] == 2 and sizes["tensor"] == 1
    return jax.shard_map(
        relay if fits else gather_whole,
        mesh=mesh,
        in_specs=(
            P(("groups", "dp"), "tensor"),
            P(("groups", "dp"), "tensor"),
            P("dp", None, "tensor"),
            P("dp", None, "tensor"),
            P(("groups", "dp")),
            P(("groups", "dp")),
        ),
        out_specs=P("tensor", ("groups", "dp")),
        check_vma=False,
    )
```

```python
import functools

import jax
import jax.numpy as jnp
from jax import lax
from jax.experimental import pallas as pl
from jax.experimental.pallas import tpu as pltpu
from jax.sharding import PartitionSpec as P

BUCKET = 128


def bucket_lengths(slot_ids):
    return BUCKET * jnp.where(
        slot_ids == 0, 1, jnp.where(slot_ids == 1, 2, jnp.where(slot_ids == 2, 4, 0))
    ).astype(jnp.int32)


def slot_matrix(slot_ids, lengths, positions):
    widths = bucket_lengths(slot_ids)
    starts = jnp.cumsum(widths) - widths
    place = jnp.arange(positions, dtype=jnp.int32)[:, None]
    inside = (place >= starts[None, :]) & (place < starts[None, :] + lengths[None, :])
    return inside.astype(jnp.float32)


def project(acts, factors):
    rows = factors.reshape(-1, factors.shape[2])
    return lax.dot_general(acts, rows, (((1,), (1,)), ((), ())), preferred_element_type=jnp.float32)


def gather_whole(hidden_acts, output_grads, query_left, query_right, bucket_ids, seq_lengths):
    tokens_here = hidden_acts.shape[0]
    rank_count = query_left.shape[1]
    left_all, right_all = (
        lax.all_gather(query_left, "dp", axis=0, tiled=True),
        lax.all_gather(query_right, "dp", axis=0, tiled=True),
    )
    left_proj = project(hidden_acts, left_all)
    right_proj = project(output_grads, right_all)
    queries = left_proj.shape[1] // rank_count
    left_terms = left_proj.reshape(tokens_here, queries, rank_count)
    right_terms = right_proj.reshape(tokens_here, queries, rank_count)
    left_terms, right_terms = lax.psum((left_terms, right_terms), "tensor")
    share_size = queries // lax.axis_size("tensor")
    first_query = lax.axis_index("tensor") * share_size
    left_terms = lax.dynamic_slice_in_dim(left_terms, first_query, share_size, 1)
    right_terms = lax.dynamic_slice_in_dim(right_terms, first_query, share_size, 1)
    token_term = jnp.sum(left_terms * right_terms, axis=2)
    slot_mask = slot_matrix(bucket_ids, seq_lengths, tokens_here)
    return jnp.dot(
        token_term.T, slot_mask, precision=lax.Precision.HIGHEST, preferred_element_type=jnp.float32
    )


CORE, COLUMN, NEAR, ACROSS = 1, 2, 4, 12
OPPOSITE = 8
LITTLE = pl.CostEstimate(flops=1, bytes_accessed=1, transcendentals=0)
VMEM_LIMIT = 40 * 1024 * 1024


def flip(array, code, count):
    return lax.ppermute(array, "dp", [(i, i ^ code) for i in range(count)])


def swap_groups(array):
    return lax.ppermute(array, "groups", [(0, 1), (1, 0)])


def after_kernel(count, *refs):
    refs[-1][0] = refs[count][0]


def after(turn, arrays):
    count = len(arrays)
    anywhere = pl.BlockSpec(memory_space=pl.ANY)
    scalar = pl.BlockSpec(memory_space=pltpu.SMEM)
    *arrays, turn = pl.pallas_call(
        functools.partial(after_kernel, count),
        out_shape=[jax.ShapeDtypeStruct(x.shape, x.dtype) for x in (*arrays, turn)],
        in_specs=[anywhere] * count + [scalar],
        out_specs=[anywhere] * count + [scalar],
        input_output_aliases={i: i for i in range(count)},
        cost_estimate=LITTLE,
    )(*arrays, turn)
    return turn, arrays


def lines(array, pairs):
    return lax.ppermute(
        array, "dp", [(a * 4 + rest, b * 4 + rest) for a, b in pairs for rest in range(4)]
    )


def proj_kernel(count, turn_ref, own_ref, other_ref, *refs):
    pieces, (out_ref, next_ref) = refs[:count], refs[count:]
    step = pl.program_id(0)
    rows = own_ref.shape[0]
    factors = jnp.concatenate([p[...] for p in pieces], axis=0)
    dims = (((1,), (1,)), ((), ()))
    top = lax.dot_general(own_ref[...], factors, dims, preferred_element_type=jnp.float32)
    low = lax.dot_general(other_ref[...], factors, dims, preferred_element_type=jnp.float32)

    @pl.when(step == 0)
    def _():
        next_ref[0] = turn_ref[0]
        out_ref[:rows] = top
        out_ref[rows:] = low

    @pl.when(step > 0)
    def _():
        out_ref[:rows] += top
        out_ref[rows:] += low


def proj(turn, own, other, pieces, first, block):
    rows, depth = own.shape[0], pieces[0].shape[1]
    steps = depth // block
    held = sum(p.shape[0] for p in pieces)
    tokens = pl.BlockSpec((rows, block), lambda k, turn: (0, turn[1] * steps + k))
    out, turn_next = pl.pallas_call(
        functools.partial(proj_kernel, len(pieces)),
        out_shape=(
            jax.ShapeDtypeStruct((2 * rows, held), jnp.float32),
            jax.ShapeDtypeStruct((1,), jnp.int32),
        ),
        grid_spec=pltpu.PrefetchScalarGridSpec(
            num_scalar_prefetch=1,
            grid=(steps,),
            in_specs=[tokens, tokens]
            + [pl.BlockSpec((p.shape[0], block), lambda k, turn: (0, k)) for p in pieces],
            out_specs=(
                pl.BlockSpec((2 * rows, held), lambda k, turn: (0, 0)),
                pl.BlockSpec(memory_space=pltpu.SMEM),
            ),
        ),
        compiler_params=pltpu.CompilerParams(vmem_limit_bytes=VMEM_LIMIT),
        cost_estimate=LITTLE,
    )(jnp.concatenate([turn, first]), own, other, *pieces)
    return turn_next, out


def score_kernel(slots, spans_ref, mine_ref, theirs_ref, right_ref, out_ref):
    rows = mine_ref.shape[0] // 2
    place = lax.broadcasted_iota(jnp.int32, (rows, 1), 0)
    for part in range(2):
        here = slice(part * rows, (part + 1) * rows)
        terms = (mine_ref[here] + theirs_ref[here]) * right_ref[here]
        for j in range(slots):
            k = part * slots + j
            inside = (place >= spans_ref[0, k]) & (place < spans_ref[1, k])
            out_ref[k : k + 1, :] = jnp.sum(
                jnp.where(inside, terms, 0.0), axis=0, keepdims=True
            )


def score(spans, mine, theirs, right):
    slots = spans.shape[1] // 2
    return pl.pallas_call(
        functools.partial(score_kernel, slots),
        out_shape=jax.ShapeDtypeStruct((2 * slots, mine.shape[1]), jnp.float32),
        in_specs=[pl.BlockSpec(memory_space=pltpu.SMEM)]
        + [pl.BlockSpec(memory_space=pltpu.VMEM)] * 3,
        out_specs=pl.BlockSpec(memory_space=pltpu.VMEM),
        compiler_params=pltpu.CompilerParams(vmem_limit_bytes=VMEM_LIMIT),
        cost_estimate=LITTLE,
    )(spans, mine, theirs, right)


def spans_of(slot_ids, lengths):
    widths = bucket_lengths(slot_ids)
    starts = jnp.cumsum(widths) - widths
    return jnp.stack([starts, starts + lengths]).astype(jnp.int32)


def relay(hidden_acts, output_grads, query_left, query_right, bucket_ids, seq_lengths):
    count = lax.axis_size("dp")
    me, group = lax.axis_index("dp"), lax.axis_index("groups")
    z = me // 4
    local, ranks = query_left.shape[:2]
    left = query_left.reshape(local * ranks, -1)
    half = left.shape[1] // 2
    send = functools.partial(flip, count=count)

    acts_there = send(hidden_acts, CORE)
    grads_there = send(output_grads, CORE)
    spans_here = spans_of(bucket_ids, seq_lengths)
    spans = jnp.concatenate([spans_here, send(spans_here, CORE)], axis=1)

    a, b, c = {}, {}, {}
    a[0] = lax.dynamic_slice_in_dim(left, group * half, half, 1)
    c[0] = lax.dynamic_slice_in_dim(left, (1 - group) * half, half, 1)
    b[0] = query_right.reshape(local * ranks, -1)
    at_end = (z == 0) | (z == 3)

    def outer(held):
        return lines(held[ACROSS], [(1, 0), (2, 3)])

    def inner(held):
        return lines(held[NEAR], [(2, 1), (1, 2)])

    def opposite(far, close):
        return jnp.where(at_end, far, close)

    def over_x(held, code):
        held[code | COLUMN] = send(held[code], COLUMN)

    mine = jnp.reshape(group, (1,)).astype(jnp.int32)
    zero = jnp.zeros((1,), jnp.int32)
    groups = (
        (0, COLUMN, NEAR),
        (ACROSS, OPPOSITE, ACROSS | COLUMN),
        (NEAR | COLUMN, OPPOSITE | COLUMN),
    )
    block = 1024

    def times_a(turn, k):
        return proj(turn, hidden_acts, acts_there, [a[i] for i in groups[k]], mine, block)

    def times_c(turn, k):
        return proj(turn, hidden_acts, acts_there, [c[i] for i in groups[k]], 1 - mine, block)

    def times_b(turn, k):
        return proj(turn, output_grads, grads_there, [b[i] for i in groups[k]], zero, block)

    over_x(a, 0)
    a[NEAR] = send(a[0], NEAR)
    a[ACROSS] = send(a[0], ACROSS)

    turn, (a[COLUMN], a[NEAR], b_out) = after(zero, [a[COLUMN], a[NEAR], b[0]])
    close = inner(a)
    b[COLUMN] = send(b_out, COLUMN)
    c[COLUMN] = swap_groups(a[COLUMN])
    turn, a_first = times_a(turn, 0)

    turn, (a[ACROSS], b[COLUMN], c[COLUMN], b_out) = after(turn, [a[ACROSS], b[COLUMN], c[COLUMN], b_out])
    far = outer(a)
    over_x(a, NEAR)
    b[NEAR] = send(b_out, NEAR)
    c[NEAR] = swap_groups(a[NEAR])

    turn, (far, close, a[NEAR | COLUMN], c[NEAR], b_out) = after(
        turn, [far, close, a[NEAR | COLUMN], c[NEAR], b_out]
    )
    over_x(a, ACROSS)
    c[ACROSS] = swap_groups(a[ACROSS])
    b[ACROSS] = send(b_out, ACROSS)
    a[OPPOSITE] = opposite(far, close)
    turn, c_first = times_c(turn, 0)

    turn, (a[ACROSS | COLUMN], b[NEAR], c[ACROSS]) = after(
        turn, [a[ACROSS | COLUMN], b[NEAR], c[ACROSS]]
    )
    over_x(a, OPPOSITE)
    close = inner(b)
    c[OPPOSITE] = swap_groups(a[OPPOSITE])
    c[NEAR | COLUMN] = swap_groups(a[NEAR | COLUMN])
    turn, b_first = times_b(turn, 0)

    turn, (a[OPPOSITE | COLUMN], b[ACROSS], c[OPPOSITE], b_over) = after(
        turn, [a[OPPOSITE | COLUMN], b[ACROSS], c[OPPOSITE], b[COLUMN]]
    )
    far = outer(b)
    over_x(b, ACROSS)
    b[NEAR | COLUMN] = send(b_over, NEAR)
    turn, a_second = times_a(turn, 1)

    turn, (b[ACROSS | COLUMN], far, close, c[NEAR | COLUMN]) = after(
        turn, [b[ACROSS | COLUMN], far, close, c[NEAR | COLUMN]]
    )
    b[OPPOSITE] = opposite(far, close)
    over_x(b, OPPOSITE)
    for code in (ACROSS | COLUMN, OPPOSITE | COLUMN):
        c[code] = swap_groups(a[code])
    turn, a_third = times_a(turn, 2)
    turn, b_second = times_b(turn, 1)
    turn, c_second = times_c(turn, 1)
    sums = [
        score(spans, a_first, c_first, b_first),
        score(spans, a_second, c_second, b_second),
    ]
    turn, b_third = times_b(turn, 2)
    turn, c_third = times_c(turn, 2)
    sums.append(score(spans, a_third, c_third, b_third))

    slots = bucket_ids.shape[0]
    ours = jnp.concatenate([x[:slots] for x in sums], axis=1)
    others = send(jnp.concatenate([x[slots:] for x in sums], axis=1), CORE)
    codes = jnp.array([k for codes in groups for k in codes], jnp.int32)
    owner = jnp.concatenate([me ^ codes, me ^ CORE ^ codes])
    query = owner[:, None] * local + jnp.arange(local, dtype=jnp.int32)[None, :]
    query = jnp.repeat(query.reshape(-1), ranks)
    placed = query[None, :] == jnp.arange(count * local, dtype=jnp.int32)[:, None]
    return lax.dot_general(
        placed.astype(jnp.float32),
        jnp.concatenate([ours, others], axis=1),
        (((1,), (1,)), ((), ())),
        precision=lax.Precision.HIGHEST,
        preferred_element_type=jnp.float32,
    )


def solution(mesh):
    sizes = mesh.shape
    fits = sizes["dp"] == 16 and sizes["groups"] == 2 and sizes["tensor"] == 1
    return jax.shard_map(
        relay if fits else gather_whole,
        mesh=mesh,
        in_specs=(
            P(("groups", "dp"), "tensor"),
            P(("groups", "dp"), "tensor"),
            P("dp", None, "tensor"),
            P("dp", None, "tensor"),
            P(("groups", "dp")),
            P(("groups", "dp")),
        ),
        out_specs=P("tensor", ("groups", "dp")),
        check_vma=False,
    )
```

```python
import functools

import jax
import jax.numpy as jnp
from jax import lax
from jax.experimental import pallas as pl
from jax.experimental.pallas import tpu as pltpu
from jax.sharding import PartitionSpec as P

BUCKET = 128


def bucket_lengths(slot_ids):
    return BUCKET * jnp.where(
        slot_ids == 0, 1, jnp.where(slot_ids == 1, 2, jnp.where(slot_ids == 2, 4, 0))
    ).astype(jnp.int32)


def slot_matrix(slot_ids, lengths, positions):
    widths = bucket_lengths(slot_ids)
    starts = jnp.cumsum(widths) - widths
    place = jnp.arange(positions, dtype=jnp.int32)[:, None]
    inside = (place >= starts[None, :]) & (place < starts[None, :] + lengths[None, :])
    return inside.astype(jnp.float32)


def project(acts, factors):
    rows = factors.reshape(-1, factors.shape[2])
    return lax.dot_general(acts, rows, (((1,), (1,)), ((), ())), preferred_element_type=jnp.float32)


def gather_whole(hidden_acts, output_grads, query_left, query_right, bucket_ids, seq_lengths):
    tokens_here = hidden_acts.shape[0]
    rank_count = query_left.shape[1]
    left_all, right_all = (
        lax.all_gather(query_left, "dp", axis=0, tiled=True),
        lax.all_gather(query_right, "dp", axis=0, tiled=True),
    )
    left_proj = project(hidden_acts, left_all)
    right_proj = project(output_grads, right_all)
    queries = left_proj.shape[1] // rank_count
    left_terms = left_proj.reshape(tokens_here, queries, rank_count)
    right_terms = right_proj.reshape(tokens_here, queries, rank_count)
    left_terms, right_terms = lax.psum((left_terms, right_terms), "tensor")
    share_size = queries // lax.axis_size("tensor")
    first_query = lax.axis_index("tensor") * share_size
    left_terms = lax.dynamic_slice_in_dim(left_terms, first_query, share_size, 1)
    right_terms = lax.dynamic_slice_in_dim(right_terms, first_query, share_size, 1)
    token_term = jnp.sum(left_terms * right_terms, axis=2)
    slot_mask = slot_matrix(bucket_ids, seq_lengths, tokens_here)
    return jnp.dot(
        token_term.T, slot_mask, precision=lax.Precision.HIGHEST, preferred_element_type=jnp.float32
    )


CORE, COLUMN, NEAR, ACROSS, OPPOSITE = 1, 2, 4, 12, 8
LITTLE = pl.CostEstimate(flops=1, bytes_accessed=1, transcendentals=0)
VMEM_LIMIT = 16 * 1024 * 1024


def flip(array, code, count):
    return lax.ppermute(array, "dp", [(i, i ^ code) for i in range(count)])


def swap_groups(array):
    return lax.ppermute(array, "groups", [(0, 1), (1, 0)])


def after_kernel(count, *refs):
    refs[-1][0] = refs[count][0]


def after(turn, arrays):
    count = len(arrays)
    anywhere = pl.BlockSpec(memory_space=pl.ANY)
    scalar = pl.BlockSpec(memory_space=pltpu.SMEM)
    *arrays, turn = pl.pallas_call(
        functools.partial(after_kernel, count),
        out_shape=[jax.ShapeDtypeStruct(x.shape, x.dtype) for x in (*arrays, turn)],
        in_specs=[anywhere] * count + [scalar],
        out_specs=[anywhere] * count + [scalar],
        input_output_aliases={i: i for i in range(count)},
        cost_estimate=LITTLE,
    )(*arrays, turn)
    return turn, arrays


def lines(array, pairs):
    return lax.ppermute(
        array, "dp", [(a * 4 + rest, b * 4 + rest) for a, b in pairs for rest in range(4)]
    )


def proj_kernel(count, at_ref, own_ref, other_ref, *refs):
    pieces, (out_ref, next_ref) = refs[:count], refs[count:]
    step = pl.program_id(0)
    rows = own_ref.shape[0]
    factors = jnp.concatenate([p[...] for p in pieces], axis=0)
    dims = (((1,), (1,)), ((), ()))
    top = lax.dot_general(own_ref[...], factors, dims, preferred_element_type=jnp.float32)
    low = lax.dot_general(other_ref[...], factors, dims, preferred_element_type=jnp.float32)

    @pl.when(step == 0)
    def _():
        next_ref[0] = at_ref[0]
        out_ref[:rows] = top
        out_ref[rows:] = low

    @pl.when(step > 0)
    def _():
        out_ref[:rows] += top
        out_ref[rows:] += low


def proj(turn, tokens, rows, pieces, first, block):
    depth = pieces[0].shape[1]
    steps = depth // block
    held = sum(p.shape[0] for p in pieces)
    (own, own_row), (other, other_row) = tokens
    out, turn_next = pl.pallas_call(
        functools.partial(proj_kernel, len(pieces)),
        out_shape=(
            jax.ShapeDtypeStruct((2 * rows, held), jnp.float32),
            jax.ShapeDtypeStruct((1,), jnp.int32),
        ),
        grid_spec=pltpu.PrefetchScalarGridSpec(
            num_scalar_prefetch=1,
            grid=(steps,),
            in_specs=[
                pl.BlockSpec((rows, block), lambda k, at: (at[2], at[1] * steps + k)),
                pl.BlockSpec((rows, block), lambda k, at: (at[3], at[1] * steps + k)),
            ]
            + [pl.BlockSpec((p.shape[0], block), lambda k, at: (0, k)) for p in pieces],
            out_specs=(
                pl.BlockSpec((2 * rows, held), lambda k, at: (0, 0)),
                pl.BlockSpec(memory_space=pltpu.SMEM),
            ),
        ),
        compiler_params=pltpu.CompilerParams(vmem_limit_bytes=VMEM_LIMIT),
        cost_estimate=LITTLE,
    )(jnp.concatenate([turn, first, own_row, other_row]), own, other, *pieces)
    return turn_next, out


def score_kernel(slots, spans_ref, mine_ref, theirs_ref, right_ref, out_ref):
    rows = mine_ref.shape[0] // 2
    place = lax.broadcasted_iota(jnp.int32, (rows, 1), 0)
    for part in range(2):
        here = slice(part * rows, (part + 1) * rows)
        terms = (mine_ref[here] + theirs_ref[here]) * right_ref[here]
        for j in range(slots):
            k = part * slots + j
            inside = (place >= spans_ref[0, k]) & (place < spans_ref[1, k])
            out_ref[k : k + 1, :] = jnp.sum(
                jnp.where(inside, terms, 0.0), axis=0, keepdims=True
            )


def score(spans, mine, theirs, right):
    slots = spans.shape[1] // 2
    return pl.pallas_call(
        functools.partial(score_kernel, slots),
        out_shape=jax.ShapeDtypeStruct((2 * slots, mine.shape[1]), jnp.float32),
        in_specs=[pl.BlockSpec(memory_space=pltpu.SMEM)]
        + [pl.BlockSpec(memory_space=pltpu.VMEM)] * 3,
        out_specs=pl.BlockSpec(memory_space=pltpu.VMEM),
        compiler_params=pltpu.CompilerParams(vmem_limit_bytes=VMEM_LIMIT),
        cost_estimate=LITTLE,
    )(spans, mine, theirs, right)


def spans_of(slot_ids, lengths):
    widths = bucket_lengths(slot_ids)
    starts = jnp.cumsum(widths) - widths
    return jnp.stack([starts, starts + lengths]).astype(jnp.int32)


def relay(hidden_acts, output_grads, query_left, query_right, bucket_ids, seq_lengths):
    count = lax.axis_size("dp")
    me, group = lax.axis_index("dp"), lax.axis_index("groups")
    z = me // 4
    local, ranks = query_left.shape[:2]
    left = query_left.reshape(local * ranks, -1)
    half = left.shape[1] // 2
    send = functools.partial(flip, count=count)

    acts_there = send(hidden_acts, CORE)
    pairs = [[i, i ^ CORE] for i in range(0, count, 2)]
    grads_both = lax.all_gather(output_grads, "dp", axis_index_groups=pairs, axis=0, tiled=True)
    spans_here = spans_of(bucket_ids, seq_lengths)
    spans = jnp.concatenate([spans_here, send(spans_here, CORE)], axis=1)

    a, b, c = {}, {}, {}
    a["own"] = lax.dynamic_slice_in_dim(left, group * half, half, 1)
    c["own"] = lax.dynamic_slice_in_dim(left, (1 - group) * half, half, 1)
    b["own"] = query_right.reshape(local * ranks, -1)
    at_end = (z == 0) | (z == 3)

    def near(piece):
        return send(piece, NEAR)

    def middle(piece):
        return lines(piece, [(1, 2), (2, 1)])

    def outward(piece):
        return lines(piece, [(1, 0), (2, 3)])

    def over_x(piece):
        return send(piece, COLUMN)

    core = (me & CORE).reshape(1).astype(jnp.int32)
    mine = jnp.reshape(group, (1,)).astype(jnp.int32)
    zero = jnp.zeros((1,), jnp.int32)
    acts = ((hidden_acts, zero), (acts_there, zero))
    grads = ((grads_both, core), (grads_both, 1 - core))
    groups = (("own", "x", "n", "f"), ("xf", "g", "xn", "xg"))
    tokens_here = hidden_acts.shape[0]
    block = 1024

    def times_a(turn, k):
        return proj(turn, acts, tokens_here, [a[i] for i in groups[k]], mine, block)

    def times_c(turn, k):
        return proj(turn, acts, tokens_here, [c[i] for i in groups[k]], 1 - mine, block)

    def times_b(turn, k):
        return proj(turn, grads, tokens_here, [b[i] for i in groups[k]], zero, block)

    a["x"] = over_x(a["own"])
    a["n"] = near(a["own"])
    a_mid = middle(a["own"])

    turn, (a["x"], a["n"], a_mid) = after(zero, [a["x"], a["n"], a_mid])
    a_in = middle(a["n"])
    a_out = outward(a_mid)
    a["xn"] = over_x(a["n"])
    c["x"] = swap_groups(a["x"])

    turn, (a_in, a_out, a["xn"], c["x"], b_own) = after(turn, [a_in, a_out, a["xn"], c["x"], b["own"]])
    a["f"] = jnp.where(at_end, a_out, a_mid)
    a_last = outward(a_in)
    a["xf"] = over_x(a["f"])
    c["n"] = swap_groups(a["n"])
    b_mid = middle(b_own)
    turn, a_first = times_a(turn, 0)

    turn, (a_last, a["xf"], c["n"], b_mid, b_own) = after(turn, [a_last, a["xf"], c["n"], b_mid, b_own])
    a["g"] = jnp.where(at_end, a_last, a_in)
    b["n"] = near(b_own)
    b["x"] = over_x(b_own)
    c["f"] = swap_groups(a["f"])

    turn, (b["n"], b["x"], c["f"]) = after(turn, [b["n"], b["x"], c["f"]])
    b_in = middle(b["n"])
    b_out = outward(b_mid)
    a["xg"] = over_x(a["g"])
    c["g"] = swap_groups(a["g"])
    turn, c_first = times_c(turn, 0)

    turn, (b_in, b_out, a["xg"], c["g"]) = after(turn, [b_in, b_out, a["xg"], c["g"]])
    b["f"] = jnp.where(at_end, b_out, b_mid)
    b_last = outward(b_in)
    b["xf"] = over_x(b["f"])
    c["xf"] = swap_groups(a["xf"])
    turn, b_first = times_b(turn, 0)

    turn, (b_last, b["xf"], c["xf"]) = after(turn, [b_last, b["xf"], c["xf"]])
    b["g"] = jnp.where(at_end, b_last, b_in)
    b["xg"] = over_x(b["g"])
    b["xn"] = near(b["x"])
    c["xn"] = swap_groups(a["xn"])
    turn, a_second = times_a(turn, 1)

    turn, (b["xg"], b["xn"], c["xn"], c["g"]) = after(turn, [b["xg"], b["xn"], c["xn"], c["g"]])
    split = c["g"].shape[0] // 2
    c_top = over_x(c["g"][:split])
    c_low = swap_groups(a["xg"][split:])
    sums = [score(spans, a_first, c_first, b_first)]
    turn, b_second = times_b(turn, 1)
    groups = (groups[0], ("xf", "g", "xn", "top", "low"))
    c["top"], c["low"] = c_top, c_low
    turn, c_second = times_c(turn, 1)
    sums.append(score(spans, a_second, c_second, b_second))

    slots = bucket_ids.shape[0]
    ours = jnp.concatenate([x[:slots] for x in sums], axis=1)
    others = send(jnp.concatenate([x[slots:] for x in sums], axis=1), CORE)
    f_code = jnp.where(at_end, OPPOSITE, ACROSS)
    g_code = jnp.where(at_end, ACROSS, OPPOSITE)
    codes = [0, COLUMN, NEAR, f_code, f_code | COLUMN, g_code, NEAR | COLUMN, g_code | COLUMN]
    codes = jnp.stack([jnp.asarray(code, jnp.int32) for code in codes])
    owner = jnp.concatenate([me ^ codes, me ^ CORE ^ codes])
    query = owner[:, None] * local + jnp.arange(local, dtype=jnp.int32)[None, :]
    query = jnp.repeat(query.reshape(-1), ranks)
    placed = query[None, :] == jnp.arange(count * local, dtype=jnp.int32)[:, None]
    return lax.dot_general(
        placed.astype(jnp.float32),
        jnp.concatenate([ours, others], axis=1),
        (((1,), (1,)), ((), ())),
        precision=lax.Precision.HIGHEST,
        preferred_element_type=jnp.float32,
    )


def solution(mesh):
    sizes = mesh.shape
    fits = sizes["dp"] == 16 and sizes["groups"] == 2 and sizes["tensor"] == 1
    return jax.shard_map(
        relay if fits else gather_whole,
        mesh=mesh,
        in_specs=(
            P(("groups", "dp"), "tensor"),
            P(("groups", "dp"), "tensor"),
            P("dp", None, "tensor"),
            P("dp", None, "tensor"),
            P(("groups", "dp")),
            P(("groups", "dp")),
        ),
        out_specs=P("tensor", ("groups", "dp")),
        check_vma=False,
    )
```

```python
import functools

import jax
import jax.numpy as jnp
from jax import lax
from jax.experimental import pallas as pl
from jax.experimental.pallas import tpu as pltpu
from jax.sharding import PartitionSpec as P

BUCKET = 128


def bucket_lengths(slot_ids):
    return BUCKET * jnp.where(
        slot_ids == 0, 1, jnp.where(slot_ids == 1, 2, jnp.where(slot_ids == 2, 4, 0))
    ).astype(jnp.int32)


def slot_matrix(slot_ids, lengths, positions):
    widths = bucket_lengths(slot_ids)
    starts = jnp.cumsum(widths) - widths
    place = jnp.arange(positions, dtype=jnp.int32)[:, None]
    inside = (place >= starts[None, :]) & (place < starts[None, :] + lengths[None, :])
    return inside.astype(jnp.float32)


def project(acts, factors):
    rows = factors.reshape(-1, factors.shape[2])
    return lax.dot_general(acts, rows, (((1,), (1,)), ((), ())), preferred_element_type=jnp.float32)


def gather_whole(hidden_acts, output_grads, query_left, query_right, bucket_ids, seq_lengths):
    tokens_here = hidden_acts.shape[0]
    rank_count = query_left.shape[1]
    left_all, right_all = (
        lax.all_gather(query_left, "dp", axis=0, tiled=True),
        lax.all_gather(query_right, "dp", axis=0, tiled=True),
    )
    left_proj = project(hidden_acts, left_all)
    right_proj = project(output_grads, right_all)
    queries = left_proj.shape[1] // rank_count
    left_terms = left_proj.reshape(tokens_here, queries, rank_count)
    right_terms = right_proj.reshape(tokens_here, queries, rank_count)
    left_terms, right_terms = lax.psum((left_terms, right_terms), "tensor")
    share_size = queries // lax.axis_size("tensor")
    first_query = lax.axis_index("tensor") * share_size
    left_terms = lax.dynamic_slice_in_dim(left_terms, first_query, share_size, 1)
    right_terms = lax.dynamic_slice_in_dim(right_terms, first_query, share_size, 1)
    token_term = jnp.sum(left_terms * right_terms, axis=2)
    slot_mask = slot_matrix(bucket_ids, seq_lengths, tokens_here)
    return jnp.dot(
        token_term.T, slot_mask, precision=lax.Precision.HIGHEST, preferred_element_type=jnp.float32
    )


CORE, COLUMN, NEAR, ACROSS, OPPOSITE = 1, 2, 4, 12, 8
LITTLE = pl.CostEstimate(flops=1, bytes_accessed=1, transcendentals=0)
VMEM_LIMIT = 63 * 1024 * 1024


def flip(array, code, count):
    return lax.ppermute(array, "dp", [(i, i ^ code) for i in range(count)])


def swap_groups(array):
    return lax.ppermute(array, "groups", [(0, 1), (1, 0)])


def after_kernel(count, *refs):
    refs[-1][0] = refs[count][0]


def after(turn, arrays):
    count = len(arrays)
    anywhere = pl.BlockSpec(memory_space=pltpu.HBM)
    scalar = pl.BlockSpec(memory_space=pltpu.SMEM)
    *arrays, turn = pl.pallas_call(
        functools.partial(after_kernel, count),
        out_shape=[jax.ShapeDtypeStruct(x.shape, x.dtype) for x in (*arrays, turn)],
        in_specs=[anywhere] * count + [scalar],
        out_specs=[anywhere] * count + [scalar],
        input_output_aliases={i: i for i in range(count)},
        compiler_params=pltpu.CompilerParams(vmem_limit_bytes=VMEM_LIMIT),
        cost_estimate=LITTLE,
    )(*arrays, turn)
    return turn, arrays


def lines(array, pairs):
    return lax.ppermute(
        array, "dp", [(a * 4 + rest, b * 4 + rest) for a, b in pairs for rest in range(4)]
    )


def proj_kernel(count, at_ref, own_ref, other_ref, *refs):
    pieces, (out_ref, next_ref) = refs[:count], refs[count:]
    step = pl.program_id(0)
    rows = own_ref.shape[0]
    factors = jnp.concatenate([p[...] for p in pieces], axis=0)
    dims = (((1,), (1,)), ((), ()))
    top = lax.dot_general(own_ref[...], factors, dims, preferred_element_type=jnp.float32)
    low = lax.dot_general(other_ref[...], factors, dims, preferred_element_type=jnp.float32)

    @pl.when(step == 0)
    def _():
        next_ref[0] = at_ref[0]
        out_ref[:rows] = top
        out_ref[rows:] = low

    @pl.when(step > 0)
    def _():
        out_ref[:rows] += top
        out_ref[rows:] += low


def proj(turn, tokens, rows, pieces, first, block):
    depth = pieces[0].shape[1]
    steps = depth // block
    held = sum(p.shape[0] for p in pieces)
    (own, own_row), (other, other_row) = tokens
    out, turn_next = pl.pallas_call(
        functools.partial(proj_kernel, len(pieces)),
        out_shape=(
            jax.ShapeDtypeStruct((2 * rows, held), jnp.float32),
            jax.ShapeDtypeStruct((1,), jnp.int32),
        ),
        grid_spec=pltpu.PrefetchScalarGridSpec(
            num_scalar_prefetch=1,
            grid=(steps,),
            in_specs=[
                pl.BlockSpec((rows, block), lambda k, at: (at[2], at[1] * steps + k)),
                pl.BlockSpec((rows, block), lambda k, at: (at[3], at[1] * steps + k)),
            ]
            + [pl.BlockSpec((p.shape[0], block), lambda k, at: (0, k)) for p in pieces],
            out_specs=(
                pl.BlockSpec((2 * rows, held), lambda k, at: (0, 0)),
                pl.BlockSpec(memory_space=pltpu.SMEM),
            ),
        ),
        compiler_params=pltpu.CompilerParams(vmem_limit_bytes=VMEM_LIMIT),
        cost_estimate=LITTLE,
    )(jnp.concatenate([turn, first, own_row, other_row]), own, other, *pieces)
    return turn_next, out


def score_kernel(slots, spans_ref, mine_ref, theirs_ref, right_ref, out_ref):
    rows = mine_ref.shape[0] // 2
    place = lax.broadcasted_iota(jnp.int32, (rows, 1), 0)
    for part in range(2):
        here = slice(part * rows, (part + 1) * rows)
        terms = (mine_ref[here] + theirs_ref[here]) * right_ref[here]
        for j in range(slots):
            k = part * slots + j
            inside = (place >= spans_ref[0, k]) & (place < spans_ref[1, k])
            out_ref[k : k + 1, :] = jnp.sum(
                jnp.where(inside, terms, 0.0), axis=0, keepdims=True
            )


def score(spans, mine, theirs, right):
    slots = spans.shape[1] // 2
    return pl.pallas_call(
        functools.partial(score_kernel, slots),
        out_shape=jax.ShapeDtypeStruct((2 * slots, mine.shape[1]), jnp.float32),
        in_specs=[pl.BlockSpec(memory_space=pltpu.SMEM)]
        + [pl.BlockSpec(memory_space=pltpu.VMEM)] * 3,
        out_specs=pl.BlockSpec(memory_space=pltpu.VMEM),
        compiler_params=pltpu.CompilerParams(vmem_limit_bytes=VMEM_LIMIT),
        cost_estimate=LITTLE,
    )(spans, mine, theirs, right)


def spans_of(slot_ids, lengths):
    widths = bucket_lengths(slot_ids)
    starts = jnp.cumsum(widths) - widths
    return jnp.stack([starts, starts + lengths]).astype(jnp.int32)


def relay(hidden_acts, output_grads, query_left, query_right, bucket_ids, seq_lengths):
    count = lax.axis_size("dp")
    me, group = lax.axis_index("dp"), lax.axis_index("groups")
    z = me // 4
    local, ranks = query_left.shape[:2]
    left = query_left.reshape(local * ranks, -1)
    half = left.shape[1] // 2
    send = functools.partial(flip, count=count)

    acts_there = send(hidden_acts, CORE)
    pairs = [[i, i ^ CORE] for i in range(0, count, 2)]
    grads_both = lax.all_gather(output_grads, "dp", axis_index_groups=pairs, axis=0, tiled=True)
    spans_here = spans_of(bucket_ids, seq_lengths)
    spans = jnp.concatenate([spans_here, send(spans_here, CORE)], axis=1)

    a, b, c = {}, {}, {}
    a["own"] = lax.dynamic_slice_in_dim(left, group * half, half, 1)
    c["own"] = lax.dynamic_slice_in_dim(left, (1 - group) * half, half, 1)
    b["own"] = query_right.reshape(local * ranks, -1)
    at_end = (z == 0) | (z == 3)

    def near(piece):
        return send(piece, NEAR)

    def middle(piece):
        return lines(piece, [(1, 2), (2, 1)])

    def outward(piece):
        return lines(piece, [(1, 0), (2, 3)])

    def over_x(piece):
        return send(piece, COLUMN)

    core = (me & CORE).reshape(1).astype(jnp.int32)
    mine = jnp.reshape(group, (1,)).astype(jnp.int32)
    zero = jnp.zeros((1,), jnp.int32)
    acts = ((hidden_acts, zero), (acts_there, zero))
    grads = ((grads_both, core), (grads_both, 1 - core))
    groups = (("own", "x", "n", "f"), ("xf", "g", "xn", "xg"))
    tokens_here = hidden_acts.shape[0]
    block = 1024

    def times_a(turn, k):
        return proj(turn, acts, tokens_here, [a[i] for i in groups[k]], mine, block)

    def times_c(turn, k):
        return proj(turn, acts, tokens_here, [c[i] for i in groups[k]], 1 - mine, block)

    def times_b(turn, k):
        return proj(turn, grads, tokens_here, [b[i] for i in groups[k]], zero, block)

    a["x"] = over_x(a["own"])
    a["n"] = near(a["own"])
    a_mid = middle(a["own"])

    turn, (a["x"], a["n"], a_mid) = after(zero, [a["x"], a["n"], a_mid])
    a_in = middle(a["n"])
    a_out = outward(a_mid)
    a["xn"] = over_x(a["n"])
    c["x"] = swap_groups(a["x"])

    turn, (a_in, a_out, a["xn"], c["x"], b_own) = after(turn, [a_in, a_out, a["xn"], c["x"], b["own"]])
    a["f"] = jnp.where(at_end, a_out, a_mid)
    a_last = outward(a_in)
    a["xf"] = over_x(a["f"])
    c["n"] = swap_groups(a["n"])
    b_mid = middle(b_own)
    turn, a_first = times_a(turn, 0)

    turn, (a_last, a["xf"], c["n"], b_mid, b_own) = after(turn, [a_last, a["xf"], c["n"], b_mid, b_own])
    a["g"] = jnp.where(at_end, a_last, a_in)
    b["n"] = near(b_own)
    b["x"] = over_x(b_own)
    c["f"] = swap_groups(a["f"])

    turn, (b["n"], b["x"], c["f"]) = after(turn, [b["n"], b["x"], c["f"]])
    b_in = middle(b["n"])
    b_out = outward(b_mid)
    a["xg"] = over_x(a["g"])
    c["g"] = swap_groups(a["g"])
    turn, c_first = times_c(turn, 0)

    turn, (b_in, b_out, a["xg"], c["g"]) = after(turn, [b_in, b_out, a["xg"], c["g"]])
    b["f"] = jnp.where(at_end, b_out, b_mid)
    b_last = outward(b_in)
    b["xf"] = over_x(b["f"])
    c["xf"] = swap_groups(a["xf"])
    turn, b_first = times_b(turn, 0)

    turn, (b_last, b["xf"], c["xf"]) = after(turn, [b_last, b["xf"], c["xf"]])
    b["g"] = jnp.where(at_end, b_last, b_in)
    b["xg"] = over_x(b["g"])
    b["xn"] = near(b["x"])
    c["xn"] = swap_groups(a["xn"])
    turn, a_second = times_a(turn, 1)

    turn, (b["xg"], b["xn"], c["xn"], c["g"]) = after(turn, [b["xg"], b["xn"], c["xn"], c["g"]])
    split = c["g"].shape[0] // 2
    c_top = over_x(c["g"][:split])
    c_low = swap_groups(a["xg"][split:])
    sums = [score(spans, a_first, c_first, b_first)]
    turn, b_second = times_b(turn, 1)
    groups = (groups[0], ("xf", "g", "xn", "top", "low"))
    c["top"], c["low"] = c_top, c_low
    turn, c_second = times_c(turn, 1)
    sums.append(score(spans, a_second, c_second, b_second))

    slots = bucket_ids.shape[0]
    ours = jnp.concatenate([x[:slots] for x in sums], axis=1)
    others = send(jnp.concatenate([x[slots:] for x in sums], axis=1), CORE)
    f_code = jnp.where(at_end, OPPOSITE, ACROSS)
    g_code = jnp.where(at_end, ACROSS, OPPOSITE)
    codes = [0, COLUMN, NEAR, f_code, f_code | COLUMN, g_code, NEAR | COLUMN, g_code | COLUMN]
    codes = jnp.stack([jnp.asarray(code, jnp.int32) for code in codes])
    owner = jnp.concatenate([me ^ codes, me ^ CORE ^ codes])
    query = owner[:, None] * local + jnp.arange(local, dtype=jnp.int32)[None, :]
    query = jnp.repeat(query.reshape(-1), ranks)
    placed = query[None, :] == jnp.arange(count * local, dtype=jnp.int32)[:, None]
    return lax.dot_general(
        placed.astype(jnp.float32),
        jnp.concatenate([ours, others], axis=1),
        (((1,), (1,)), ((), ())),
        precision=lax.Precision.HIGHEST,
        preferred_element_type=jnp.float32,
    )


def solution(mesh):
    sizes = mesh.shape
    fits = sizes["dp"] == 16 and sizes["groups"] == 2 and sizes["tensor"] == 1
    return jax.shard_map(
        relay if fits else gather_whole,
        mesh=mesh,
        in_specs=(
            P(("groups", "dp"), "tensor"),
            P(("groups", "dp"), "tensor"),
            P("dp", None, "tensor"),
            P("dp", None, "tensor"),
            P(("groups", "dp")),
            P(("groups", "dp")),
        ),
        out_specs=P("tensor", ("groups", "dp")),
        check_vma=False,
    )
```

```python
import functools

import jax
import jax.numpy as jnp
from jax import lax
from jax.experimental import pallas as pl
from jax.experimental.pallas import tpu as pltpu
from jax.sharding import PartitionSpec as P

BUCKET = 128


def bucket_lengths(slot_ids):
    return BUCKET * jnp.where(
        slot_ids == 0, 1, jnp.where(slot_ids == 1, 2, jnp.where(slot_ids == 2, 4, 0))
    ).astype(jnp.int32)


def slot_matrix(slot_ids, lengths, positions):
    widths = bucket_lengths(slot_ids)
    starts = jnp.cumsum(widths) - widths
    place = jnp.arange(positions, dtype=jnp.int32)[:, None]
    inside = (place >= starts[None, :]) & (place < starts[None, :] + lengths[None, :])
    return inside.astype(jnp.float32)


def project(acts, factors):
    rows = factors.reshape(-1, factors.shape[2])
    return lax.dot_general(acts, rows, (((1,), (1,)), ((), ())), preferred_element_type=jnp.float32)


def gather_whole(hidden_acts, output_grads, query_left, query_right, bucket_ids, seq_lengths):
    tokens_here = hidden_acts.shape[0]
    rank_count = query_left.shape[1]
    left_all, right_all = (
        lax.all_gather(query_left, "dp", axis=0, tiled=True),
        lax.all_gather(query_right, "dp", axis=0, tiled=True),
    )
    left_proj = project(hidden_acts, left_all)
    right_proj = project(output_grads, right_all)
    queries = left_proj.shape[1] // rank_count
    left_terms = left_proj.reshape(tokens_here, queries, rank_count)
    right_terms = right_proj.reshape(tokens_here, queries, rank_count)
    left_terms, right_terms = lax.psum((left_terms, right_terms), "tensor")
    share_size = queries // lax.axis_size("tensor")
    first_query = lax.axis_index("tensor") * share_size
    left_terms = lax.dynamic_slice_in_dim(left_terms, first_query, share_size, 1)
    right_terms = lax.dynamic_slice_in_dim(right_terms, first_query, share_size, 1)
    token_term = jnp.sum(left_terms * right_terms, axis=2)
    slot_mask = slot_matrix(bucket_ids, seq_lengths, tokens_here)
    return jnp.dot(
        token_term.T, slot_mask, precision=lax.Precision.HIGHEST, preferred_element_type=jnp.float32
    )


CORE, COLUMN, NEAR, ACROSS, OPPOSITE = 1, 2, 4, 12, 8
LITTLE = pl.CostEstimate(flops=1, bytes_accessed=1, transcendentals=0)
VMEM_LIMIT = 63 * 1024 * 1024


def flip(array, code, count):
    return lax.ppermute(array, "dp", [(i, i ^ code) for i in range(count)])


def swap_groups(array):
    return lax.ppermute(array, "groups", [(0, 1), (1, 0)])


def after_kernel(count, merge, inside_ref, turn_ref, *refs):
    arrays, next_ref = refs[-1 - count : -1], refs[-1]
    next_ref[0] = turn_ref[0]
    if merge is not None:
        kept, over = (arrays[i] for i in merge)

        @pl.when(inside_ref[0] == 1)
        def _():
            def copy(sem):
                moved = pltpu.make_async_copy(over, kept, sem)
                moved.start()
                moved.wait()

            pl.run_scoped(copy, pltpu.SemaphoreType.DMA(()))


def after(turn, arrays, inside, merge=None, there=()):
    count = len(arrays)
    hbm = pl.BlockSpec(memory_space=pltpu.HBM)
    scalar = pl.BlockSpec(memory_space=pltpu.SMEM)
    *arrays, turn = pl.pallas_call(
        functools.partial(after_kernel, count, merge),
        out_shape=[jax.ShapeDtypeStruct(x.shape, x.dtype) for x in (*arrays, turn)],
        in_specs=[scalar] * 2 + [hbm] * (len(there) + count),
        out_specs=[hbm] * count + [scalar],
        input_output_aliases={2 + len(there) + i: i for i in range(count)},
        compiler_params=pltpu.CompilerParams(vmem_limit_bytes=VMEM_LIMIT),
        cost_estimate=LITTLE,
    )(inside, turn, *there, *arrays)
    return turn, arrays


def lines(array, pairs):
    return lax.ppermute(
        array, "dp", [(a * 4 + rest, b * 4 + rest) for a, b in pairs for rest in range(4)]
    )


def score_into(out_ref, spans_ref, terms_of, rows):
    slots = out_ref.shape[0] // 2
    place = lax.broadcasted_iota(jnp.int32, (rows, 1), 0)
    for part in range(2):
        terms = terms_of(slice(part * rows, (part + 1) * rows))
        for j in range(slots):
            k = part * slots + j
            inside = (place >= spans_ref[0, k]) & (place < spans_ref[1, k])
            out_ref[k : k + 1, :] = jnp.sum(jnp.where(inside, terms, 0.0), axis=0, keepdims=True)


def proj_kernel(count, last, turn_ref, at_ref, own_ref, other_ref, *refs):
    del at_ref
    pieces, refs = refs[:count], refs[count:]
    if last is None:
        acc_ref, next_ref = refs
    else:
        spans_ref, left_ref, second_ref, out_ref, next_ref, acc_ref = refs
    step = pl.program_id(0)
    rows = own_ref.shape[0]

    @pl.when(step == 0)
    def _():
        next_ref[0] = turn_ref[0]
        acc_ref[...] = jnp.zeros_like(acc_ref)

    factors = jnp.concatenate([p[...] for p in pieces], axis=0)
    for part, tokens in enumerate((own_ref, other_ref)):
        acc_ref[part * rows : (part + 1) * rows] += lax.dot_general(
            tokens[...], factors, (((1,), (1,)), ((), ())), preferred_element_type=jnp.float32
        )

    if last is not None:

        @pl.when(step == pl.num_programs(0) - 1)
        def _():
            def terms(here):
                if last:
                    return (left_ref[here] + second_ref[here]) * acc_ref[here]
                return (left_ref[here] + acc_ref[here]) * second_ref[here]

            score_into(out_ref, spans_ref, terms, rows)


def proj(turn, tokens, rows, pieces, first, steps, last=None, spans=None, others=()):
    depth = pieces[0].shape[1]
    block = depth // steps
    held = sum(p.shape[0] for p in pieces)
    (own, own_row), (other, other_row) = tokens
    whole = pl.BlockSpec((2 * rows, held), lambda k, turn, at: (0, 0))
    scalar = pl.BlockSpec(memory_space=pltpu.SMEM)
    if last is None:
        more_specs, more, scratch = [], (), []
        out_shape, out_spec = (2 * rows, held), whole
    else:
        more_specs, more = [scalar, whole, whole], (spans, *others)
        scratch = [pltpu.VMEM((2 * rows, held), jnp.float32)]
        out_shape = (spans.shape[1], held)
        out_spec = pl.BlockSpec(out_shape, lambda k, turn, at: (0, 0))
    out, turn_next = pl.pallas_call(
        functools.partial(proj_kernel, len(pieces), last),
        out_shape=(
            jax.ShapeDtypeStruct(out_shape, jnp.float32),
            jax.ShapeDtypeStruct((1,), jnp.int32),
        ),
        grid_spec=pltpu.PrefetchScalarGridSpec(
            num_scalar_prefetch=2,
            grid=(steps,),
            in_specs=[
                pl.BlockSpec((rows, block), lambda k, turn, at: (at[1], at[0] * steps + k)),
                pl.BlockSpec((rows, block), lambda k, turn, at: (at[2], at[0] * steps + k)),
            ]
            + [pl.BlockSpec((p.shape[0], block), lambda k, turn, at: (0, k)) for p in pieces]
            + more_specs,
            out_specs=(out_spec, scalar),
            scratch_shapes=scratch,
        ),
        compiler_params=pltpu.CompilerParams(vmem_limit_bytes=VMEM_LIMIT),
        cost_estimate=LITTLE,
    )(turn, jnp.concatenate([first, own_row, other_row]), own, other, *pieces, *more)
    return turn_next, out


def spans_of(slot_ids, lengths):
    widths = bucket_lengths(slot_ids)
    starts = jnp.cumsum(widths) - widths
    return jnp.stack([starts, starts + lengths]).astype(jnp.int32)


def relay(hidden_acts, output_grads, query_left, query_right, bucket_ids, seq_lengths):
    count = lax.axis_size("dp")
    me, group = lax.axis_index("dp"), lax.axis_index("groups")
    z = me // 4
    local, ranks = query_left.shape[:2]
    left = query_left.reshape(local * ranks, -1)
    half = left.shape[1] // 2
    send = functools.partial(flip, count=count)

    acts_there = send(hidden_acts, CORE)
    grads_there = send(output_grads, CORE)
    spans_here = spans_of(bucket_ids, seq_lengths)
    spans = jnp.concatenate([spans_here, send(spans_here, CORE)], axis=1)

    a, b, c = {}, {}, {}
    a["own"] = lax.dynamic_slice_in_dim(left, group * half, half, 1)
    c["own"] = lax.dynamic_slice_in_dim(left, (1 - group) * half, half, 1)
    b["own"] = query_right.reshape(local * ranks, -1)
    at_end = (z == 0) | (z == 3)

    def near(piece):
        return send(piece, NEAR)

    def middle(piece):
        return lines(piece, [(1, 2), (2, 1)])

    def outward(piece):
        return lines(piece, [(1, 0), (2, 3)])

    def over_x(piece):
        return send(piece, COLUMN)

    inside = (~at_end).reshape(1).astype(jnp.int32)
    mine = jnp.reshape(group, (1,)).astype(jnp.int32)
    zero = jnp.zeros((1,), jnp.int32)
    acts = ((hidden_acts, zero), (acts_there, zero))
    grads = ((output_grads, zero), (grads_there, zero))
    groups = (("own", "x", "n", "f"), ("xf", "g", "xn", "xg"))
    tokens_here = hidden_acts.shape[0]
    steps = 4

    def times_a(turn, k):
        return proj(turn, acts, tokens_here, [a[i] for i in groups[k]], mine, steps)

    def times_c(turn, k, *score):
        return proj(turn, acts, tokens_here, [c[i] for i in groups[k]], 1 - mine, steps, *score)

    def times_b(turn, k, *score):
        return proj(turn, grads, tokens_here, [b[i] for i in groups[k]], zero, steps, *score)

    a["x"] = over_x(a["own"])
    a["n"] = near(a["own"])
    a_mid = middle(a["own"])

    turn, (a["x"], a["n"], a_mid) = after(zero, [a["x"], a["n"], a_mid], inside, None, [acts_there])
    a_in = middle(a["n"])
    a_out = outward(a_mid)
    a["xn"] = over_x(a["n"])
    c["x"] = swap_groups(a["x"])

    turn, (a["f"], a_in, a["xn"], c["x"], b_own, a_mid) = after(
        turn, [a_out, a_in, a["xn"], c["x"], b["own"], a_mid], inside, (0, 5), [grads_there]
    )
    a_last = outward(a_in)
    a["xf"] = over_x(a["f"])
    c["n"] = swap_groups(a["n"])
    b_mid = middle(b_own)
    turn, a_first = times_a(turn, 0)

    turn, (a["g"], a["xf"], c["n"], b_mid, b_own, a_in) = after(
        turn, [a_last, a["xf"], c["n"], b_mid, b_own, a_in], inside, (0, 5)
    )
    b["n"] = near(b_own)
    b["x"] = over_x(b_own)
    c["f"] = swap_groups(a["f"])

    turn, (b["n"], b["x"], c["f"]) = after(turn, [b["n"], b["x"], c["f"]], inside)
    b_in = middle(b["n"])
    b_out = outward(b_mid)
    a["xg"] = over_x(a["g"])
    c["g"] = swap_groups(a["g"])
    turn, c_first = times_c(turn, 0)

    turn, (b["f"], b_in, a["xg"], c["g"], b_mid) = after(
        turn, [b_out, b_in, a["xg"], c["g"], b_mid], inside, (0, 4)
    )
    b_last = outward(b_in)
    b["xf"] = over_x(b["f"])
    c["xf"] = swap_groups(a["xf"])
    turn, score_first = times_b(turn, 0, True, spans, (a_first, c_first))

    turn, (b["g"], b["xf"], c["xf"], b_in) = after(turn, [b_last, b["xf"], c["xf"], b_in], inside, (0, 3))
    b["xg"] = over_x(b["g"])
    b["xn"] = near(b["x"])
    c["xn"] = swap_groups(a["xn"])
    turn, a_second = times_a(turn, 1)

    turn, (b["xg"], b["xn"], c["xn"], c["g"]) = after(turn, [b["xg"], b["xn"], c["xn"], c["g"]], inside)
    split = c["g"].shape[0] // 2
    c["top"] = over_x(c["g"][:split])
    c["low"] = swap_groups(a["xg"][split:])
    turn, b_second = times_b(turn, 1)
    groups = (groups[0], ("xf", "g", "xn", "top", "low"))
    turn, score_second = times_c(turn, 1, False, spans, (a_second, b_second))
    sums = [score_first, score_second]

    slots = bucket_ids.shape[0]
    ours = jnp.concatenate([x[:slots] for x in sums], axis=1)
    others = send(jnp.concatenate([x[slots:] for x in sums], axis=1), CORE)
    f_code = jnp.where(at_end, OPPOSITE, ACROSS)
    g_code = jnp.where(at_end, ACROSS, OPPOSITE)
    codes = [0, COLUMN, NEAR, f_code, f_code | COLUMN, g_code, NEAR | COLUMN, g_code | COLUMN]
    codes = jnp.stack([jnp.asarray(code, jnp.int32) for code in codes])
    owner = jnp.concatenate([me ^ codes, me ^ CORE ^ codes])
    query = owner[:, None] * local + jnp.arange(local, dtype=jnp.int32)[None, :]
    query = jnp.repeat(query.reshape(-1), ranks)
    placed = query[None, :] == jnp.arange(count * local, dtype=jnp.int32)[:, None]
    return lax.dot_general(
        placed.astype(jnp.float32),
        jnp.concatenate([ours, others], axis=1),
        (((1,), (1,)), ((), ())),
        precision=lax.Precision.HIGHEST,
        preferred_element_type=jnp.float32,
    )


def solution(mesh):
    sizes = mesh.shape
    fits = sizes["dp"] == 16 and sizes["groups"] == 2 and sizes["tensor"] == 1
    return jax.shard_map(
        relay if fits else gather_whole,
        mesh=mesh,
        in_specs=(
            P(("groups", "dp"), "tensor"),
            P(("groups", "dp"), "tensor"),
            P("dp", None, "tensor"),
            P("dp", None, "tensor"),
            P(("groups", "dp")),
            P(("groups", "dp")),
        ),
        out_specs=P("tensor", ("groups", "dp")),
        check_vma=False,
    )
```

```python
import functools

import jax
import jax.numpy as jnp
from jax import lax
from jax.experimental import pallas as pl
from jax.experimental.pallas import tpu as pltpu
from jax.sharding import PartitionSpec as P

BUCKET = 128


def bucket_lengths(slot_ids):
    return BUCKET * jnp.where(
        slot_ids == 0, 1, jnp.where(slot_ids == 1, 2, jnp.where(slot_ids == 2, 4, 0))
    ).astype(jnp.int32)


def slot_matrix(slot_ids, lengths, positions):
    widths = bucket_lengths(slot_ids)
    starts = jnp.cumsum(widths) - widths
    place = jnp.arange(positions, dtype=jnp.int32)[:, None]
    inside = (place >= starts[None, :]) & (place < starts[None, :] + lengths[None, :])
    return inside.astype(jnp.float32)


def project(acts, factors):
    rows = factors.reshape(-1, factors.shape[2])
    return lax.dot_general(acts, rows, (((1,), (1,)), ((), ())), preferred_element_type=jnp.float32)


def gather_whole(hidden_acts, output_grads, query_left, query_right, bucket_ids, seq_lengths):
    tokens_here = hidden_acts.shape[0]
    rank_count = query_left.shape[1]
    left_all, right_all = (
        lax.all_gather(query_left, "dp", axis=0, tiled=True),
        lax.all_gather(query_right, "dp", axis=0, tiled=True),
    )
    left_proj = project(hidden_acts, left_all)
    right_proj = project(output_grads, right_all)
    queries = left_proj.shape[1] // rank_count
    left_terms = left_proj.reshape(tokens_here, queries, rank_count)
    right_terms = right_proj.reshape(tokens_here, queries, rank_count)
    left_terms, right_terms = lax.psum((left_terms, right_terms), "tensor")
    share_size = queries // lax.axis_size("tensor")
    first_query = lax.axis_index("tensor") * share_size
    left_terms = lax.dynamic_slice_in_dim(left_terms, first_query, share_size, 1)
    right_terms = lax.dynamic_slice_in_dim(right_terms, first_query, share_size, 1)
    token_term = jnp.sum(left_terms * right_terms, axis=2)
    slot_mask = slot_matrix(bucket_ids, seq_lengths, tokens_here)
    return jnp.dot(
        token_term.T, slot_mask, precision=lax.Precision.HIGHEST, preferred_element_type=jnp.float32
    )


CORE, COLUMN, NEAR, ACROSS, OPPOSITE = 1, 2, 4, 12, 8
LITTLE = pl.CostEstimate(flops=1, bytes_accessed=1, transcendentals=0)
VMEM_LIMIT = 63 * 1024 * 1024


def flip(array, code, count):
    return lax.ppermute(array, "dp", [(i, i ^ code) for i in range(count)])


def swap_groups(array):
    return lax.ppermute(array, "groups", [(0, 1), (1, 0)])


PARTS = 4


def after_kernel(count, merge, inside_ref, turn_ref, *refs):
    if merge is None:
        next_ref = refs[-1]
    else:
        refs, (held, arrived, gone) = refs[:-3], refs[-3:]
        arrays, next_ref = refs[-1 - count : -1], refs[-1]
        kept, over = (arrays[i] for i in merge)
        rows = held.shape[0] // PARTS

        @pl.when(inside_ref[0] == 1)
        def _():
            parts = [pl.ds(i * rows, rows) for i in range(PARTS)]
            come = [pltpu.make_async_copy(over.at[p], held.at[p], arrived.at[i]) for i, p in enumerate(parts)]
            go = [pltpu.make_async_copy(held.at[p], kept.at[p], gone.at[i]) for i, p in enumerate(parts)]
            for copy in come:
                copy.start()
            for first, second in zip(come, go):
                first.wait()
                second.start()
            for copy in go:
                copy.wait()

    next_ref[0] = turn_ref[0]


def after(turn, arrays, inside, merge=None, there=()):
    count = len(arrays)
    scratch = []
    if merge is not None:
        kept = arrays[merge[0]]
        scratch = [pltpu.VMEM(kept.shape, kept.dtype)] + [pltpu.SemaphoreType.DMA((PARTS,))] * 2
    hbm = pl.BlockSpec(memory_space=pltpu.HBM)
    scalar = pl.BlockSpec(memory_space=pltpu.SMEM)
    *arrays, turn = pl.pallas_call(
        functools.partial(after_kernel, count, merge),
        out_shape=[jax.ShapeDtypeStruct(x.shape, x.dtype) for x in (*arrays, turn)],
        in_specs=[scalar] * 2 + [hbm] * (len(there) + count),
        out_specs=[hbm] * count + [scalar],
        input_output_aliases={2 + len(there) + i: i for i in range(count)},
        scratch_shapes=scratch,
        compiler_params=pltpu.CompilerParams(vmem_limit_bytes=VMEM_LIMIT),
        cost_estimate=LITTLE,
    )(inside, turn, *there, *arrays)
    return turn, arrays


def lines(array, pairs):
    return lax.ppermute(
        array, "dp", [(a * 4 + rest, b * 4 + rest) for a, b in pairs for rest in range(4)]
    )


def score_into(out_ref, spans_ref, terms_of, rows):
    slots = out_ref.shape[0] // 2
    place = lax.broadcasted_iota(jnp.int32, (rows, 1), 0)
    for part in range(2):
        terms = terms_of(slice(part * rows, (part + 1) * rows))
        for j in range(slots):
            k = part * slots + j
            inside = (place >= spans_ref[0, k]) & (place < spans_ref[1, k])
            out_ref[k : k + 1, :] = jnp.sum(jnp.where(inside, terms, 0.0), axis=0, keepdims=True)


def proj_kernel(count, last, turn_ref, at_ref, own_ref, other_ref, *refs):
    del at_ref
    pieces, refs = refs[:count], refs[count:]
    if last is None:
        acc_ref, next_ref = refs
    else:
        spans_ref, left_ref, second_ref, out_ref, next_ref, acc_ref = refs
    step = pl.program_id(0)
    rows = own_ref.shape[0]

    @pl.when(step == 0)
    def _():
        next_ref[0] = turn_ref[0]
        acc_ref[...] = jnp.zeros_like(acc_ref)

    factors = jnp.concatenate([p[...] for p in pieces], axis=0)
    for part, tokens in enumerate((own_ref, other_ref)):
        acc_ref[part * rows : (part + 1) * rows] += lax.dot_general(
            tokens[...], factors, (((1,), (1,)), ((), ())), preferred_element_type=jnp.float32
        )

    if last is not None:

        @pl.when(step == pl.num_programs(0) - 1)
        def _():
            def terms(here):
                if last:
                    return (left_ref[here] + second_ref[here]) * acc_ref[here]
                return (left_ref[here] + acc_ref[here]) * second_ref[here]

            score_into(out_ref, spans_ref, terms, rows)


def proj(turn, tokens, rows, pieces, first, steps, last=None, spans=None, others=()):
    depth = pieces[0].shape[1]
    block = depth // steps
    held = sum(p.shape[0] for p in pieces)
    (own, own_row), (other, other_row) = tokens
    whole = pl.BlockSpec((2 * rows, held), lambda k, turn, at: (0, 0))
    scalar = pl.BlockSpec(memory_space=pltpu.SMEM)
    if last is None:
        more_specs, more, scratch = [], (), []
        out_shape, out_spec = (2 * rows, held), whole
    else:
        more_specs, more = [scalar, whole, whole], (spans, *others)
        scratch = [pltpu.VMEM((2 * rows, held), jnp.float32)]
        out_shape = (spans.shape[1], held)
        out_spec = pl.BlockSpec(out_shape, lambda k, turn, at: (0, 0))
    out, turn_next = pl.pallas_call(
        functools.partial(proj_kernel, len(pieces), last),
        out_shape=(
            jax.ShapeDtypeStruct(out_shape, jnp.float32),
            jax.ShapeDtypeStruct((1,), jnp.int32),
        ),
        grid_spec=pltpu.PrefetchScalarGridSpec(
            num_scalar_prefetch=2,
            grid=(steps,),
            in_specs=[
                pl.BlockSpec((rows, block), lambda k, turn, at: (at[1], at[0] * steps + k)),
                pl.BlockSpec((rows, block), lambda k, turn, at: (at[2], at[0] * steps + k)),
            ]
            + [pl.BlockSpec((p.shape[0], block), lambda k, turn, at: (0, k)) for p in pieces]
            + more_specs,
            out_specs=(out_spec, scalar),
            scratch_shapes=scratch,
        ),
        compiler_params=pltpu.CompilerParams(vmem_limit_bytes=VMEM_LIMIT),
        cost_estimate=LITTLE,
    )(turn, jnp.concatenate([first, own_row, other_row]), own, other, *pieces, *more)
    return turn_next, out


def own_kernel(lefts, turn_ref, at_ref, acts_ref, grads_ref, left_ref, right_ref, spans_ref, before_ref, *refs):
    out_ref, next_ref, left_acc, right_acc = refs[-4:]
    step = pl.program_id(0)

    def add(acc_ref, tokens_ref, factors_ref):
        acc_ref[...] += lax.dot_general(
            tokens_ref[...], factors_ref[...], (((1,), (1,)), ((), ())), preferred_element_type=jnp.float32
        )

    @pl.when(step == 0)
    def _():
        next_ref[0] = turn_ref[0]
        out_ref[...] = before_ref[...]
        left_acc[...] = jnp.zeros_like(left_acc)
        right_acc[...] = jnp.zeros_like(right_acc)

    @pl.when((at_ref[0] == 1) & (step < lefts))
    def _():
        add(left_acc, acts_ref, left_ref)

    @pl.when((at_ref[0] == 1) & (step >= lefts))
    def _():
        add(right_acc, grads_ref, right_ref)

    @pl.when((at_ref[0] == 1) & (step == pl.num_programs(0) - 1))
    def _():
        terms = left_acc[...] * right_acc[...]
        place = lax.broadcasted_iota(jnp.int32, (terms.shape[0], 1), 0)
        for j in range(out_ref.shape[0]):
            inside = (place >= spans_ref[0, j]) & (place < spans_ref[1, j])
            out_ref[j : j + 1, :] = jnp.sum(jnp.where(inside, terms, 0.0), axis=0, keepdims=True)


def own_scores(turn, works, acts, grads, left, right, spans, before, passed, block=2048):
    lefts, rights = left.shape[1] // block, right.shape[1] // block
    rows, held = acts.shape[0], left.shape[0]
    scalar = pl.BlockSpec(memory_space=pltpu.SMEM)
    hbm = pl.BlockSpec(memory_space=pltpu.HBM)
    small = pl.BlockSpec(before.shape, lambda k, turn, at: (0, 0))

    def at_left(k, turn, at):
        return (0, at[0] * jnp.minimum(k, lefts - 1))

    def at_right(k, turn, at):
        return (0, at[0] * jnp.maximum(k - lefts, 0))

    *passed, out, turn = pl.pallas_call(
        functools.partial(own_kernel, lefts),
        out_shape=[jax.ShapeDtypeStruct(x.shape, x.dtype) for x in (*passed, before, turn)],
        grid_spec=pltpu.PrefetchScalarGridSpec(
            num_scalar_prefetch=2,
            grid=(lefts + rights,),
            in_specs=[
                pl.BlockSpec((rows, block), at_left),
                pl.BlockSpec((rows, block), at_right),
                pl.BlockSpec((held, block), at_left),
                pl.BlockSpec((held, block), at_right),
                scalar,
                small,
            ]
            + [hbm] * len(passed),
            out_specs=[hbm] * len(passed) + [small, scalar],
            scratch_shapes=[pltpu.VMEM((rows, held), jnp.float32)] * 2,
        ),
        input_output_aliases={8 + i: i for i in range(len(passed))},
        compiler_params=pltpu.CompilerParams(vmem_limit_bytes=VMEM_LIMIT),
        cost_estimate=LITTLE,
    )(turn, works, acts, grads, left, right, spans, before, *passed)
    return turn, out, passed


def spans_of(slot_ids, lengths):
    widths = bucket_lengths(slot_ids)
    starts = jnp.cumsum(widths) - widths
    return jnp.stack([starts, starts + lengths]).astype(jnp.int32)


def relay(hidden_acts, output_grads, query_left, query_right, bucket_ids, seq_lengths):
    count = lax.axis_size("dp")
    me, group = lax.axis_index("dp"), lax.axis_index("groups")
    z = me // 4
    local, ranks = query_left.shape[:2]
    left = query_left.reshape(local * ranks, -1)
    half = left.shape[1] // 2
    send = functools.partial(flip, count=count)

    acts_there = send(hidden_acts, CORE)
    grads_there = send(output_grads, CORE)
    spans_here = spans_of(bucket_ids, seq_lengths)
    spans = jnp.concatenate([spans_here, send(spans_here, CORE)], axis=1)

    a, b, c = {}, {}, {}
    a["own"] = lax.dynamic_slice_in_dim(left, group * half, half, 1)
    b["own"] = query_right.reshape(local * ranks, -1)
    at_end = (z == 0) | (z == 3)

    def near(piece):
        return send(piece, NEAR)

    def middle(piece):
        return lines(piece, [(1, 2), (2, 1)])

    def outward(piece):
        return lines(piece, [(1, 0), (2, 3)])

    def over_x(piece):
        return send(piece, COLUMN)

    inside = (~at_end).reshape(1).astype(jnp.int32)
    mine = jnp.reshape(group, (1,)).astype(jnp.int32)
    zero = jnp.zeros((1,), jnp.int32)
    acts = ((hidden_acts, zero), (acts_there, zero))
    grads = ((output_grads, zero), (grads_there, zero))
    groups = (("x", "n", "f"), ("xf", "g", "xn", "xg"))
    tokens_here = hidden_acts.shape[0]
    steps = 4

    def times_a(turn, k):
        return proj(turn, acts, tokens_here, [a[i] for i in groups[k]], mine, steps)

    def times_c(turn, k, *score):
        return proj(turn, acts, tokens_here, [c[i] for i in groups[k]], 1 - mine, steps, *score)

    def times_b(turn, k, *score):
        return proj(turn, grads, tokens_here, [b[i] for i in groups[k]], zero, steps, *score)

    core = (me & CORE).reshape(1).astype(jnp.int32)
    none = jnp.zeros((bucket_ids.shape[0], local * ranks), jnp.float32)
    here = (hidden_acts, output_grads, left, b["own"], spans_here)
    turn, own_first, (a["own"],) = own_scores(zero, core, *here, none, [a["own"]])

    a["x"] = over_x(a["own"])
    a["n"] = near(a["own"])
    a_mid = middle(a["own"])

    turn, own_first, _ = own_scores(turn, 1 - core, *here, own_first, [])
    turn, (a["x"], a["n"], a_mid) = after(turn, [a["x"], a["n"], a_mid], inside, None, [acts_there])
    a_in = middle(a["n"])
    a_out = outward(a_mid)
    a["xn"] = over_x(a["n"])
    c["x"] = swap_groups(a["x"])

    turn, (a["f"], a_in, a["xn"], c["x"], b_own, a_mid) = after(
        turn, [a_out, a_in, a["xn"], c["x"], b["own"], a_mid], inside, (0, 5), [grads_there]
    )
    a_last = outward(a_in)
    a["xf"] = over_x(a["f"])
    c["n"] = swap_groups(a["n"])
    b_mid = middle(b_own)
    turn, a_first = times_a(turn, 0)

    turn, (a["g"], a["xf"], c["n"], b_mid, b_own, a_in) = after(
        turn, [a_last, a["xf"], c["n"], b_mid, b_own, a_in], inside, (0, 5)
    )
    b["n"] = near(b_own)
    b["x"] = over_x(b_own)
    c["f"] = swap_groups(a["f"])
    there = (acts_there, grads_there, left, b["own"], spans[:, bucket_ids.shape[0] :])
    turn, own_second, _ = own_scores(turn, zero + 1, *there, none, [])

    turn, (b["n"], b["x"], c["f"]) = after(turn, [b["n"], b["x"], c["f"]], inside)
    b_in = middle(b["n"])
    b_out = outward(b_mid)
    a["xg"] = over_x(a["g"])
    c["g"] = swap_groups(a["g"])
    turn, c_first = times_c(turn, 0)

    turn, (b["f"], b_in, a["xg"], c["g"], b_mid) = after(
        turn, [b_out, b_in, a["xg"], c["g"], b_mid], inside, (0, 4)
    )
    b_last = outward(b_in)
    b["xf"] = over_x(b["f"])
    c["xf"] = swap_groups(a["xf"])
    turn, score_first = times_b(turn, 0, True, spans, (a_first, c_first))

    turn, (b["g"], b["xf"], c["xf"], b_in) = after(turn, [b_last, b["xf"], c["xf"], b_in], inside, (0, 3))
    b["xg"] = over_x(b["g"])
    b["xn"] = near(b["x"])
    c["xn"] = swap_groups(a["xn"])
    turn, a_second = times_a(turn, 1)

    turn, (b["xg"], b["xn"], c["xn"], c["g"]) = after(turn, [b["xg"], b["xn"], c["xn"], c["g"]], inside)
    split = c["g"].shape[0] // 2
    c["top"] = over_x(c["g"][:split])
    c["low"] = swap_groups(a["xg"][split:])
    turn, b_second = times_b(turn, 1)
    groups = (groups[0], ("xf", "g", "xn", "top", "low"))
    turn, score_second = times_c(turn, 1, False, spans, (a_second, b_second))
    sums = [score_first, score_second]

    slots = bucket_ids.shape[0]
    ours = jnp.concatenate([own_first] + [x[:slots] for x in sums], axis=1)
    others = send(jnp.concatenate([own_second] + [x[slots:] for x in sums], axis=1), CORE)
    f_code = jnp.where(at_end, OPPOSITE, ACROSS)
    g_code = jnp.where(at_end, ACROSS, OPPOSITE)
    codes = [0, COLUMN, NEAR, f_code, f_code | COLUMN, g_code, NEAR | COLUMN, g_code | COLUMN]
    codes = jnp.stack([jnp.asarray(code, jnp.int32) for code in codes])
    owner = jnp.concatenate([me ^ codes, me ^ CORE ^ codes])
    query = owner[:, None] * local + jnp.arange(local, dtype=jnp.int32)[None, :]
    query = jnp.repeat(query.reshape(-1), ranks)
    placed = query[None, :] == jnp.arange(count * local, dtype=jnp.int32)[:, None]
    return lax.dot_general(
        placed.astype(jnp.float32),
        jnp.concatenate([ours, others], axis=1),
        (((1,), (1,)), ((), ())),
        precision=lax.Precision.HIGHEST,
        preferred_element_type=jnp.float32,
    )


def solution(mesh):
    sizes = mesh.shape
    fits = sizes["dp"] == 16 and sizes["groups"] == 2 and sizes["tensor"] == 1
    return jax.shard_map(
        relay if fits else gather_whole,
        mesh=mesh,
        in_specs=(
            P(("groups", "dp"), "tensor"),
            P(("groups", "dp"), "tensor"),
            P("dp", None, "tensor"),
            P("dp", None, "tensor"),
            P(("groups", "dp")),
            P(("groups", "dp")),
        ),
        out_specs=P("tensor", ("groups", "dp")),
        check_vma=False,
    )
```

```python
import functools

import jax
import jax.numpy as jnp
from jax import lax
from jax.experimental import pallas as pl
from jax.experimental.pallas import tpu as pltpu
from jax.sharding import PartitionSpec as P

BUCKET = 128


def bucket_lengths(slot_ids):
    return BUCKET * jnp.where(
        slot_ids == 0, 1, jnp.where(slot_ids == 1, 2, jnp.where(slot_ids == 2, 4, 0))
    ).astype(jnp.int32)


def slot_matrix(slot_ids, lengths, positions):
    widths = bucket_lengths(slot_ids)
    starts = jnp.cumsum(widths) - widths
    place = jnp.arange(positions, dtype=jnp.int32)[:, None]
    inside = (place >= starts[None, :]) & (place < starts[None, :] + lengths[None, :])
    return inside.astype(jnp.float32)


def project(acts, factors):
    rows = factors.reshape(-1, factors.shape[2])
    return lax.dot_general(acts, rows, (((1,), (1,)), ((), ())), preferred_element_type=jnp.float32)


def gather_whole(hidden_acts, output_grads, query_left, query_right, bucket_ids, seq_lengths):
    tokens_here = hidden_acts.shape[0]
    rank_count = query_left.shape[1]
    left_all, right_all = (
        lax.all_gather(query_left, "dp", axis=0, tiled=True),
        lax.all_gather(query_right, "dp", axis=0, tiled=True),
    )
    left_proj = project(hidden_acts, left_all)
    right_proj = project(output_grads, right_all)
    queries = left_proj.shape[1] // rank_count
    left_terms = left_proj.reshape(tokens_here, queries, rank_count)
    right_terms = right_proj.reshape(tokens_here, queries, rank_count)
    left_terms, right_terms = lax.psum((left_terms, right_terms), "tensor")
    share_size = queries // lax.axis_size("tensor")
    first_query = lax.axis_index("tensor") * share_size
    left_terms = lax.dynamic_slice_in_dim(left_terms, first_query, share_size, 1)
    right_terms = lax.dynamic_slice_in_dim(right_terms, first_query, share_size, 1)
    token_term = jnp.sum(left_terms * right_terms, axis=2)
    slot_mask = slot_matrix(bucket_ids, seq_lengths, tokens_here)
    return jnp.dot(
        token_term.T, slot_mask, precision=lax.Precision.HIGHEST, preferred_element_type=jnp.float32
    )


CORE, COLUMN, NEAR, ACROSS, OPPOSITE = 1, 2, 4, 12, 8
LITTLE = pl.CostEstimate(flops=1, bytes_accessed=1, transcendentals=0)
VMEM_LIMIT = 63 * 1024 * 1024


def flip(array, code, count):
    return lax.ppermute(array, "dp", [(i, i ^ code) for i in range(count)])


def swap_groups(array):
    return lax.ppermute(array, "groups", [(0, 1), (1, 0)])


PARTS = 4


def after_kernel(count, merge, inside_ref, turn_ref, *refs):
    if merge is None:
        next_ref = refs[-1]
    else:
        refs, (held, arrived, gone) = refs[:-3], refs[-3:]
        arrays, next_ref = refs[-1 - count : -1], refs[-1]
        kept, over = (arrays[i] for i in merge)
        rows = held.shape[0] // PARTS

        @pl.when(inside_ref[0] == 1)
        def _():
            parts = [pl.ds(i * rows, rows) for i in range(PARTS)]
            come = [pltpu.make_async_copy(over.at[p], held.at[p], arrived.at[i]) for i, p in enumerate(parts)]
            go = [pltpu.make_async_copy(held.at[p], kept.at[p], gone.at[i]) for i, p in enumerate(parts)]
            for copy in come:
                copy.start()
            for first, second in zip(come, go):
                first.wait()
                second.start()
            for copy in go:
                copy.wait()

    next_ref[0] = turn_ref[0]


def after(turn, arrays, inside, merge=None, there=()):
    count = len(arrays)
    scratch = []
    if merge is not None:
        kept = arrays[merge[0]]
        scratch = [pltpu.VMEM(kept.shape, kept.dtype)] + [pltpu.SemaphoreType.DMA((PARTS,))] * 2
    hbm = pl.BlockSpec(memory_space=pltpu.HBM)
    scalar = pl.BlockSpec(memory_space=pltpu.SMEM)
    *arrays, turn = pl.pallas_call(
        functools.partial(after_kernel, count, merge),
        out_shape=[jax.ShapeDtypeStruct(x.shape, x.dtype) for x in (*arrays, turn)],
        in_specs=[scalar] * 2 + [hbm] * (len(there) + count),
        out_specs=[hbm] * count + [scalar],
        input_output_aliases={2 + len(there) + i: i for i in range(count)},
        scratch_shapes=scratch,
        compiler_params=pltpu.CompilerParams(vmem_limit_bytes=VMEM_LIMIT),
        cost_estimate=LITTLE,
    )(inside, turn, *there, *arrays)
    return turn, arrays


def lines(array, pairs):
    return lax.ppermute(
        array, "dp", [(a * 4 + rest, b * 4 + rest) for a, b in pairs for rest in range(4)]
    )


def score_into(out_ref, spans_ref, terms_of, rows):
    slots = out_ref.shape[0] // 2
    place = lax.broadcasted_iota(jnp.int32, (rows, 1), 0)
    for part in range(2):
        terms = terms_of(slice(part * rows, (part + 1) * rows))
        for j in range(slots):
            k = part * slots + j
            inside = (place >= spans_ref[0, k]) & (place < spans_ref[1, k])
            out_ref[k : k + 1, :] = jnp.sum(jnp.where(inside, terms, 0.0), axis=0, keepdims=True)


def proj_kernel(count, last, turn_ref, at_ref, own_ref, other_ref, *refs):
    del at_ref
    pieces, refs = refs[:count], refs[count:]
    if last is None:
        acc_ref, next_ref = refs
    else:
        spans_ref, left_ref, second_ref, out_ref, next_ref, acc_ref = refs
    step = pl.program_id(0)
    rows = own_ref.shape[0]

    @pl.when(step == 0)
    def _():
        next_ref[0] = turn_ref[0]
        acc_ref[...] = jnp.zeros_like(acc_ref)

    factors = jnp.concatenate([p[...] for p in pieces], axis=0)
    for part, tokens in enumerate((own_ref, other_ref)):
        acc_ref[part * rows : (part + 1) * rows] += lax.dot_general(
            tokens[...], factors, (((1,), (1,)), ((), ())), preferred_element_type=jnp.float32
        )

    if last is not None:

        @pl.when(step == pl.num_programs(0) - 1)
        def _():
            def terms(here):
                if last:
                    return (left_ref[here] + second_ref[here]) * acc_ref[here]
                return (left_ref[here] + acc_ref[here]) * second_ref[here]

            score_into(out_ref, spans_ref, terms, rows)


def proj(turn, tokens, rows, pieces, first, steps, last=None, spans=None, others=()):
    depth = pieces[0].shape[1]
    block = depth // steps
    held = sum(p.shape[0] for p in pieces)
    (own, own_row), (other, other_row) = tokens
    whole = pl.BlockSpec((2 * rows, held), lambda k, turn, at: (0, 0))
    scalar = pl.BlockSpec(memory_space=pltpu.SMEM)
    if last is None:
        more_specs, more, scratch = [], (), []
        out_shape, out_spec = (2 * rows, held), whole
    else:
        more_specs, more = [scalar, whole, whole], (spans, *others)
        scratch = [pltpu.VMEM((2 * rows, held), jnp.float32)]
        out_shape = (spans.shape[1], held)
        out_spec = pl.BlockSpec(out_shape, lambda k, turn, at: (0, 0))
    out, turn_next = pl.pallas_call(
        functools.partial(proj_kernel, len(pieces), last),
        out_shape=(
            jax.ShapeDtypeStruct(out_shape, jnp.float32),
            jax.ShapeDtypeStruct((1,), jnp.int32),
        ),
        grid_spec=pltpu.PrefetchScalarGridSpec(
            num_scalar_prefetch=2,
            grid=(steps,),
            in_specs=[
                pl.BlockSpec((rows, block), lambda k, turn, at: (at[1], at[0] * steps + k)),
                pl.BlockSpec((rows, block), lambda k, turn, at: (at[2], at[0] * steps + k)),
            ]
            + [pl.BlockSpec((p.shape[0], block), lambda k, turn, at: (0, k)) for p in pieces]
            + more_specs,
            out_specs=(out_spec, scalar),
            scratch_shapes=scratch,
        ),
        compiler_params=pltpu.CompilerParams(vmem_limit_bytes=VMEM_LIMIT),
        cost_estimate=LITTLE,
    )(turn, jnp.concatenate([first, own_row, other_row]), own, other, *pieces, *more)
    return turn_next, out


def own_kernel(lefts, turn_ref, at_ref, acts_ref, grads_ref, left_ref, right_ref, spans_ref, before_ref, *refs):
    out_ref, next_ref, left_acc, right_acc = refs[-4:]
    step = pl.program_id(0)

    def add(acc_ref, tokens_ref, factors_ref):
        acc_ref[...] += lax.dot_general(
            tokens_ref[...], factors_ref[...], (((1,), (1,)), ((), ())), preferred_element_type=jnp.float32
        )

    @pl.when(step == 0)
    def _():
        next_ref[0] = turn_ref[0]
        out_ref[...] = before_ref[...]
        left_acc[...] = jnp.zeros_like(left_acc)
        right_acc[...] = jnp.zeros_like(right_acc)

    @pl.when((at_ref[0] == 1) & (step < lefts))
    def _():
        add(left_acc, acts_ref, left_ref)

    @pl.when((at_ref[0] == 1) & (step >= lefts))
    def _():
        add(right_acc, grads_ref, right_ref)

    @pl.when((at_ref[0] == 1) & (step == pl.num_programs(0) - 1))
    def _():
        terms = left_acc[...] * right_acc[...]
        place = lax.broadcasted_iota(jnp.int32, (terms.shape[0], 1), 0)
        for j in range(out_ref.shape[0]):
            inside = (place >= spans_ref[0, j]) & (place < spans_ref[1, j])
            out_ref[j : j + 1, :] = jnp.sum(jnp.where(inside, terms, 0.0), axis=0, keepdims=True)


def own_scores(turn, works, acts, grads, left, right, spans, before, passed, block=2048):
    lefts, rights = left.shape[1] // block, right.shape[1] // block
    rows, held = acts.shape[0], left.shape[0]
    scalar = pl.BlockSpec(memory_space=pltpu.SMEM)
    hbm = pl.BlockSpec(memory_space=pltpu.HBM)
    small = pl.BlockSpec(before.shape, lambda k, turn, at: (0, 0))

    def at_left(k, turn, at):
        return (0, at[0] * jnp.minimum(k, lefts - 1))

    def at_right(k, turn, at):
        return (0, at[0] * jnp.maximum(k - lefts, 0))

    *passed, out, turn = pl.pallas_call(
        functools.partial(own_kernel, lefts),
        out_shape=[jax.ShapeDtypeStruct(x.shape, x.dtype) for x in (*passed, before, turn)],
        grid_spec=pltpu.PrefetchScalarGridSpec(
            num_scalar_prefetch=2,
            grid=(lefts + rights,),
            in_specs=[
                pl.BlockSpec((rows, block), at_left),
                pl.BlockSpec((rows, block), at_right),
                pl.BlockSpec((held, block), at_left),
                pl.BlockSpec((held, block), at_right),
                scalar,
                small,
            ]
            + [hbm] * len(passed),
            out_specs=[hbm] * len(passed) + [small, scalar],
            scratch_shapes=[pltpu.VMEM((rows, held), jnp.float32)] * 2,
        ),
        input_output_aliases={8 + i: i for i in range(len(passed))},
        compiler_params=pltpu.CompilerParams(vmem_limit_bytes=VMEM_LIMIT),
        cost_estimate=LITTLE,
    )(turn, works, acts, grads, left, right, spans, before, *passed)
    return turn, out, passed


def spans_of(slot_ids, lengths):
    widths = bucket_lengths(slot_ids)
    starts = jnp.cumsum(widths) - widths
    return jnp.stack([starts, starts + lengths]).astype(jnp.int32)


def relay(hidden_acts, output_grads, query_left, query_right, bucket_ids, seq_lengths):
    count = lax.axis_size("dp")
    me, group = lax.axis_index("dp"), lax.axis_index("groups")
    z = me // 4
    local, ranks = query_left.shape[:2]
    left = query_left.reshape(local * ranks, -1)
    half = left.shape[1] // 2
    send = functools.partial(flip, count=count)

    acts_there = send(hidden_acts, CORE)
    spans_here = spans_of(bucket_ids, seq_lengths)
    spans = jnp.concatenate([spans_here, send(spans_here, CORE)], axis=1)

    a, b, c = {}, {}, {}
    a["own"] = lax.dynamic_slice_in_dim(left, group * half, half, 1)
    b["own"] = query_right.reshape(local * ranks, -1)
    at_end = (z == 0) | (z == 3)

    def near(piece):
        return send(piece, NEAR)

    def middle(piece):
        return lines(piece, [(1, 2), (2, 1)])

    def outward(piece):
        return lines(piece, [(1, 0), (2, 3)])

    def inward(piece):
        return lines(piece, [(0, 1), (3, 2)])

    def over_x(piece):
        return send(piece, COLUMN)

    inside = (~at_end).reshape(1).astype(jnp.int32)
    mine = jnp.reshape(group, (1,)).astype(jnp.int32)
    zero = jnp.zeros((1,), jnp.int32)
    acts = ((hidden_acts, zero), (acts_there, zero))
    groups = (("x", "n", "f"), ("xf", "g", "xn", "xg"))
    tokens_here = hidden_acts.shape[0]
    steps = 4

    def times_a(turn, k):
        return proj(turn, acts, tokens_here, [a[i] for i in groups[k]], mine, steps)

    def times_c(turn, k, *score):
        return proj(turn, acts, tokens_here, [c[i] for i in groups[k]], 1 - mine, steps, *score)

    def times_b(turn, k, *score):
        return proj(turn, grads, tokens_here, [b[i] for i in groups[k]], zero, steps, *score)

    none = jnp.zeros((bucket_ids.shape[0], local * ranks), jnp.float32)
    one = zero + 1

    a["x"] = over_x(a["own"])
    a["n"] = near(a["own"])
    a_mid = middle(a["own"])
    turn, own_first, _ = own_scores(
        zero, one, hidden_acts, output_grads, left, b["own"], spans_here, none, []
    )

    turn, (a["x"], a["n"], a_mid, b_own) = after(
        turn, [a["x"], a["n"], a_mid, b["own"]], inside, None, [acts_there]
    )
    b["x"] = over_x(b_own)
    a_out = outward(a_mid)
    a_in = middle(a["n"])
    c["x"] = swap_groups(a["x"])
    grads_there = send(output_grads, CORE)
    grads = ((output_grads, zero), (grads_there, zero))

    turn, (a["f"], a_in, c["x"], a_mid, b["x"], b_own) = after(
        turn, [a_out, a_in, c["x"], a_mid, b["x"], b_own], inside, (0, 3), [grads_there]
    )
    a_last = outward(a_in)
    a["xn"] = over_x(a["n"])
    a["xf"] = over_x(a["f"])
    b_mid = middle(b_own)
    c["n"] = swap_groups(a["n"])
    turn, a_first = times_a(turn, 0)

    turn, (a["g"], a["xn"], b_mid, c["n"], a_in, b_own) = after(
        turn, [a_last, a["xn"], b_mid, c["n"], a_in, b_own], inside, (0, 4)
    )
    b_out = outward(b_mid)
    a["xg"] = over_x(a["g"])
    b_near = inward(b_own)
    c["f"] = swap_groups(a["f"])
    there = (acts_there, grads_there, left, b["own"], spans[:, bucket_ids.shape[0] :])
    turn, own_second, _ = own_scores(turn, one, *there, none, [])

    turn, (b["f"], a["xf"], b_near, c["f"], b_mid, b_own) = after(
        turn, [b_out, a["xf"], b_near, c["f"], b_mid, b_own], inside, (0, 4)
    )
    b_in = middle(b_near)
    b_far = outward(b_own)
    b["xf"] = over_x(b["f"])
    c["g"] = swap_groups(a["g"])
    turn, c_first = times_c(turn, 0)

    turn, (b["n"], b_in, a["xg"], c["g"], b_near) = after(
        turn, [b_far, b_in, a["xg"], c["g"], b_near], inside, (0, 4)
    )
    b_last = outward(b_in)
    c["xn"] = swap_groups(a["xn"])
    c["xf"] = swap_groups(a["xf"])
    turn, a_second = times_a(turn, 1)

    split = c["g"].shape[0] // 2
    turn, (b["g"], b["xf"], c["xn"], b_in, b_over) = after(
        turn, [b_last, b["xf"], c["xn"], b_in, b["x"]], inside, (0, 3)
    )
    b["x"] = b_over
    b["xg"] = over_x(b["g"])
    b["xn"] = near(b_over)
    c["top"] = over_x(c["g"][:split])
    c["low"] = swap_groups(a["xg"][split:])
    turn, score_first = times_b(turn, 0, True, spans, (a_first, c_first))

    turn, (b["xg"], b["xn"], c["xf"]) = after(turn, [b["xg"], b["xn"], c["xf"]], inside)
    turn, b_second = times_b(turn, 1)
    groups = (groups[0], ("xf", "g", "xn", "top", "low"))
    turn, score_second = times_c(turn, 1, False, spans, (a_second, b_second))
    sums = [score_first, score_second]

    slots = bucket_ids.shape[0]
    ours = jnp.concatenate([own_first] + [x[:slots] for x in sums], axis=1)
    others = send(jnp.concatenate([own_second] + [x[slots:] for x in sums], axis=1), CORE)
    f_code = jnp.where(at_end, OPPOSITE, ACROSS)
    g_code = jnp.where(at_end, ACROSS, OPPOSITE)
    codes = [0, COLUMN, NEAR, f_code, f_code | COLUMN, g_code, NEAR | COLUMN, g_code | COLUMN]
    codes = jnp.stack([jnp.asarray(code, jnp.int32) for code in codes])
    owner = jnp.concatenate([me ^ codes, me ^ CORE ^ codes])
    query = owner[:, None] * local + jnp.arange(local, dtype=jnp.int32)[None, :]
    query = jnp.repeat(query.reshape(-1), ranks)
    placed = query[None, :] == jnp.arange(count * local, dtype=jnp.int32)[:, None]
    return lax.dot_general(
        placed.astype(jnp.float32),
        jnp.concatenate([ours, others], axis=1),
        (((1,), (1,)), ((), ())),
        precision=lax.Precision.HIGHEST,
        preferred_element_type=jnp.float32,
    )


def solution(mesh):
    sizes = mesh.shape
    fits = sizes["dp"] == 16 and sizes["groups"] == 2 and sizes["tensor"] == 1
    return jax.shard_map(
        relay if fits else gather_whole,
        mesh=mesh,
        in_specs=(
            P(("groups", "dp"), "tensor"),
            P(("groups", "dp"), "tensor"),
            P("dp", None, "tensor"),
            P("dp", None, "tensor"),
            P(("groups", "dp")),
            P(("groups", "dp")),
        ),
        out_specs=P("tensor", ("groups", "dp")),
        check_vma=False,
    )
```

```python
import functools

import jax
import jax.numpy as jnp
from jax import lax
from jax.experimental import pallas as pl
from jax.experimental.pallas import tpu as pltpu
from jax.sharding import PartitionSpec as P

BUCKET = 128


def bucket_lengths(slot_ids):
    return BUCKET * jnp.where(
        slot_ids == 0, 1, jnp.where(slot_ids == 1, 2, jnp.where(slot_ids == 2, 4, 0))
    ).astype(jnp.int32)


def slot_matrix(slot_ids, lengths, positions):
    widths = bucket_lengths(slot_ids)
    starts = jnp.cumsum(widths) - widths
    place = jnp.arange(positions, dtype=jnp.int32)[:, None]
    inside = (place >= starts[None, :]) & (place < starts[None, :] + lengths[None, :])
    return inside.astype(jnp.float32)


def project(acts, factors):
    rows = factors.reshape(-1, factors.shape[2])
    return lax.dot_general(acts, rows, (((1,), (1,)), ((), ())), preferred_element_type=jnp.float32)


def gather_whole(hidden_acts, output_grads, query_left, query_right, bucket_ids, seq_lengths):
    tokens_here = hidden_acts.shape[0]
    rank_count = query_left.shape[1]
    left_all, right_all = (
        lax.all_gather(query_left, "dp", axis=0, tiled=True),
        lax.all_gather(query_right, "dp", axis=0, tiled=True),
    )
    left_proj = project(hidden_acts, left_all)
    right_proj = project(output_grads, right_all)
    queries = left_proj.shape[1] // rank_count
    left_terms = left_proj.reshape(tokens_here, queries, rank_count)
    right_terms = right_proj.reshape(tokens_here, queries, rank_count)
    left_terms, right_terms = lax.psum((left_terms, right_terms), "tensor")
    share_size = queries // lax.axis_size("tensor")
    first_query = lax.axis_index("tensor") * share_size
    left_terms = lax.dynamic_slice_in_dim(left_terms, first_query, share_size, 1)
    right_terms = lax.dynamic_slice_in_dim(right_terms, first_query, share_size, 1)
    token_term = jnp.sum(left_terms * right_terms, axis=2)
    slot_mask = slot_matrix(bucket_ids, seq_lengths, tokens_here)
    return jnp.dot(
        token_term.T, slot_mask, precision=lax.Precision.HIGHEST, preferred_element_type=jnp.float32
    )


CORE, COLUMN, NEAR, ACROSS, OPPOSITE = 1, 2, 4, 12, 8
LITTLE = pl.CostEstimate(flops=1, bytes_accessed=1, transcendentals=0)
VMEM_LIMIT = 63 * 1024 * 1024


def flip(array, code, count):
    return lax.ppermute(array, "dp", [(i, i ^ code) for i in range(count)])


def swap_groups(array):
    return lax.ppermute(array, "groups", [(0, 1), (1, 0)])


PARTS = 4


def after_kernel(count, merge, inside_ref, turn_ref, *refs):
    if merge is None:
        next_ref = refs[-1]
    else:
        refs, (held, arrived, gone) = refs[:-3], refs[-3:]
        arrays, next_ref = refs[-1 - count : -1], refs[-1]
        kept, over = (arrays[i] for i in merge)
        rows = held.shape[0] // PARTS

        @pl.when(inside_ref[0] == 1)
        def _():
            parts = [pl.ds(i * rows, rows) for i in range(PARTS)]
            come = [pltpu.make_async_copy(over.at[p], held.at[p], arrived.at[i]) for i, p in enumerate(parts)]
            go = [pltpu.make_async_copy(held.at[p], kept.at[p], gone.at[i]) for i, p in enumerate(parts)]
            for copy in come:
                copy.start()
            for first, second in zip(come, go):
                first.wait()
                second.start()
            for copy in go:
                copy.wait()

    next_ref[0] = turn_ref[0]


def after(turn, arrays, inside, merge=None, there=()):
    count = len(arrays)
    scratch = []
    if merge is not None:
        kept = arrays[merge[0]]
        scratch = [pltpu.VMEM(kept.shape, kept.dtype)] + [pltpu.SemaphoreType.DMA((PARTS,))] * 2
    hbm = pl.BlockSpec(memory_space=pltpu.HBM)
    scalar = pl.BlockSpec(memory_space=pltpu.SMEM)
    *arrays, turn = pl.pallas_call(
        functools.partial(after_kernel, count, merge),
        out_shape=[jax.ShapeDtypeStruct(x.shape, x.dtype) for x in (*arrays, turn)],
        in_specs=[scalar] * 2 + [hbm] * (len(there) + count),
        out_specs=[hbm] * count + [scalar],
        input_output_aliases={2 + len(there) + i: i for i in range(count)},
        scratch_shapes=scratch,
        compiler_params=pltpu.CompilerParams(vmem_limit_bytes=VMEM_LIMIT),
        cost_estimate=LITTLE,
    )(inside, turn, *there, *arrays)
    return turn, arrays


def lines(array, pairs):
    return lax.ppermute(
        array, "dp", [(a * 4 + rest, b * 4 + rest) for a, b in pairs for rest in range(4)]
    )


def score_into(out_ref, spans_ref, terms_of, rows):
    slots = out_ref.shape[0] // 2
    place = lax.broadcasted_iota(jnp.int32, (rows, 1), 0)
    for part in range(2):
        terms = terms_of(slice(part * rows, (part + 1) * rows))
        for j in range(slots):
            k = part * slots + j
            inside = (place >= spans_ref[0, k]) & (place < spans_ref[1, k])
            out_ref[k : k + 1, :] = jnp.sum(jnp.where(inside, terms, 0.0), axis=0, keepdims=True)


def proj_kernel(count, last, turn_ref, at_ref, own_ref, other_ref, *refs):
    del at_ref
    pieces, refs = refs[:count], refs[count:]
    if last is None:
        acc_ref, next_ref = refs
    else:
        spans_ref, left_ref, second_ref, out_ref, next_ref, acc_ref = refs
    step = pl.program_id(0)
    rows = own_ref.shape[0]

    @pl.when(step == 0)
    def _():
        next_ref[0] = turn_ref[0]
        acc_ref[...] = jnp.zeros_like(acc_ref)

    factors = jnp.concatenate([p[...] for p in pieces], axis=0)
    for part, tokens in enumerate((own_ref, other_ref)):
        acc_ref[part * rows : (part + 1) * rows] += lax.dot_general(
            tokens[...], factors, (((1,), (1,)), ((), ())), preferred_element_type=jnp.float32
        )

    if last is not None:

        @pl.when(step == pl.num_programs(0) - 1)
        def _():
            def terms(here):
                if last:
                    return (left_ref[here] + second_ref[here]) * acc_ref[here]
                return (left_ref[here] + acc_ref[here]) * second_ref[here]

            score_into(out_ref, spans_ref, terms, rows)


def proj(turn, tokens, rows, pieces, first, steps, last=None, spans=None, others=()):
    depth = pieces[0].shape[1]
    block = depth // steps
    held = sum(p.shape[0] for p in pieces)
    (own, own_row), (other, other_row) = tokens
    whole = pl.BlockSpec((2 * rows, held), lambda k, turn, at: (0, 0))
    scalar = pl.BlockSpec(memory_space=pltpu.SMEM)
    if last is None:
        more_specs, more, scratch = [], (), []
        out_shape, out_spec = (2 * rows, held), whole
    else:
        more_specs, more = [scalar, whole, whole], (spans, *others)
        scratch = [pltpu.VMEM((2 * rows, held), jnp.float32)]
        out_shape = (spans.shape[1], held)
        out_spec = pl.BlockSpec(out_shape, lambda k, turn, at: (0, 0))
    out, turn_next = pl.pallas_call(
        functools.partial(proj_kernel, len(pieces), last),
        out_shape=(
            jax.ShapeDtypeStruct(out_shape, jnp.float32),
            jax.ShapeDtypeStruct((1,), jnp.int32),
        ),
        grid_spec=pltpu.PrefetchScalarGridSpec(
            num_scalar_prefetch=2,
            grid=(steps,),
            in_specs=[
                pl.BlockSpec((rows, block), lambda k, turn, at: (at[1], at[0] * steps + k)),
                pl.BlockSpec((rows, block), lambda k, turn, at: (at[2], at[0] * steps + k)),
            ]
            + [pl.BlockSpec((p.shape[0], block), lambda k, turn, at: (0, k)) for p in pieces]
            + more_specs,
            out_specs=(out_spec, scalar),
            scratch_shapes=scratch,
        ),
        compiler_params=pltpu.CompilerParams(vmem_limit_bytes=VMEM_LIMIT),
        cost_estimate=LITTLE,
    )(turn, jnp.concatenate([first, own_row, other_row]), own, other, *pieces, *more)
    return turn_next, out


def spans_of(slot_ids, lengths):
    widths = bucket_lengths(slot_ids)
    starts = jnp.cumsum(widths) - widths
    return jnp.stack([starts, starts + lengths]).astype(jnp.int32)


def relay(hidden_acts, output_grads, query_left, query_right, bucket_ids, seq_lengths):
    count = lax.axis_size("dp")
    me, group = lax.axis_index("dp"), lax.axis_index("groups")
    z = me // 4
    local, ranks = query_left.shape[:2]
    left = query_left.reshape(local * ranks, -1)
    half = left.shape[1] // 2
    send = functools.partial(flip, count=count)

    acts_there = send(hidden_acts, CORE)
    spans_here = spans_of(bucket_ids, seq_lengths)
    spans = jnp.concatenate([spans_here, send(spans_here, CORE)], axis=1)

    a, b, c = {}, {}, {}
    a["own"] = lax.dynamic_slice_in_dim(left, group * half, half, 1)
    c["own"] = lax.dynamic_slice_in_dim(left, (1 - group) * half, half, 1)
    b["own"] = query_right.reshape(local * ranks, -1)
    at_end = (z == 0) | (z == 3)

    def near(piece):
        return send(piece, NEAR)

    def middle(piece):
        return lines(piece, [(1, 2), (2, 1)])

    def outward(piece):
        return lines(piece, [(1, 0), (2, 3)])

    def across(piece):
        return send(piece, ACROSS)

    def over_x(piece):
        return send(piece, COLUMN)

    inside = (~at_end).reshape(1).astype(jnp.int32)
    mine = jnp.reshape(group, (1,)).astype(jnp.int32)
    zero = jnp.zeros((1,), jnp.int32)
    acts = ((hidden_acts, zero), (acts_there, zero))
    groups = (("own", "x", "n", "f"), ("xo", "o", "xn", "xf"))
    tokens_here = hidden_acts.shape[0]
    steps = 4

    def times_a(turn, k):
        return proj(turn, acts, tokens_here, [a[i] for i in groups[k]], mine, steps)

    def times_c(turn, k, *score):
        return proj(turn, acts, tokens_here, [c[i] for i in groups[k]], 1 - mine, steps, *score)

    def times_b(turn, k, *score):
        return proj(turn, grads, tokens_here, [b[i] for i in groups[k]], zero, steps, *score)

    def pause(turn):
        return after(turn, [], inside)[0]

    grads_there = send(output_grads, CORE)
    grads = ((output_grads, zero), (grads_there, zero))
    a["x"] = over_x(a["own"])
    a["n"] = near(a["own"])
    a_mid = middle(a["own"])
    turn = pause(zero)

    turn, (a["x"], a["n"], a_mid, b_own) = after(
        turn, [a["x"], a["n"], a_mid, b["own"]], inside, None, [acts_there]
    )
    a_out = outward(a_mid)
    a_in = middle(a["n"])
    b["x"] = over_x(b_own)
    c["x"] = swap_groups(a["x"])
    turn = pause(turn)

    turn, (a_out, a_in, b["x"], c["x"], b_own) = after(
        turn, [a_out, a_in, b["x"], c["x"], b_own], inside, None, [grads_there]
    )
    a_last = outward(a_in)
    a["xn"] = over_x(a["n"])
    c["n"] = swap_groups(a["n"])
    b["f"] = across(b_own)
    turn, (a["o"], a_in) = after(turn, [a_out, a_in], inside, (0, 1))
    a["xo"] = over_x(a["o"])
    turn = pause(turn)

    turn, (a_last, a["xn"], c["n"], b_own) = after(turn, [a_last, a["xn"], c["n"], b["own"]], inside)
    b["n"] = near(b_own)
    turn, (a["f"], a_mid) = after(turn, [a_last, a_mid], inside, (0, 1))
    a["xf"] = over_x(a["f"])
    c["f"] = swap_groups(a["f"])
    turn, a_first = times_a(turn, 0)

    turn, (a["xo"], c["f"], b["n"], a["o"], a["xn"]) = after(
        turn, [a["xo"], c["f"], b["n"], a["o"], a["xn"]], inside
    )
    b_in = middle(b["n"])
    c["o"] = swap_groups(a["o"])
    c["xn"] = swap_groups(a["xn"])
    turn, c_first = times_c(turn, 0)

    turn, (b["f"], a["xf"], c["o"], a["xo"]) = after(turn, [b["f"], a["xf"], c["o"], a["xo"]], inside)
    b_out = outward(b["f"])
    b["xf"] = over_x(b["f"])
    c["xo"] = swap_groups(a["xo"])
    turn, score_first = times_b(turn, 0, True, spans, (a_first, c_first))

    split = c["f"].shape[0] // 2
    turn, (b["o"], b["xf"], c["xn"], b_in, b_over, a["xf"], c["f"]) = after(
        turn, [b_out, b["xf"], c["xn"], b_in, b["x"], a["xf"], c["f"]], inside, (0, 3)
    )
    b["xo"] = over_x(b["o"])
    b["xn"] = near(b_over)
    c["top"] = over_x(c["f"][:split])
    c["low"] = swap_groups(a["xf"][split:])
    turn, a_second = times_a(turn, 1)

    turn, (b["xo"], b["xn"], c["xo"]) = after(turn, [b["xo"], b["xn"], c["xo"]], inside)
    turn, b_second = times_b(turn, 1)
    groups = (groups[0], ("xo", "o", "xn", "top", "low"))
    turn, score_second = times_c(turn, 1, False, spans, (a_second, b_second))
    sums = [score_first, score_second]

    slots = bucket_ids.shape[0]
    ours = jnp.concatenate([x[:slots] for x in sums], axis=1)
    others = send(jnp.concatenate([x[slots:] for x in sums], axis=1), CORE)
    codes = (0, COLUMN, NEAR, ACROSS, OPPOSITE | COLUMN, OPPOSITE, NEAR | COLUMN, ACROSS | COLUMN)
    codes = jnp.array(codes, jnp.int32)
    owner = jnp.concatenate([me ^ codes, me ^ CORE ^ codes])
    query = owner[:, None] * local + jnp.arange(local, dtype=jnp.int32)[None, :]
    query = jnp.repeat(query.reshape(-1), ranks)
    placed = query[None, :] == jnp.arange(count * local, dtype=jnp.int32)[:, None]
    return lax.dot_general(
        placed.astype(jnp.float32),
        jnp.concatenate([ours, others], axis=1),
        (((1,), (1,)), ((), ())),
        precision=lax.Precision.HIGHEST,
        preferred_element_type=jnp.float32,
    )


def solution(mesh):
    sizes = mesh.shape
    fits = sizes["dp"] == 16 and sizes["groups"] == 2 and sizes["tensor"] == 1
    return jax.shard_map(
        relay if fits else gather_whole,
        mesh=mesh,
        in_specs=(
            P(("groups", "dp"), "tensor"),
            P(("groups", "dp"), "tensor"),
            P("dp", None, "tensor"),
            P("dp", None, "tensor"),
            P(("groups", "dp")),
            P(("groups", "dp")),
        ),
        out_specs=P("tensor", ("groups", "dp")),
        check_vma=False,
    )
```

```python
import functools

import jax
import jax.numpy as jnp
from jax import lax
from jax.experimental import pallas as pl
from jax.experimental.pallas import tpu as pltpu
from jax.sharding import PartitionSpec as P

BUCKET = 128


def bucket_lengths(slot_ids):
    return BUCKET * jnp.where(
        slot_ids == 0, 1, jnp.where(slot_ids == 1, 2, jnp.where(slot_ids == 2, 4, 0))
    ).astype(jnp.int32)


def slot_matrix(slot_ids, lengths, positions):
    widths = bucket_lengths(slot_ids)
    starts = jnp.cumsum(widths) - widths
    place = jnp.arange(positions, dtype=jnp.int32)[:, None]
    inside = (place >= starts[None, :]) & (place < starts[None, :] + lengths[None, :])
    return inside.astype(jnp.float32)


def project(acts, factors):
    rows = factors.reshape(-1, factors.shape[2])
    return lax.dot_general(acts, rows, (((1,), (1,)), ((), ())), preferred_element_type=jnp.float32)


def gather_whole(hidden_acts, output_grads, query_left, query_right, bucket_ids, seq_lengths):
    tokens_here = hidden_acts.shape[0]
    rank_count = query_left.shape[1]
    left_all, right_all = (
        lax.all_gather(query_left, "dp", axis=0, tiled=True),
        lax.all_gather(query_right, "dp", axis=0, tiled=True),
    )
    left_proj = project(hidden_acts, left_all)
    right_proj = project(output_grads, right_all)
    queries = left_proj.shape[1] // rank_count
    left_terms = left_proj.reshape(tokens_here, queries, rank_count)
    right_terms = right_proj.reshape(tokens_here, queries, rank_count)
    left_terms, right_terms = lax.psum((left_terms, right_terms), "tensor")
    share_size = queries // lax.axis_size("tensor")
    first_query = lax.axis_index("tensor") * share_size
    left_terms = lax.dynamic_slice_in_dim(left_terms, first_query, share_size, 1)
    right_terms = lax.dynamic_slice_in_dim(right_terms, first_query, share_size, 1)
    token_term = jnp.sum(left_terms * right_terms, axis=2)
    slot_mask = slot_matrix(bucket_ids, seq_lengths, tokens_here)
    return jnp.dot(
        token_term.T, slot_mask, precision=lax.Precision.HIGHEST, preferred_element_type=jnp.float32
    )


CORE, COLUMN, NEAR, ACROSS, OPPOSITE = 1, 2, 4, 12, 8
LITTLE = pl.CostEstimate(flops=1, bytes_accessed=1, transcendentals=0)
VMEM_LIMIT = 63 * 1024 * 1024


def flip(array, code, count):
    return lax.ppermute(array, "dp", [(i, i ^ code) for i in range(count)])


def swap_groups(array):
    return lax.ppermute(array, "groups", [(0, 1), (1, 0)])


PARTS = 4


def through(held, arrived, gone, source, target):
    rows = source.shape[0] // PARTS
    parts = [pl.ds(i * rows, rows) for i in range(PARTS)]
    come = [pltpu.make_async_copy(source.at[p], held.at[p], arrived.at[i]) for i, p in enumerate(parts)]
    go = [pltpu.make_async_copy(held.at[p], target.at[p], gone.at[i]) for i, p in enumerate(parts)]
    for copy in come:
        copy.start()
    for first, second in zip(come, go):
        first.wait()
        second.start()
    for copy in go:
        copy.wait()


def after_kernel(count, merges, inside_ref, turn_ref, *refs):
    if merges:
        refs, staging = refs[:-3], refs[-3:]
        source, target = refs[0], refs[-1 - count]

        @pl.when(inside_ref[0] == 1)
        def _():
            through(*staging, source, target)

    refs[-1][0] = turn_ref[0]


def after(turn, arrays, inside, merge=None, there=()):
    count = len(arrays)
    scratch = []
    if merge is not None:
        there = (merge, *there)
        scratch = [pltpu.VMEM(merge.shape, merge.dtype)] + [pltpu.SemaphoreType.DMA((PARTS,))] * 2
    hbm = pl.BlockSpec(memory_space=pltpu.HBM)
    scalar = pl.BlockSpec(memory_space=pltpu.SMEM)
    *arrays, turn = pl.pallas_call(
        functools.partial(after_kernel, count, merge is not None),
        out_shape=[jax.ShapeDtypeStruct(x.shape, x.dtype) for x in (*arrays, turn)],
        in_specs=[scalar] * 2 + [hbm] * (len(there) + count),
        out_specs=[hbm] * count + [scalar],
        input_output_aliases={2 + len(there) + i: i for i in range(count)},
        scratch_shapes=scratch,
        compiler_params=pltpu.CompilerParams(vmem_limit_bytes=VMEM_LIMIT),
        cost_estimate=LITTLE,
    )(inside, turn, *there, *arrays)
    return turn, arrays


def prepare_kernel(works_ref, turn_ref, first_ref, left_ref, right_ref, *refs):
    half_ref, one_ref, two_ref, next_ref, half_held, right_held, arrived, gone = refs[-8:]
    next_ref[0] = turn_ref[0]
    width = half_ref.shape[1]

    @pl.when(works_ref[0] == 1)
    def _():
        start = pl.multiple_of(first_ref[0] * width, width)
        through(half_held, arrived, gone, left_ref.at[:, pl.ds(start, width)], half_ref)
        for target in (one_ref, two_ref):
            through(right_held, arrived, gone, right_ref, target)


def prepare(turn, works, first, left, right, made, passed):
    rows, width = left.shape[0], left.shape[1] // 2
    shapes = [(rows, width), right.shape, right.shape]
    out_shape = [jax.ShapeDtypeStruct(x, left.dtype) for x in shapes]
    made = () if made is None else made
    given = (*passed, *made)
    hbm = pl.BlockSpec(memory_space=pltpu.HBM)
    scalar = pl.BlockSpec(memory_space=pltpu.SMEM)
    aliases = {5 + i: i for i in range(len(given))}
    outs = pl.pallas_call(
        prepare_kernel,
        out_shape=[jax.ShapeDtypeStruct(x.shape, x.dtype) for x in passed]
        + out_shape
        + [jax.ShapeDtypeStruct(turn.shape, turn.dtype)],
        in_specs=[scalar] * 3 + [hbm] * (2 + len(given)),
        out_specs=[hbm] * (len(passed) + 3) + [scalar],
        input_output_aliases=aliases,
        scratch_shapes=[pltpu.VMEM((rows, width), left.dtype), pltpu.VMEM(right.shape, right.dtype)]
        + [pltpu.SemaphoreType.DMA((PARTS,))] * 2,
        compiler_params=pltpu.CompilerParams(vmem_limit_bytes=VMEM_LIMIT),
        cost_estimate=LITTLE,
    )(works, turn, first, left, right, *given)
    return outs[-1], outs[len(passed) : -1], outs[: len(passed)]


def lines(array, pairs):
    return lax.ppermute(
        array, "dp", [(a * 4 + rest, b * 4 + rest) for a, b in pairs for rest in range(4)]
    )


def score_into(out_ref, spans_ref, terms_of, rows):
    slots = out_ref.shape[0] // 2
    place = lax.broadcasted_iota(jnp.int32, (rows, 1), 0)
    for part in range(2):
        terms = terms_of(slice(part * rows, (part + 1) * rows))
        for j in range(slots):
            k = part * slots + j
            inside = (place >= spans_ref[0, k]) & (place < spans_ref[1, k])
            out_ref[k : k + 1, :] = jnp.sum(jnp.where(inside, terms, 0.0), axis=0, keepdims=True)


def proj_kernel(count, last, turn_ref, at_ref, own_ref, other_ref, *refs):
    del at_ref
    pieces, refs = refs[:count], refs[count:]
    if last is None:
        acc_ref, next_ref = refs
    else:
        spans_ref, left_ref, second_ref, out_ref, next_ref, acc_ref = refs
    step = pl.program_id(0)
    rows = own_ref.shape[0]

    @pl.when(step == 0)
    def _():
        next_ref[0] = turn_ref[0]
        acc_ref[...] = jnp.zeros_like(acc_ref)

    factors = jnp.concatenate([p[...] for p in pieces], axis=0)
    for part, tokens in enumerate((own_ref, other_ref)):
        acc_ref[part * rows : (part + 1) * rows] += lax.dot_general(
            tokens[...], factors, (((1,), (1,)), ((), ())), preferred_element_type=jnp.float32
        )

    if last is not None:

        @pl.when(step == pl.num_programs(0) - 1)
        def _():
            def terms(here):
                if last:
                    return (left_ref[here] + second_ref[here]) * acc_ref[here]
                return (left_ref[here] + acc_ref[here]) * second_ref[here]

            score_into(out_ref, spans_ref, terms, rows)


def proj(turn, tokens, rows, pieces, first, steps, last=None, spans=None, others=()):
    depth = pieces[0].shape[1]
    block = depth // steps
    held = sum(p.shape[0] for p in pieces)
    (own, own_row), (other, other_row) = tokens
    whole = pl.BlockSpec((2 * rows, held), lambda k, turn, at: (0, 0))
    scalar = pl.BlockSpec(memory_space=pltpu.SMEM)
    if last is None:
        more_specs, more, scratch = [], (), []
        out_shape, out_spec = (2 * rows, held), whole
    else:
        more_specs, more = [scalar, whole, whole], (spans, *others)
        scratch = [pltpu.VMEM((2 * rows, held), jnp.float32)]
        out_shape = (spans.shape[1], held)
        out_spec = pl.BlockSpec(out_shape, lambda k, turn, at: (0, 0))
    out, turn_next = pl.pallas_call(
        functools.partial(proj_kernel, len(pieces), last),
        out_shape=(
            jax.ShapeDtypeStruct(out_shape, jnp.float32),
            jax.ShapeDtypeStruct((1,), jnp.int32),
        ),
        grid_spec=pltpu.PrefetchScalarGridSpec(
            num_scalar_prefetch=2,
            grid=(steps,),
            in_specs=[
                pl.BlockSpec((rows, block), lambda k, turn, at: (at[1], at[0] * steps + k)),
                pl.BlockSpec((rows, block), lambda k, turn, at: (at[2], at[0] * steps + k)),
            ]
            + [pl.BlockSpec((p.shape[0], block), lambda k, turn, at: (0, k)) for p in pieces]
            + more_specs,
            out_specs=(out_spec, scalar),
            scratch_shapes=scratch,
        ),
        compiler_params=pltpu.CompilerParams(vmem_limit_bytes=VMEM_LIMIT),
        cost_estimate=LITTLE,
    )(turn, jnp.concatenate([first, own_row, other_row]), own, other, *pieces, *more)
    return turn_next, out


def spans_of(slot_ids, lengths):
    widths = bucket_lengths(slot_ids)
    starts = jnp.cumsum(widths) - widths
    return jnp.stack([starts, starts + lengths]).astype(jnp.int32)


def relay(hidden_acts, output_grads, query_left, query_right, bucket_ids, seq_lengths):
    count = lax.axis_size("dp")
    me, group = lax.axis_index("dp"), lax.axis_index("groups")
    z = me // 4
    local, ranks = query_left.shape[:2]
    left = query_left.reshape(local * ranks, -1)
    half = left.shape[1] // 2
    send = functools.partial(flip, count=count)

    acts_there = send(hidden_acts, CORE)
    spans_here = spans_of(bucket_ids, seq_lengths)
    spans = jnp.concatenate([spans_here, send(spans_here, CORE)], axis=1)

    a, b, c = {}, {}, {}
    a["own"] = lax.dynamic_slice_in_dim(left, group * half, half, 1)
    b["own"] = query_right.reshape(local * ranks, -1)
    at_end = (z == 0) | (z == 3)

    def near(piece):
        return send(piece, NEAR)

    def middle(piece):
        return lines(piece, [(1, 2), (2, 1)])

    def outward(piece):
        return lines(piece, [(1, 0), (2, 3)])

    def across(piece):
        return send(piece, ACROSS)

    def over_x(piece):
        return send(piece, COLUMN)

    inside = (~at_end).reshape(1).astype(jnp.int32)
    mine = jnp.reshape(group, (1,)).astype(jnp.int32)
    zero = jnp.zeros((1,), jnp.int32)
    acts = ((hidden_acts, zero), (acts_there, zero))
    groups = (("own", "x", "n", "f"), ("xo", "o", "xn", "xf"))
    tokens_here = hidden_acts.shape[0]
    steps = 4

    def times_a(turn, k):
        return proj(turn, acts, tokens_here, [a[i] for i in groups[k]], mine, steps)

    def times_c(turn, k, *score):
        return proj(turn, acts, tokens_here, [c[i] for i in groups[k]], 1 - mine, steps, *score)

    def times_b(turn, k, *score):
        return proj(turn, grads, tokens_here, [b[i] for i in groups[k]], zero, steps, *score)

    def pause(turn):
        return after(turn, [], inside)[0]

    grads_there = send(output_grads, CORE)
    grads = ((output_grads, zero), (grads_there, zero))

    core = (me & CORE).reshape(1).astype(jnp.int32)
    copies = (1 - mine, left, b["own"])
    turn, made, (a["own"],) = prepare(zero, core, *copies, None, [a["own"]])
    a_mid = middle(a["own"])
    a["n"] = near(a["own"])
    a["x"] = over_x(a["own"])
    turn, (c["own"], b_one, b_two), _ = prepare(turn, 1 - core, *copies, made, [])

    turn, (a_mid, a["n"], a["x"]) = after(turn, [a_mid, a["n"], a["x"]], inside, None, [acts_there])
    a_out = outward(a_mid)
    a_in = middle(a["n"])
    b["x"] = over_x(b_one)
    c["x"] = swap_groups(a["x"])
    turn = pause(turn)

    turn, (a_out, b["x"], a_in, c["x"]) = after(turn, [a_out, b["x"], a_in, c["x"]], inside, None, [grads_there])
    a_last = outward(a_in)
    a["xn"] = over_x(a["n"])
    c["n"] = swap_groups(a["n"])
    b["f"] = across(b_one)
    turn, (a["o"],) = after(turn, [a_out], inside, a_in)
    a["xo"] = over_x(a["o"])
    turn = pause(turn)

    turn, (a["f"], a["xn"], c["n"], b_two) = after(turn, [a_last, a["xn"], c["n"], b_two], inside, a_mid)
    b["n"] = near(b_two)
    a["xf"] = over_x(a["f"])
    c["f"] = swap_groups(a["f"])
    turn, a_first = times_a(turn, 0)

    turn, (b["n"], a["xo"], c["f"], a["o"], a["xn"]) = after(
        turn, [b["n"], a["xo"], c["f"], a["o"], a["xn"]], inside
    )
    b_in = middle(b["n"])
    c["o"] = swap_groups(a["o"])
    c["xn"] = swap_groups(a["xn"])
    turn, c_first = times_c(turn, 0)

    turn, (b["f"], a["xf"], c["o"], a["xo"]) = after(turn, [b["f"], a["xf"], c["o"], a["xo"]], inside)
    b_out = outward(b["f"])
    b["xf"] = over_x(b["f"])
    c["xo"] = swap_groups(a["xo"])
    turn, score_first = times_b(turn, 0, True, spans, (a_first, c_first))

    split = c["f"].shape[0] // 2
    turn, (b["o"], b["xf"], c["xn"], b_over, a["xf"], c["f"]) = after(
        turn, [b_out, b["xf"], c["xn"], b["x"], a["xf"], c["f"]], inside, b_in
    )
    b["xo"] = over_x(b["o"])
    b["xn"] = near(b_over)
    c["top"] = over_x(c["f"][:split])
    c["low"] = swap_groups(a["xf"][split:])
    turn, a_second = times_a(turn, 1)

    turn, (b["xo"], c["xo"], b["xn"]) = after(turn, [b["xo"], c["xo"], b["xn"]], inside)
    turn, b_second = times_b(turn, 1)
    groups = (groups[0], ("xo", "o", "xn", "top", "low"))
    turn, score_second = times_c(turn, 1, False, spans, (a_second, b_second))
    sums = [score_first, score_second]

    slots = bucket_ids.shape[0]
    ours = jnp.concatenate([x[:slots] for x in sums], axis=1)
    others = send(jnp.concatenate([x[slots:] for x in sums], axis=1), CORE)
    codes = (0, COLUMN, NEAR, ACROSS, OPPOSITE | COLUMN, OPPOSITE, NEAR | COLUMN, ACROSS | COLUMN)
    codes = jnp.array(codes, jnp.int32)
    owner = jnp.concatenate([me ^ codes, me ^ CORE ^ codes])
    query = owner[:, None] * local + jnp.arange(local, dtype=jnp.int32)[None, :]
    query = jnp.repeat(query.reshape(-1), ranks)
    placed = query[None, :] == jnp.arange(count * local, dtype=jnp.int32)[:, None]
    return lax.dot_general(
        placed.astype(jnp.float32),
        jnp.concatenate([ours, others], axis=1),
        (((1,), (1,)), ((), ())),
        precision=lax.Precision.HIGHEST,
        preferred_element_type=jnp.float32,
    )


def solution(mesh):
    sizes = mesh.shape
    fits = sizes["dp"] == 16 and sizes["groups"] == 2 and sizes["tensor"] == 1
    return jax.shard_map(
        relay if fits else gather_whole,
        mesh=mesh,
        in_specs=(
            P(("groups", "dp"), "tensor"),
            P(("groups", "dp"), "tensor"),
            P("dp", None, "tensor"),
            P("dp", None, "tensor"),
            P(("groups", "dp")),
            P(("groups", "dp")),
        ),
        out_specs=P("tensor", ("groups", "dp")),
        check_vma=False,
    )
```

```python
import functools

import jax
import jax.numpy as jnp
from jax import lax
from jax.experimental import pallas as pl
from jax.experimental.pallas import tpu as pltpu
from jax.sharding import PartitionSpec as P

BUCKET = 128


def bucket_lengths(slot_ids):
    return BUCKET * jnp.where(
        slot_ids == 0, 1, jnp.where(slot_ids == 1, 2, jnp.where(slot_ids == 2, 4, 0))
    ).astype(jnp.int32)


def slot_matrix(slot_ids, lengths, positions):
    widths = bucket_lengths(slot_ids)
    starts = jnp.cumsum(widths) - widths
    place = jnp.arange(positions, dtype=jnp.int32)[:, None]
    inside = (place >= starts[None, :]) & (place < starts[None, :] + lengths[None, :])
    return inside.astype(jnp.float32)


def project(acts, factors):
    rows = factors.reshape(-1, factors.shape[2])
    return lax.dot_general(acts, rows, (((1,), (1,)), ((), ())), preferred_element_type=jnp.float32)


def gather_whole(hidden_acts, output_grads, query_left, query_right, bucket_ids, seq_lengths):
    tokens_here = hidden_acts.shape[0]
    rank_count = query_left.shape[1]
    left_all, right_all = (
        lax.all_gather(query_left, "dp", axis=0, tiled=True),
        lax.all_gather(query_right, "dp", axis=0, tiled=True),
    )
    left_proj = project(hidden_acts, left_all)
    right_proj = project(output_grads, right_all)
    queries = left_proj.shape[1] // rank_count
    left_terms = left_proj.reshape(tokens_here, queries, rank_count)
    right_terms = right_proj.reshape(tokens_here, queries, rank_count)
    left_terms, right_terms = lax.psum((left_terms, right_terms), "tensor")
    share_size = queries // lax.axis_size("tensor")
    first_query = lax.axis_index("tensor") * share_size
    left_terms = lax.dynamic_slice_in_dim(left_terms, first_query, share_size, 1)
    right_terms = lax.dynamic_slice_in_dim(right_terms, first_query, share_size, 1)
    token_term = jnp.sum(left_terms * right_terms, axis=2)
    slot_mask = slot_matrix(bucket_ids, seq_lengths, tokens_here)
    return jnp.dot(
        token_term.T, slot_mask, precision=lax.Precision.HIGHEST, preferred_element_type=jnp.float32
    )


CORE, COLUMN, NEAR, ACROSS, OPPOSITE = 1, 2, 4, 12, 8
LITTLE = pl.CostEstimate(flops=1, bytes_accessed=1, transcendentals=0)
VMEM_LIMIT = 63 * 1024 * 1024


def flip(array, code, count):
    return lax.ppermute(array, "dp", [(i, i ^ code) for i in range(count)])


def swap_groups(array):
    return lax.ppermute(array, "groups", [(0, 1), (1, 0)])


PARTS = 4


def through(held, arrived, gone, source, target):
    rows = source.shape[0] // PARTS
    parts = [pl.ds(i * rows, rows) for i in range(PARTS)]
    come = [pltpu.make_async_copy(source.at[p], held.at[p], arrived.at[i]) for i, p in enumerate(parts)]
    go = [pltpu.make_async_copy(held.at[p], target.at[p], gone.at[i]) for i, p in enumerate(parts)]
    for copy in come:
        copy.start()
    for first, second in zip(come, go):
        first.wait()
        second.start()
    for copy in go:
        copy.wait()


def after_kernel(count, merges, turn_ref, *refs):
    if merges:
        refs, staging = refs[:-3], refs[-3:]
        inside_ref, source, target = refs[0], refs[1], refs[-1 - count]

        @pl.when(inside_ref[0] == 1)
        def _():
            through(*staging, source, target)

    refs[-1][0] = turn_ref[0]


def after(turn, arrays, there=(), merge=None):
    count = len(arrays)
    hbm = pl.BlockSpec(memory_space=pltpu.HBM)
    scalar = pl.BlockSpec(memory_space=pltpu.SMEM)
    first, specs, scratch = (), [], []
    if merge is not None:
        first, specs = merge, [scalar, hbm]
        scratch = [pltpu.VMEM(merge[1].shape, merge[1].dtype)] + [pltpu.SemaphoreType.DMA((PARTS,))] * 2
    ahead = 1 + len(first) + len(there)
    *arrays, turn = pl.pallas_call(
        functools.partial(after_kernel, count, merge is not None),
        out_shape=[jax.ShapeDtypeStruct(x.shape, x.dtype) for x in (*arrays, turn)],
        in_specs=[scalar] + specs + [hbm] * (len(there) + count),
        out_specs=[hbm] * count + [scalar],
        input_output_aliases={ahead + i: i for i in range(count)},
        scratch_shapes=scratch,
        compiler_params=pltpu.CompilerParams(vmem_limit_bytes=VMEM_LIMIT),
        cost_estimate=LITTLE,
    )(turn, *first, *there, *arrays)
    return turn, arrays


def prepare_kernel(works_ref, turn_ref, first_ref, left_ref, right_ref, *refs):
    half_ref, one_ref, two_ref, next_ref, half_held, right_held, arrived, gone = refs[-8:]
    next_ref[0] = turn_ref[0]
    width = half_ref.shape[1]

    @pl.when(works_ref[0] == 1)
    def _():
        start = pl.multiple_of(first_ref[0] * width, width)
        through(half_held, arrived, gone, left_ref.at[:, pl.ds(start, width)], half_ref)
        for target in (one_ref, two_ref):
            through(right_held, arrived, gone, right_ref, target)


def prepare(turn, works, first, left, right, made, passed):
    rows, width = left.shape[0], left.shape[1] // 2
    shapes = [(rows, width), right.shape, right.shape]
    out_shape = [jax.ShapeDtypeStruct(x, left.dtype) for x in shapes]
    made = () if made is None else made
    given = (*passed, *made)
    hbm = pl.BlockSpec(memory_space=pltpu.HBM)
    scalar = pl.BlockSpec(memory_space=pltpu.SMEM)
    aliases = {5 + i: i for i in range(len(given))}
    outs = pl.pallas_call(
        prepare_kernel,
        out_shape=[jax.ShapeDtypeStruct(x.shape, x.dtype) for x in passed]
        + out_shape
        + [jax.ShapeDtypeStruct(turn.shape, turn.dtype)],
        in_specs=[scalar] * 3 + [hbm] * (2 + len(given)),
        out_specs=[hbm] * (len(passed) + 3) + [scalar],
        input_output_aliases=aliases,
        scratch_shapes=[pltpu.VMEM((rows, width), left.dtype), pltpu.VMEM(right.shape, right.dtype)]
        + [pltpu.SemaphoreType.DMA((PARTS,))] * 2,
        compiler_params=pltpu.CompilerParams(vmem_limit_bytes=VMEM_LIMIT),
        cost_estimate=LITTLE,
    )(works, turn, first, left, right, *given)
    return outs[-1], outs[len(passed) : -1], outs[: len(passed)]


def score_into(out_ref, spans_ref, terms_of, rows):
    slots = out_ref.shape[0] // 2
    place = lax.broadcasted_iota(jnp.int32, (rows, 1), 0)
    for part in range(2):
        terms = terms_of(slice(part * rows, (part + 1) * rows))
        for j in range(slots):
            k = part * slots + j
            inside = (place >= spans_ref[0, k]) & (place < spans_ref[1, k])
            out_ref[k : k + 1, :] = jnp.sum(jnp.where(inside, terms, 0.0), axis=0, keepdims=True)


def proj_kernel(count, last, turn_ref, at_ref, own_ref, other_ref, *refs):
    del at_ref
    pieces, refs = refs[:count], refs[count:]
    if last is None:
        acc_ref, next_ref = refs
    else:
        spans_ref, left_ref, second_ref, out_ref, next_ref, acc_ref = refs
    step = pl.program_id(0)
    rows = own_ref.shape[0]

    @pl.when(step == 0)
    def _():
        next_ref[0] = turn_ref[0]
        acc_ref[...] = jnp.zeros_like(acc_ref)

    factors = jnp.concatenate([p[...] for p in pieces], axis=0)
    for part, tokens in enumerate((own_ref, other_ref)):
        acc_ref[part * rows : (part + 1) * rows] += lax.dot_general(
            tokens[...], factors, (((1,), (1,)), ((), ())), preferred_element_type=jnp.float32
        )

    if last is not None:

        @pl.when(step == pl.num_programs(0) - 1)
        def _():
            def terms(here):
                if last:
                    return (left_ref[here] + second_ref[here]) * acc_ref[here]
                return (left_ref[here] + acc_ref[here]) * second_ref[here]

            score_into(out_ref, spans_ref, terms, rows)


def proj(turn, tokens, rows, pieces, first, steps, last=None, spans=None, others=()):
    depth = pieces[0].shape[1]
    block = depth // steps
    held = sum(p.shape[0] for p in pieces)
    (own, own_row), (other, other_row) = tokens
    whole = pl.BlockSpec((2 * rows, held), lambda k, turn, at: (0, 0))
    scalar = pl.BlockSpec(memory_space=pltpu.SMEM)
    if last is None:
        more_specs, more, scratch = [], (), []
        out_shape, out_spec = (2 * rows, held), whole
    else:
        more_specs, more = [scalar, whole, whole], (spans, *others)
        scratch = [pltpu.VMEM((2 * rows, held), jnp.float32)]
        out_shape = (spans.shape[1], held)
        out_spec = pl.BlockSpec(out_shape, lambda k, turn, at: (0, 0))
    out, turn_next = pl.pallas_call(
        functools.partial(proj_kernel, len(pieces), last),
        out_shape=(
            jax.ShapeDtypeStruct(out_shape, jnp.float32),
            jax.ShapeDtypeStruct((1,), jnp.int32),
        ),
        grid_spec=pltpu.PrefetchScalarGridSpec(
            num_scalar_prefetch=2,
            grid=(steps,),
            in_specs=[
                pl.BlockSpec((rows, block), lambda k, turn, at: (at[1], at[0] * steps + k)),
                pl.BlockSpec((rows, block), lambda k, turn, at: (at[2], at[0] * steps + k)),
            ]
            + [pl.BlockSpec((p.shape[0], block), lambda k, turn, at: (0, k)) for p in pieces]
            + more_specs,
            out_specs=(out_spec, scalar),
            scratch_shapes=scratch,
        ),
        compiler_params=pltpu.CompilerParams(vmem_limit_bytes=VMEM_LIMIT),
        cost_estimate=LITTLE,
    )(turn, jnp.concatenate([first, own_row, other_row]), own, other, *pieces, *more)
    return turn_next, out


def spans_of(slot_ids, lengths):
    widths = bucket_lengths(slot_ids)
    starts = jnp.cumsum(widths) - widths
    return jnp.stack([starts, starts + lengths]).astype(jnp.int32)


def relay(hidden_acts, output_grads, query_left, query_right, bucket_ids, seq_lengths):
    count = lax.axis_size("dp")
    me, group = lax.axis_index("dp"), lax.axis_index("groups")
    local, ranks = query_left.shape[:2]
    left = query_left.reshape(local * ranks, -1)
    half = left.shape[1] // 2
    send = functools.partial(flip, count=count)

    acts_there = send(hidden_acts, CORE)
    spans_here = spans_of(bucket_ids, seq_lengths)
    spans = jnp.concatenate([spans_here, send(spans_here, CORE)], axis=1)

    a, b, c = {}, {}, {}
    a["own"] = lax.dynamic_slice_in_dim(left, group * half, half, 1)
    b["own"] = query_right.reshape(local * ranks, -1)

    def near(piece):
        return send(piece, NEAR)

    def lines(piece, pairs):
        pairs = [(i * 4 + rest, j * 4 + rest) for i, j in pairs for rest in range(4)]
        return lax.ppermute(piece, "dp", pairs)

    def across(piece):
        return send(piece, ACROSS)

    def over_x(piece):
        return send(piece, COLUMN)

    mine = jnp.reshape(group, (1,)).astype(jnp.int32)
    zero = jnp.zeros((1,), jnp.int32)
    acts = ((hidden_acts, zero), (acts_there, zero))
    groups = (("own", "x", "n", "f"), ("xn", "xf", "o", "xo"))
    tokens_here = hidden_acts.shape[0]
    steps = 4

    def times_a(turn, k):
        return proj(turn, acts, tokens_here, [a[i] for i in groups[k]], mine, steps)

    def times_c(turn, k, *score):
        return proj(turn, acts, tokens_here, [c[i] for i in groups[k]], 1 - mine, steps, *score)

    def times_b(turn, k, *score):
        return proj(turn, grads, tokens_here, [b[i] for i in groups[k]], zero, steps, *score)

    inside = ((me // 4) % 3 != 0).reshape(1).astype(jnp.int32)

    def pause(turn):
        return after(turn, [])[0]

    grads_there = send(output_grads, CORE)
    grads = ((output_grads, zero), (grads_there, zero))

    core = (me & CORE).reshape(1).astype(jnp.int32)
    copies = (1 - mine, left, b["own"])
    turn, made, (a["own"],) = prepare(zero, core, *copies, None, [a["own"]])
    a["x"] = over_x(a["own"])
    a["n"] = near(a["own"])
    a_mid = lines(a["own"], [(1, 2), (2, 1)])
    turn, (c["own"], b_one, b_two), _ = prepare(turn, 1 - core, *copies, made, [])

    turn, (a["x"], a["n"], a_mid, b_one, ends) = after(
        turn, [a["x"], a["n"], a_mid, b_one, a["own"]], [acts_there]
    )
    a_end = lines(ends, [(0, 3), (3, 0)])
    a["own"] = ends
    b["x"] = over_x(b_one)
    c["x"] = swap_groups(a["x"])
    turn = pause(turn)

    turn, (a["f"], b["x"], c["x"], b_one, a["n"]) = after(
        turn, [a_end, b["x"], c["x"], b_one, a["n"]], [grads_there], (inside, a_mid)
    )
    a["o"] = near(a["f"])
    a["xn"] = over_x(a["n"])
    c["n"] = swap_groups(a["n"])
    b["f"] = across(b_one)
    turn, a_first = times_a(turn, 0)

    turn, (a["o"], a["xn"], c["n"], b_two) = after(turn, [a["o"], a["xn"], c["n"], b_two])
    a["xf"] = over_x(a["f"])
    c["f"] = swap_groups(a["f"])
    b["n"] = near(b_two)
    turn = pause(turn)

    turn, (a["xf"], c["f"], b["n"], b["f"], a["o"]) = after(turn, [a["xf"], c["f"], b["n"], b["f"], a["o"]])
    a["xo"] = over_x(a["o"])
    c["o"] = swap_groups(a["o"])
    b["o"] = near(b["f"])
    turn, c_first = times_c(turn, 0)

    turn, (a["xo"], c["o"], b["o"], a["xn"], b["x"]) = after(
        turn, [a["xo"], c["o"], b["o"], a["xn"], b["x"]]
    )
    b["xf"] = over_x(b["f"])
    c["xn"] = swap_groups(a["xn"])
    b["xn"] = near(b["x"])
    turn, score_first = times_b(turn, 0, True, spans, (a_first, c_first))

    split = c["o"].shape[0] // 2
    turn, (b["xf"], c["xn"], b["xn"], a["xf"], a["xo"], c["o"]) = after(
        turn, [b["xf"], c["xn"], b["xn"], a["xf"], a["xo"], c["o"]]
    )
    b["xo"] = over_x(b["o"])
    c["xf"] = swap_groups(a["xf"])
    c["top"] = over_x(c["o"][:split])
    c["low"] = swap_groups(a["xo"][split:])
    turn, a_second = times_a(turn, 1)

    turn, (b["xo"], c["xf"]) = after(turn, [b["xo"], c["xf"]])
    turn, b_second = times_b(turn, 1)
    groups = (groups[0], ("xn", "xf", "o", "top", "low"))
    turn, score_second = times_c(turn, 1, False, spans, (a_second, b_second))
    sums = [score_first, score_second]

    slots = bucket_ids.shape[0]
    ours = jnp.concatenate([x[:slots] for x in sums], axis=1)
    others = send(jnp.concatenate([x[slots:] for x in sums], axis=1), CORE)
    codes = (0, COLUMN, NEAR, ACROSS, NEAR | COLUMN, ACROSS | COLUMN, OPPOSITE, OPPOSITE | COLUMN)
    codes = jnp.array(codes, jnp.int32)
    owner = jnp.concatenate([me ^ codes, me ^ CORE ^ codes])
    query = owner[:, None] * local + jnp.arange(local, dtype=jnp.int32)[None, :]
    query = jnp.repeat(query.reshape(-1), ranks)
    placed = query[None, :] == jnp.arange(count * local, dtype=jnp.int32)[:, None]
    return lax.dot_general(
        placed.astype(jnp.float32),
        jnp.concatenate([ours, others], axis=1),
        (((1,), (1,)), ((), ())),
        precision=lax.Precision.HIGHEST,
        preferred_element_type=jnp.float32,
    )


def solution(mesh):
    sizes = mesh.shape
    fits = sizes["dp"] == 16 and sizes["groups"] == 2 and sizes["tensor"] == 1
    return jax.shard_map(
        relay if fits else gather_whole,
        mesh=mesh,
        in_specs=(
            P(("groups", "dp"), "tensor"),
            P(("groups", "dp"), "tensor"),
            P("dp", None, "tensor"),
            P("dp", None, "tensor"),
            P(("groups", "dp")),
            P(("groups", "dp")),
        ),
        out_specs=P("tensor", ("groups", "dp")),
        check_vma=False,
    )
```

```python
import functools

import jax
import jax.numpy as jnp
from jax import lax
from jax.experimental import pallas as pl
from jax.experimental.pallas import tpu as pltpu
from jax.sharding import PartitionSpec as P

BUCKET = 128


def bucket_lengths(slot_ids):
    return BUCKET * jnp.where(
        slot_ids == 0, 1, jnp.where(slot_ids == 1, 2, jnp.where(slot_ids == 2, 4, 0))
    ).astype(jnp.int32)


def slot_matrix(slot_ids, lengths, positions):
    widths = bucket_lengths(slot_ids)
    starts = jnp.cumsum(widths) - widths
    place = jnp.arange(positions, dtype=jnp.int32)[:, None]
    inside = (place >= starts[None, :]) & (place < starts[None, :] + lengths[None, :])
    return inside.astype(jnp.float32)


def project(acts, factors):
    rows = factors.reshape(-1, factors.shape[2])
    return lax.dot_general(acts, rows, (((1,), (1,)), ((), ())), preferred_element_type=jnp.float32)


def gather_whole(hidden_acts, output_grads, query_left, query_right, bucket_ids, seq_lengths):
    tokens_here = hidden_acts.shape[0]
    rank_count = query_left.shape[1]
    left_all, right_all = (
        lax.all_gather(query_left, "dp", axis=0, tiled=True),
        lax.all_gather(query_right, "dp", axis=0, tiled=True),
    )
    left_proj = project(hidden_acts, left_all)
    right_proj = project(output_grads, right_all)
    queries = left_proj.shape[1] // rank_count
    left_terms = left_proj.reshape(tokens_here, queries, rank_count)
    right_terms = right_proj.reshape(tokens_here, queries, rank_count)
    left_terms, right_terms = lax.psum((left_terms, right_terms), "tensor")
    share_size = queries // lax.axis_size("tensor")
    first_query = lax.axis_index("tensor") * share_size
    left_terms = lax.dynamic_slice_in_dim(left_terms, first_query, share_size, 1)
    right_terms = lax.dynamic_slice_in_dim(right_terms, first_query, share_size, 1)
    token_term = jnp.sum(left_terms * right_terms, axis=2)
    slot_mask = slot_matrix(bucket_ids, seq_lengths, tokens_here)
    return jnp.dot(
        token_term.T, slot_mask, precision=lax.Precision.HIGHEST, preferred_element_type=jnp.float32
    )


CORE, COLUMN, NEAR, ACROSS, OPPOSITE = 1, 2, 4, 12, 8
LITTLE = pl.CostEstimate(flops=1, bytes_accessed=1, transcendentals=0)
VMEM_LIMIT = 63 * 1024 * 1024


def flip(array, code, count):
    return lax.ppermute(array, "dp", [(i, i ^ code) for i in range(count)])


def swap_groups(array):
    return lax.ppermute(array, "groups", [(0, 1), (1, 0)])


PARTS = 4


def through(held, arrived, gone, source, target):
    rows = source.shape[0] // PARTS
    parts = [pl.ds(i * rows, rows) for i in range(PARTS)]
    come = [pltpu.make_async_copy(source.at[p], held.at[p], arrived.at[i]) for i, p in enumerate(parts)]
    go = [pltpu.make_async_copy(held.at[p], target.at[p], gone.at[i]) for i, p in enumerate(parts)]
    for copy in come:
        copy.start()
    for first, second in zip(come, go):
        first.wait()
        second.start()
    for copy in go:
        copy.wait()


def after_kernel(count, merges, turn_ref, *refs):
    if merges:
        refs, staging = refs[:-3], refs[-3:]
        inside_ref, source, target = refs[0], refs[1], refs[-1 - count]

        @pl.when(inside_ref[0] == 1)
        def _():
            through(*staging, source, target)

    refs[-1][0] = turn_ref[0]


def after(turn, arrays, there=(), merge=None):
    count = len(arrays)
    hbm = pl.BlockSpec(memory_space=pltpu.HBM)
    scalar = pl.BlockSpec(memory_space=pltpu.SMEM)
    first, specs, scratch = (), [], []
    if merge is not None:
        first, specs = merge, [scalar, hbm]
        scratch = [pltpu.VMEM(merge[1].shape, merge[1].dtype)] + [pltpu.SemaphoreType.DMA((PARTS,))] * 2
    ahead = 1 + len(first) + len(there)
    *arrays, turn = pl.pallas_call(
        functools.partial(after_kernel, count, merge is not None),
        out_shape=[jax.ShapeDtypeStruct(x.shape, x.dtype) for x in (*arrays, turn)],
        in_specs=[scalar] + specs + [hbm] * (len(there) + count),
        out_specs=[hbm] * count + [scalar],
        input_output_aliases={ahead + i: i for i in range(count)},
        scratch_shapes=scratch,
        compiler_params=pltpu.CompilerParams(vmem_limit_bytes=VMEM_LIMIT),
        cost_estimate=LITTLE,
    )(turn, *first, *there, *arrays)
    return turn, arrays


def prepare_kernel(works_ref, turn_ref, first_ref, left_ref, right_ref, *refs):
    half_ref, one_ref, two_ref, next_ref, half_held, right_held, arrived, gone = refs[-8:]
    next_ref[0] = turn_ref[0]
    width = half_ref.shape[1]

    @pl.when(works_ref[0] == 1)
    def _():
        start = pl.multiple_of(first_ref[0] * width, width)
        through(half_held, arrived, gone, left_ref.at[:, pl.ds(start, width)], half_ref)
        for target in (one_ref, two_ref):
            through(right_held, arrived, gone, right_ref, target)


def prepare(turn, works, first, left, right, made, passed):
    rows, width = left.shape[0], left.shape[1] // 2
    shapes = [(rows, width), right.shape, right.shape]
    out_shape = [jax.ShapeDtypeStruct(x, left.dtype) for x in shapes]
    made = () if made is None else made
    given = (*passed, *made)
    hbm = pl.BlockSpec(memory_space=pltpu.HBM)
    scalar = pl.BlockSpec(memory_space=pltpu.SMEM)
    aliases = {5 + i: i for i in range(len(given))}
    outs = pl.pallas_call(
        prepare_kernel,
        out_shape=[jax.ShapeDtypeStruct(x.shape, x.dtype) for x in passed]
        + out_shape
        + [jax.ShapeDtypeStruct(turn.shape, turn.dtype)],
        in_specs=[scalar] * 3 + [hbm] * (2 + len(given)),
        out_specs=[hbm] * (len(passed) + 3) + [scalar],
        input_output_aliases=aliases,
        scratch_shapes=[pltpu.VMEM((rows, width), left.dtype), pltpu.VMEM(right.shape, right.dtype)]
        + [pltpu.SemaphoreType.DMA((PARTS,))] * 2,
        compiler_params=pltpu.CompilerParams(vmem_limit_bytes=VMEM_LIMIT),
        cost_estimate=LITTLE,
    )(works, turn, first, left, right, *given)
    return outs[-1], outs[len(passed) : -1], outs[: len(passed)]


def score_into(out_ref, spans_ref, terms_of, rows):
    slots = out_ref.shape[0] // 2
    place = lax.broadcasted_iota(jnp.int32, (rows, 1), 0)
    for part in range(2):
        terms = terms_of(slice(part * rows, (part + 1) * rows))
        for j in range(slots):
            k = part * slots + j
            inside = (place >= spans_ref[0, k]) & (place < spans_ref[1, k])
            out_ref[k : k + 1, :] = jnp.sum(jnp.where(inside, terms, 0.0), axis=0, keepdims=True)


def proj_kernel(count, last, turn_ref, at_ref, own_ref, other_ref, *refs):
    del at_ref
    pieces, refs = refs[:count], refs[count:]
    if last is None:
        acc_ref, next_ref = refs
    else:
        spans_ref, left_ref, second_ref, out_ref, next_ref, acc_ref = refs
    step = pl.program_id(0)
    rows = own_ref.shape[0]

    @pl.when(step == 0)
    def _():
        next_ref[0] = turn_ref[0]
        acc_ref[...] = jnp.zeros_like(acc_ref)

    factors = jnp.concatenate([p[...] for p in pieces], axis=0)
    for part, tokens in enumerate((own_ref, other_ref)):
        acc_ref[part * rows : (part + 1) * rows] += lax.dot_general(
            tokens[...], factors, (((1,), (1,)), ((), ())), preferred_element_type=jnp.float32
        )

    if last is not None:

        @pl.when(step == pl.num_programs(0) - 1)
        def _():
            def terms(here):
                if last:
                    return (left_ref[here] + second_ref[here]) * acc_ref[here]
                return (left_ref[here] + acc_ref[here]) * second_ref[here]

            score_into(out_ref, spans_ref, terms, rows)


def proj(turn, tokens, rows, pieces, first, steps, last=None, spans=None, others=()):
    depth = pieces[0].shape[1]
    block = depth // steps
    held = sum(p.shape[0] for p in pieces)
    (own, own_row), (other, other_row) = tokens
    whole = pl.BlockSpec((2 * rows, held), lambda k, turn, at: (0, 0))
    scalar = pl.BlockSpec(memory_space=pltpu.SMEM)
    if last is None:
        more_specs, more, scratch = [], (), []
        out_shape, out_spec = (2 * rows, held), whole
    else:
        more_specs, more = [scalar, whole, whole], (spans, *others)
        scratch = [pltpu.VMEM((2 * rows, held), jnp.float32)]
        out_shape = (spans.shape[1], held)
        out_spec = pl.BlockSpec(out_shape, lambda k, turn, at: (0, 0))
    out, turn_next = pl.pallas_call(
        functools.partial(proj_kernel, len(pieces), last),
        out_shape=(
            jax.ShapeDtypeStruct(out_shape, jnp.float32),
            jax.ShapeDtypeStruct((1,), jnp.int32),
        ),
        grid_spec=pltpu.PrefetchScalarGridSpec(
            num_scalar_prefetch=2,
            grid=(steps,),
            in_specs=[
                pl.BlockSpec((rows, block), lambda k, turn, at: (at[1], at[0] * steps + k)),
                pl.BlockSpec((rows, block), lambda k, turn, at: (at[2], at[0] * steps + k)),
            ]
            + [pl.BlockSpec((p.shape[0], block), lambda k, turn, at: (0, k)) for p in pieces]
            + more_specs,
            out_specs=(out_spec, scalar),
            scratch_shapes=scratch,
        ),
        compiler_params=pltpu.CompilerParams(vmem_limit_bytes=VMEM_LIMIT),
        cost_estimate=LITTLE,
    )(turn, jnp.concatenate([first, own_row, other_row]), own, other, *pieces, *more)
    return turn_next, out


def spans_of(slot_ids, lengths):
    widths = bucket_lengths(slot_ids)
    starts = jnp.cumsum(widths) - widths
    return jnp.stack([starts, starts + lengths]).astype(jnp.int32)


def relay(hidden_acts, output_grads, query_left, query_right, bucket_ids, seq_lengths):
    count = lax.axis_size("dp")
    me, group = lax.axis_index("dp"), lax.axis_index("groups")
    local, ranks = query_left.shape[:2]
    left = query_left.reshape(local * ranks, -1)
    half = left.shape[1] // 2
    send = functools.partial(flip, count=count)

    acts_there = send(hidden_acts, CORE)
    spans_here = spans_of(bucket_ids, seq_lengths)
    spans = jnp.concatenate([spans_here, send(spans_here, CORE)], axis=1)

    a, b, c = {}, {}, {}
    a["own"] = lax.dynamic_slice_in_dim(left, group * half, half, 1)
    b["own"] = query_right.reshape(local * ranks, -1)

    def near(piece):
        return send(piece, NEAR)

    def lines(piece, pairs):
        pairs = [(i * 4 + rest, j * 4 + rest) for i, j in pairs for rest in range(4)]
        return lax.ppermute(piece, "dp", pairs)

    def middle(piece):
        return lines(piece, [(1, 2), (2, 1)])

    def ends(piece):
        return lines(piece, [(0, 3), (3, 0)])

    def over_x(piece):
        return send(piece, COLUMN)

    mine = jnp.reshape(group, (1,)).astype(jnp.int32)
    zero = jnp.zeros((1,), jnp.int32)
    acts = ((hidden_acts, zero), (acts_there, zero))
    groups = (("own", "x", "n", "f"), ("xn", "xf", "o", "xo"))
    tokens_here = hidden_acts.shape[0]
    steps = 4

    def times_a(turn, k):
        return proj(turn, acts, tokens_here, [a[i] for i in groups[k]], mine, steps)

    def times_c(turn, k, *score):
        return proj(turn, acts, tokens_here, [c[i] for i in groups[k]], 1 - mine, steps, *score)

    def times_b(turn, k, *score):
        return proj(turn, grads, tokens_here, [b[i] for i in groups[k]], zero, steps, *score)

    inside = ((me // 4) % 3 != 0).reshape(1).astype(jnp.int32)

    def pause(turn):
        return after(turn, [])[0]

    grads_there = send(output_grads, CORE)
    grads = ((output_grads, zero), (grads_there, zero))

    core = (me & CORE).reshape(1).astype(jnp.int32)
    copies = (1 - mine, left, b["own"])
    turn, made, (a["own"],) = prepare(zero, core, *copies, None, [a["own"]])
    a["x"] = over_x(a["own"])
    a["n"] = near(a["own"])
    a_mid = middle(a["own"])
    turn, (c["own"], b_one, b_two), _ = prepare(turn, 1 - core, *copies, made, [])

    turn, (a["x"], a["n"], a_mid, b_one, a["own"]) = after(
        turn, [a["x"], a["n"], a_mid, b_one, a["own"]], [acts_there]
    )
    a_end = ends(a["own"])
    b["x"] = over_x(b_one)
    c["x"] = swap_groups(a["x"])
    turn = pause(turn)

    turn, (a["f"], b["x"], c["x"], b_one, a["n"]) = after(
        turn, [a_end, b["x"], c["x"], b_one, a["n"]], [grads_there], (inside, a_mid)
    )
    a["o"] = near(a["f"])
    a["xn"] = over_x(a["n"])
    c["n"] = swap_groups(a["n"])
    b_mid = middle(b_one)
    turn, a_first = times_a(turn, 0)

    turn, (a["o"], a["xn"], c["n"], b_mid, b_two) = after(turn, [a["o"], a["xn"], c["n"], b_mid, b_two])
    a["xf"] = over_x(a["f"])
    c["f"] = swap_groups(a["f"])
    b_end = ends(b_two)
    turn = pause(turn)

    turn, (b["f"], a["xf"], c["f"], a["o"], b_two) = after(
        turn, [b_end, a["xf"], c["f"], a["o"], b_two], (), (inside, b_mid)
    )
    a["xo"] = over_x(a["o"])
    c["o"] = swap_groups(a["o"])
    b["o"] = near(b["f"])
    turn, c_first = times_c(turn, 0)

    turn, (a["xo"], c["o"], b["o"], a["xn"], b_two) = after(
        turn, [a["xo"], c["o"], b["o"], a["xn"], b_two]
    )
    b["xf"] = over_x(b["f"])
    c["xn"] = swap_groups(a["xn"])
    b["n"] = near(b_two)
    turn, a_second = times_a(turn, 1)

    split = c["o"].shape[0] // 2
    turn, (b["xf"], c["xn"], b["n"], a["xf"], a["xo"], c["o"], b["x"]) = after(
        turn, [b["xf"], c["xn"], b["n"], a["xf"], a["xo"], c["o"], b["x"]]
    )
    b["xo"] = over_x(b["o"])
    c["xf"] = swap_groups(a["xf"])
    b["xn"] = near(b["x"])
    c["top"] = over_x(c["o"][:split])
    c["low"] = swap_groups(a["xo"][split:])
    turn, score_first = times_b(turn, 0, True, spans, (a_first, c_first))

    turn, (b["xo"], c["xf"], b["xn"]) = after(turn, [b["xo"], c["xf"], b["xn"]])
    turn, b_second = times_b(turn, 1)
    groups = (groups[0], ("xn", "xf", "o", "top", "low"))
    turn, score_second = times_c(turn, 1, False, spans, (a_second, b_second))
    sums = [score_first, score_second]

    slots = bucket_ids.shape[0]
    ours = jnp.concatenate([x[:slots] for x in sums], axis=1)
    others = send(jnp.concatenate([x[slots:] for x in sums], axis=1), CORE)
    codes = (0, COLUMN, NEAR, ACROSS, NEAR | COLUMN, ACROSS | COLUMN, OPPOSITE, OPPOSITE | COLUMN)
    codes = jnp.array(codes, jnp.int32)
    owner = jnp.concatenate([me ^ codes, me ^ CORE ^ codes])
    query = owner[:, None] * local + jnp.arange(local, dtype=jnp.int32)[None, :]
    query = jnp.repeat(query.reshape(-1), ranks)
    placed = query[None, :] == jnp.arange(count * local, dtype=jnp.int32)[:, None]
    return lax.dot_general(
        placed.astype(jnp.float32),
        jnp.concatenate([ours, others], axis=1),
        (((1,), (1,)), ((), ())),
        precision=lax.Precision.HIGHEST,
        preferred_element_type=jnp.float32,
    )


def solution(mesh):
    sizes = mesh.shape
    fits = sizes["dp"] == 16 and sizes["groups"] == 2 and sizes["tensor"] == 1
    return jax.shard_map(
        relay if fits else gather_whole,
        mesh=mesh,
        in_specs=(
            P(("groups", "dp"), "tensor"),
            P(("groups", "dp"), "tensor"),
            P("dp", None, "tensor"),
            P("dp", None, "tensor"),
            P(("groups", "dp")),
            P(("groups", "dp")),
        ),
        out_specs=P("tensor", ("groups", "dp")),
        check_vma=False,
    )
```

```python
import functools

import jax
import jax.numpy as jnp
from jax import lax
from jax.experimental import pallas as pl
from jax.experimental.pallas import tpu as pltpu
from jax.sharding import PartitionSpec as P

BUCKET = 128


def bucket_lengths(slot_ids):
    return BUCKET * jnp.where(
        slot_ids == 0, 1, jnp.where(slot_ids == 1, 2, jnp.where(slot_ids == 2, 4, 0))
    ).astype(jnp.int32)


def slot_matrix(slot_ids, lengths, positions):
    widths = bucket_lengths(slot_ids)
    starts = jnp.cumsum(widths) - widths
    place = jnp.arange(positions, dtype=jnp.int32)[:, None]
    inside = (place >= starts[None, :]) & (place < starts[None, :] + lengths[None, :])
    return inside.astype(jnp.float32)


def project(acts, factors):
    rows = factors.reshape(-1, factors.shape[2])
    return lax.dot_general(acts, rows, (((1,), (1,)), ((), ())), preferred_element_type=jnp.float32)


def gather_whole(hidden_acts, output_grads, query_left, query_right, bucket_ids, seq_lengths):
    tokens_here = hidden_acts.shape[0]
    rank_count = query_left.shape[1]
    left_all, right_all = (
        lax.all_gather(query_left, "dp", axis=0, tiled=True),
        lax.all_gather(query_right, "dp", axis=0, tiled=True),
    )
    left_proj = project(hidden_acts, left_all)
    right_proj = project(output_grads, right_all)
    queries = left_proj.shape[1] // rank_count
    left_terms = left_proj.reshape(tokens_here, queries, rank_count)
    right_terms = right_proj.reshape(tokens_here, queries, rank_count)
    left_terms, right_terms = lax.psum((left_terms, right_terms), "tensor")
    share_size = queries // lax.axis_size("tensor")
    first_query = lax.axis_index("tensor") * share_size
    left_terms = lax.dynamic_slice_in_dim(left_terms, first_query, share_size, 1)
    right_terms = lax.dynamic_slice_in_dim(right_terms, first_query, share_size, 1)
    token_term = jnp.sum(left_terms * right_terms, axis=2)
    slot_mask = slot_matrix(bucket_ids, seq_lengths, tokens_here)
    return jnp.dot(
        token_term.T, slot_mask, precision=lax.Precision.HIGHEST, preferred_element_type=jnp.float32
    )


CORE, COLUMN, NEAR, ACROSS, OPPOSITE = 1, 2, 4, 12, 8
LITTLE = pl.CostEstimate(flops=1, bytes_accessed=1, transcendentals=0)
VMEM_LIMIT = 127 * 512 * 1024


def flip(array, code, count):
    return lax.ppermute(array, "dp", [(i, i ^ code) for i in range(count)])


def swap_groups(array):
    return lax.ppermute(array, "groups", [(0, 1), (1, 0)])


PARTS = 4


def through(held, arrived, gone, source, target):
    rows = source.shape[0] // PARTS
    parts = [pl.ds(i * rows, rows) for i in range(PARTS)]
    come = [pltpu.make_async_copy(source.at[p], held.at[p], arrived.at[i]) for i, p in enumerate(parts)]
    go = [pltpu.make_async_copy(held.at[p], target.at[p], gone.at[i]) for i, p in enumerate(parts)]
    for copy in come:
        copy.start()
    for first, second in zip(come, go):
        first.wait()
        second.start()
    for copy in go:
        copy.wait()


def after_kernel(count, merges, turn_ref, *refs):
    if merges:
        refs, staging = refs[:-3], refs[-3:]
        inside_ref, source, target = refs[0], refs[1], refs[-1 - count]

        @pl.when(inside_ref[0] == 1)
        def _():
            through(*staging, source, target)

    refs[-1][0] = turn_ref[0]


def after(turn, arrays, there=(), merge=None):
    count = len(arrays)
    hbm = pl.BlockSpec(memory_space=pltpu.HBM)
    scalar = pl.BlockSpec(memory_space=pltpu.SMEM)
    first, specs, scratch = (), [], []
    if merge is not None:
        first, specs = merge, [scalar, hbm]
        scratch = [pltpu.VMEM(merge[1].shape, merge[1].dtype)] + [pltpu.SemaphoreType.DMA((PARTS,))] * 2
    ahead = 1 + len(first) + len(there)
    *arrays, turn = pl.pallas_call(
        functools.partial(after_kernel, count, merge is not None),
        out_shape=[jax.ShapeDtypeStruct(x.shape, x.dtype) for x in (*arrays, turn)],
        in_specs=[scalar] + specs + [hbm] * (len(there) + count),
        out_specs=[hbm] * count + [scalar],
        input_output_aliases={ahead + i: i for i in range(count)},
        scratch_shapes=scratch,
        compiler_params=pltpu.CompilerParams(vmem_limit_bytes=VMEM_LIMIT),
        cost_estimate=LITTLE,
    )(turn, *first, *there, *arrays)
    return turn, arrays


def prepare_kernel(works_ref, turn_ref, first_ref, left_ref, right_ref, *refs):
    half_ref, one_ref, two_ref, next_ref, half_held, right_held, arrived, gone = refs[-8:]
    next_ref[0] = turn_ref[0]
    width = half_ref.shape[1]

    @pl.when(works_ref[0] == 1)
    def _():
        start = pl.multiple_of(first_ref[0] * width, width)
        through(half_held, arrived, gone, left_ref.at[:, pl.ds(start, width)], half_ref)
        for target in (one_ref, two_ref):
            through(right_held, arrived, gone, right_ref, target)


def prepare(turn, works, first, left, right, made, passed):
    rows, width = left.shape[0], left.shape[1] // 2
    shapes = [(rows, width), right.shape, right.shape]
    out_shape = [jax.ShapeDtypeStruct(x, left.dtype) for x in shapes]
    made = () if made is None else made
    given = (*passed, *made)
    hbm = pl.BlockSpec(memory_space=pltpu.HBM)
    scalar = pl.BlockSpec(memory_space=pltpu.SMEM)
    aliases = {5 + i: i for i in range(len(given))}
    outs = pl.pallas_call(
        prepare_kernel,
        out_shape=[jax.ShapeDtypeStruct(x.shape, x.dtype) for x in passed]
        + out_shape
        + [jax.ShapeDtypeStruct(turn.shape, turn.dtype)],
        in_specs=[scalar] * 3 + [hbm] * (2 + len(given)),
        out_specs=[hbm] * (len(passed) + 3) + [scalar],
        input_output_aliases=aliases,
        scratch_shapes=[pltpu.VMEM((rows, width), left.dtype), pltpu.VMEM(right.shape, right.dtype)]
        + [pltpu.SemaphoreType.DMA((PARTS,))] * 2,
        compiler_params=pltpu.CompilerParams(vmem_limit_bytes=VMEM_LIMIT),
        cost_estimate=LITTLE,
    )(works, turn, first, left, right, *given)
    return outs[-1], outs[len(passed) : -1], outs[: len(passed)]


def score_into(out_ref, spans_ref, terms_of, rows):
    slots = out_ref.shape[0] // 2
    place = lax.broadcasted_iota(jnp.int32, (rows, 1), 0)
    for part in range(2):
        terms = terms_of(slice(part * rows, (part + 1) * rows))
        for j in range(slots):
            k = part * slots + j
            inside = (place >= spans_ref[0, k]) & (place < spans_ref[1, k])
            out_ref[k : k + 1, :] = jnp.sum(jnp.where(inside, terms, 0.0), axis=0, keepdims=True)


def proj_kernel(count, last, turn_ref, at_ref, own_ref, other_ref, *refs):
    del at_ref
    pieces, refs = refs[:count], refs[count:]
    if last is None:
        acc_ref, next_ref = refs
    else:
        spans_ref, left_ref, second_ref, out_ref, next_ref, acc_ref = refs
    step = pl.program_id(0)
    rows = own_ref.shape[0]

    @pl.when(step == 0)
    def _():
        next_ref[0] = turn_ref[0]
        acc_ref[...] = jnp.zeros_like(acc_ref)

    factors = jnp.concatenate([p[...] for p in pieces], axis=0)
    for part, tokens in enumerate((own_ref, other_ref)):
        acc_ref[part * rows : (part + 1) * rows] += lax.dot_general(
            tokens[...], factors, (((1,), (1,)), ((), ())), preferred_element_type=jnp.float32
        )

    if last is not None:

        @pl.when(step == pl.num_programs(0) - 1)
        def _():
            def terms(here):
                if last:
                    return (left_ref[here] + second_ref[here]) * acc_ref[here]
                return (left_ref[here] + acc_ref[here]) * second_ref[here]

            score_into(out_ref, spans_ref, terms, rows)


def proj(turn, tokens, rows, pieces, first, steps, last=None, spans=None, others=()):
    depth = pieces[0].shape[1]
    block = depth // steps
    held = sum(p.shape[0] for p in pieces)
    (own, own_row), (other, other_row) = tokens
    whole = pl.BlockSpec((2 * rows, held), lambda k, turn, at: (0, 0))
    scalar = pl.BlockSpec(memory_space=pltpu.SMEM)
    if last is None:
        more_specs, more, scratch = [], (), []
        out_shape, out_spec = (2 * rows, held), whole
    else:
        more_specs, more = [scalar, whole, whole], (spans, *others)
        scratch = [pltpu.VMEM((2 * rows, held), jnp.float32)]
        out_shape = (spans.shape[1], held)
        out_spec = pl.BlockSpec(out_shape, lambda k, turn, at: (0, 0))
    out, turn_next = pl.pallas_call(
        functools.partial(proj_kernel, len(pieces), last),
        out_shape=(
            jax.ShapeDtypeStruct(out_shape, jnp.float32),
            jax.ShapeDtypeStruct((1,), jnp.int32),
        ),
        grid_spec=pltpu.PrefetchScalarGridSpec(
            num_scalar_prefetch=2,
            grid=(steps,),
            in_specs=[
                pl.BlockSpec((rows, block), lambda k, turn, at: (at[1], at[0] * steps + k)),
                pl.BlockSpec((rows, block), lambda k, turn, at: (at[2], at[0] * steps + k)),
            ]
            + [pl.BlockSpec((p.shape[0], block), lambda k, turn, at: (0, k)) for p in pieces]
            + more_specs,
            out_specs=(out_spec, scalar),
            scratch_shapes=scratch,
        ),
        compiler_params=pltpu.CompilerParams(vmem_limit_bytes=VMEM_LIMIT),
        cost_estimate=LITTLE,
    )(turn, jnp.concatenate([first, own_row, other_row]), own, other, *pieces, *more)
    return turn_next, out


def spans_of(slot_ids, lengths):
    widths = bucket_lengths(slot_ids)
    starts = jnp.cumsum(widths) - widths
    return jnp.stack([starts, starts + lengths]).astype(jnp.int32)


def relay(hidden_acts, output_grads, query_left, query_right, bucket_ids, seq_lengths):
    count = lax.axis_size("dp")
    me, group = lax.axis_index("dp"), lax.axis_index("groups")
    local, ranks = query_left.shape[:2]
    left = query_left.reshape(local * ranks, -1)
    half = left.shape[1] // 2
    send = functools.partial(flip, count=count)

    acts_there = send(hidden_acts, CORE)
    spans_here = spans_of(bucket_ids, seq_lengths)
    spans = jnp.concatenate([spans_here, send(spans_here, CORE)], axis=1)

    a, b, c = {}, {}, {}
    a["own"] = lax.dynamic_slice_in_dim(left, group * half, half, 1)
    b["own"] = query_right.reshape(local * ranks, -1)

    def near(piece):
        return send(piece, NEAR)

    def lines(piece, pairs):
        pairs = [(i * 4 + rest, j * 4 + rest) for i, j in pairs for rest in range(4)]
        return lax.ppermute(piece, "dp", pairs)

    def middle(piece):
        return lines(piece, [(1, 2), (2, 1)])

    def ends(piece):
        return lines(piece, [(0, 3), (3, 0)])

    def over_x(piece):
        return send(piece, COLUMN)

    mine = jnp.reshape(group, (1,)).astype(jnp.int32)
    zero = jnp.zeros((1,), jnp.int32)
    acts = ((hidden_acts, zero), (acts_there, zero))
    groups = (("own", "x", "n", "f"), ("xn", "xf", "o", "xo"))
    tokens_here = hidden_acts.shape[0]
    steps = 4

    def times_a(turn, k):
        return proj(turn, acts, tokens_here, [a[i] for i in groups[k]], mine, steps)

    def times_c(turn, k, *score):
        return proj(turn, acts, tokens_here, [c[i] for i in groups[k]], 1 - mine, steps, *score)

    def times_b(turn, k, *score):
        return proj(turn, grads, tokens_here, [b[i] for i in groups[k]], zero, steps, *score)

    inside = ((me // 4) % 3 != 0).reshape(1).astype(jnp.int32)

    def pause(turn):
        return after(turn, [])[0]

    grads_there = send(output_grads, CORE)
    grads = ((output_grads, zero), (grads_there, zero))

    core = (me & CORE).reshape(1).astype(jnp.int32)
    copies = (1 - mine, left, b["own"])
    turn, made, (a["own"],) = prepare(zero, core, *copies, None, [a["own"]])
    a["x"] = over_x(a["own"])
    a["n"] = near(a["own"])
    a_mid = middle(a["own"])
    turn, (c["own"], b_one, b_two), _ = prepare(turn, 1 - core, *copies, made, [])

    turn, (a["x"], a["n"], a_mid, b_one, a["own"]) = after(
        turn, [a["x"], a["n"], a_mid, b_one, a["own"]], [acts_there]
    )
    a_end = ends(a["own"])
    b["x"] = over_x(b_one)
    c["x"] = swap_groups(a["x"])
    turn = pause(turn)

    turn, (a["f"], b["x"], c["x"], b_one) = after(
        turn, [a_end, b["x"], c["x"], b_one], [grads_there], (inside, a_mid)
    )
    a["o"] = near(a["f"])
    a["xn"] = over_x(a["n"])
    c["n"] = swap_groups(a["n"])
    b_mid = middle(b_one)
    turn = pause(turn)

    turn, (c["n"], a["o"], a["xn"], b_mid, b_two) = after(turn, [c["n"], a["o"], a["xn"], b_mid, b_two])
    a["xf"] = over_x(a["f"])
    c["f"] = swap_groups(a["f"])
    b_end = ends(b_two)
    turn, a_first = times_a(turn, 0)

    turn, (b["f"], a["xf"], c["f"], a["o"], b_two) = after(
        turn, [b_end, a["xf"], c["f"], a["o"], b_two], (), (inside, b_mid)
    )
    a["xo"] = over_x(a["o"])
    c["o"] = swap_groups(a["o"])
    b["o"] = near(b["f"])
    turn, c_first = times_c(turn, 0)

    turn, (a["xo"], c["o"], b["o"], a["xn"], b_two) = after(
        turn, [a["xo"], c["o"], b["o"], a["xn"], b_two]
    )
    b["xf"] = over_x(b["f"])
    c["xn"] = swap_groups(a["xn"])
    b["n"] = near(b_two)
    turn, a_second = times_a(turn, 1)

    split = c["o"].shape[0] // 2
    turn, (b["xf"], c["xn"], b["n"], a["xf"], a["xo"], c["o"], b["x"]) = after(
        turn, [b["xf"], c["xn"], b["n"], a["xf"], a["xo"], c["o"], b["x"]]
    )
    b["xo"] = over_x(b["o"])
    c["xf"] = swap_groups(a["xf"])
    b["xn"] = near(b["x"])
    c["top"] = over_x(c["o"][:split])
    c["low"] = swap_groups(a["xo"][split:])
    turn, score_first = times_b(turn, 0, True, spans, (a_first, c_first))

    turn, (b["xo"], c["xf"], b["xn"]) = after(turn, [b["xo"], c["xf"], b["xn"]])
    turn, b_second = times_b(turn, 1)
    groups = (groups[0], ("xn", "xf", "o", "top", "low"))
    turn, score_second = times_c(turn, 1, False, spans, (a_second, b_second))
    sums = [score_first, score_second]

    slots = bucket_ids.shape[0]
    ours = jnp.concatenate([x[:slots] for x in sums], axis=1)
    others = send(jnp.concatenate([x[slots:] for x in sums], axis=1), CORE)
    codes = (0, COLUMN, NEAR, ACROSS, NEAR | COLUMN, ACROSS | COLUMN, OPPOSITE, OPPOSITE | COLUMN)
    codes = jnp.array(codes, jnp.int32)
    owner = jnp.concatenate([me ^ codes, me ^ CORE ^ codes])
    query = owner[:, None] * local + jnp.arange(local, dtype=jnp.int32)[None, :]
    query = jnp.repeat(query.reshape(-1), ranks)
    placed = query[None, :] == jnp.arange(count * local, dtype=jnp.int32)[:, None]
    return lax.dot_general(
        placed.astype(jnp.float32),
        jnp.concatenate([ours, others], axis=1),
        (((1,), (1,)), ((), ())),
        precision=lax.Precision.HIGHEST,
        preferred_element_type=jnp.float32,
    )


def solution(mesh):
    sizes = mesh.shape
    fits = sizes["dp"] == 16 and sizes["groups"] == 2 and sizes["tensor"] == 1
    return jax.shard_map(
        relay if fits else gather_whole,
        mesh=mesh,
        in_specs=(
            P(("groups", "dp"), "tensor"),
            P(("groups", "dp"), "tensor"),
            P("dp", None, "tensor"),
            P("dp", None, "tensor"),
            P(("groups", "dp")),
            P(("groups", "dp")),
        ),
        out_specs=P("tensor", ("groups", "dp")),
        check_vma=False,
    )
```

```python
import functools

import jax
import jax.numpy as jnp
from jax import lax
from jax.experimental import pallas as pl
from jax.experimental.pallas import tpu as pltpu
from jax.sharding import PartitionSpec as P

BUCKET = 128


def bucket_lengths(slot_ids):
    return BUCKET * jnp.where(
        slot_ids == 0, 1, jnp.where(slot_ids == 1, 2, jnp.where(slot_ids == 2, 4, 0))
    ).astype(jnp.int32)


def slot_matrix(slot_ids, lengths, positions):
    widths = bucket_lengths(slot_ids)
    starts = jnp.cumsum(widths) - widths
    place = jnp.arange(positions, dtype=jnp.int32)[:, None]
    inside = (place >= starts[None, :]) & (place < starts[None, :] + lengths[None, :])
    return inside.astype(jnp.float32)


def project(acts, factors):
    rows = factors.reshape(-1, factors.shape[2])
    return lax.dot_general(acts, rows, (((1,), (1,)), ((), ())), preferred_element_type=jnp.float32)


def gather_whole(hidden_acts, output_grads, query_left, query_right, bucket_ids, seq_lengths):
    tokens_here = hidden_acts.shape[0]
    rank_count = query_left.shape[1]
    left_all, right_all = (
        lax.all_gather(query_left, "dp", axis=0, tiled=True),
        lax.all_gather(query_right, "dp", axis=0, tiled=True),
    )
    left_proj = project(hidden_acts, left_all)
    right_proj = project(output_grads, right_all)
    queries = left_proj.shape[1] // rank_count
    left_terms = left_proj.reshape(tokens_here, queries, rank_count)
    right_terms = right_proj.reshape(tokens_here, queries, rank_count)
    left_terms, right_terms = lax.psum((left_terms, right_terms), "tensor")
    share_size = queries // lax.axis_size("tensor")
    first_query = lax.axis_index("tensor") * share_size
    left_terms = lax.dynamic_slice_in_dim(left_terms, first_query, share_size, 1)
    right_terms = lax.dynamic_slice_in_dim(right_terms, first_query, share_size, 1)
    token_term = jnp.sum(left_terms * right_terms, axis=2)
    slot_mask = slot_matrix(bucket_ids, seq_lengths, tokens_here)
    return jnp.dot(
        token_term.T, slot_mask, precision=lax.Precision.HIGHEST, preferred_element_type=jnp.float32
    )


CORE, COLUMN, NEAR, ACROSS, OPPOSITE = 1, 2, 4, 12, 8
LITTLE = pl.CostEstimate(flops=1, bytes_accessed=1, transcendentals=0)
VMEM_LIMIT = 127 * 512 * 1024


def flip(array, code, count):
    return lax.ppermute(array, "dp", [(i, i ^ code) for i in range(count)])


def swap_groups(array):
    return lax.ppermute(array, "groups", [(0, 1), (1, 0)])


PARTS = 4


def through(held, arrived, gone, source, target):
    rows = source.shape[0] // PARTS
    parts = [pl.ds(i * rows, rows) for i in range(PARTS)]
    come = [pltpu.make_async_copy(source.at[p], held.at[p], arrived.at[i]) for i, p in enumerate(parts)]
    go = [pltpu.make_async_copy(held.at[p], target.at[p], gone.at[i]) for i, p in enumerate(parts)]
    for copy in come:
        copy.start()
    for first, second in zip(come, go):
        first.wait()
        second.start()
    for copy in go:
        copy.wait()


def after_kernel(count, merges, turn_ref, *refs):
    if merges:
        refs, staging = refs[:-3], refs[-3:]
        inside_ref, source, target = refs[0], refs[1], refs[-1 - count]

        @pl.when(inside_ref[0] == 1)
        def _():
            through(*staging, source, target)

    refs[-1][0] = turn_ref[0]


def after(turn, arrays, there=(), merge=None):
    count = len(arrays)
    hbm = pl.BlockSpec(memory_space=pltpu.HBM)
    scalar = pl.BlockSpec(memory_space=pltpu.SMEM)
    first, specs, scratch = (), [], []
    if merge is not None:
        first, specs = merge, [scalar, hbm]
        scratch = [pltpu.VMEM(merge[1].shape, merge[1].dtype)] + [pltpu.SemaphoreType.DMA((PARTS,))] * 2
    ahead = 1 + len(first) + len(there)
    *arrays, turn = pl.pallas_call(
        functools.partial(after_kernel, count, merge is not None),
        out_shape=[jax.ShapeDtypeStruct(x.shape, x.dtype) for x in (*arrays, turn)],
        in_specs=[scalar] + specs + [hbm] * (len(there) + count),
        out_specs=[hbm] * count + [scalar],
        input_output_aliases={ahead + i: i for i in range(count)},
        scratch_shapes=scratch,
        compiler_params=pltpu.CompilerParams(vmem_limit_bytes=VMEM_LIMIT),
        cost_estimate=LITTLE,
    )(turn, *first, *there, *arrays)
    return turn, arrays


def prepare_kernel(works_ref, turn_ref, first_ref, left_ref, right_ref, *refs):
    half_ref, one_ref, two_ref, next_ref, half_held, right_held, arrived, gone = refs[-8:]
    next_ref[0] = turn_ref[0]
    width = half_ref.shape[1]

    @pl.when(works_ref[0] == 1)
    def _():
        start = pl.multiple_of(first_ref[0] * width, width)
        through(half_held, arrived, gone, left_ref.at[:, pl.ds(start, width)], half_ref)
        for target in (one_ref, two_ref):
            through(right_held, arrived, gone, right_ref, target)


def prepare(turn, works, first, left, right, made, passed):
    rows, width = left.shape[0], left.shape[1] // 2
    shapes = [(rows, width), right.shape, right.shape]
    out_shape = [jax.ShapeDtypeStruct(x, left.dtype) for x in shapes]
    made = () if made is None else made
    given = (*passed, *made)
    hbm = pl.BlockSpec(memory_space=pltpu.HBM)
    scalar = pl.BlockSpec(memory_space=pltpu.SMEM)
    aliases = {5 + i: i for i in range(len(given))}
    outs = pl.pallas_call(
        prepare_kernel,
        out_shape=[jax.ShapeDtypeStruct(x.shape, x.dtype) for x in passed]
        + out_shape
        + [jax.ShapeDtypeStruct(turn.shape, turn.dtype)],
        in_specs=[scalar] * 3 + [hbm] * (2 + len(given)),
        out_specs=[hbm] * (len(passed) + 3) + [scalar],
        input_output_aliases=aliases,
        scratch_shapes=[pltpu.VMEM((rows, width), left.dtype), pltpu.VMEM(right.shape, right.dtype)]
        + [pltpu.SemaphoreType.DMA((PARTS,))] * 2,
        compiler_params=pltpu.CompilerParams(vmem_limit_bytes=VMEM_LIMIT),
        cost_estimate=LITTLE,
    )(works, turn, first, left, right, *given)
    return outs[-1], outs[len(passed) : -1], outs[: len(passed)]


def score_into(out_ref, spans_ref, terms_of, rows):
    slots = out_ref.shape[0] // 2
    place = lax.broadcasted_iota(jnp.int32, (rows, 1), 0)
    for part in range(2):
        terms = terms_of(slice(part * rows, (part + 1) * rows))
        for j in range(slots):
            k = part * slots + j
            inside = (place >= spans_ref[0, k]) & (place < spans_ref[1, k])
            out_ref[k : k + 1, :] = jnp.sum(jnp.where(inside, terms, 0.0), axis=0, keepdims=True)


def proj_kernel(count, last, turn_ref, at_ref, own_ref, other_ref, *refs):
    del at_ref
    pieces, refs = refs[:count], refs[count:]
    if last is None:
        acc_ref, next_ref = refs
    else:
        spans_ref, left_ref, second_ref, out_ref, next_ref, acc_ref = refs
    step = pl.program_id(0)
    rows = own_ref.shape[0]

    @pl.when(step == 0)
    def _():
        next_ref[0] = turn_ref[0]
        acc_ref[...] = jnp.zeros_like(acc_ref)

    factors = jnp.concatenate([p[...] for p in pieces], axis=0)
    for part, tokens in enumerate((own_ref, other_ref)):
        acc_ref[part * rows : (part + 1) * rows] += lax.dot_general(
            tokens[...], factors, (((1,), (1,)), ((), ())), preferred_element_type=jnp.float32
        )

    if last is not None:

        @pl.when(step == pl.num_programs(0) - 1)
        def _():
            def terms(here):
                if last:
                    return (left_ref[here] + second_ref[here]) * acc_ref[here]
                return (left_ref[here] + acc_ref[here]) * second_ref[here]

            score_into(out_ref, spans_ref, terms, rows)


def proj(turn, tokens, rows, pieces, first, steps, last=None, spans=None, others=(), column=0):
    depth = pieces[0].shape[1]
    block = depth // steps
    held = sum(p.shape[0] for p in pieces)
    (own, own_row), (other, other_row) = tokens
    whole = pl.BlockSpec((2 * rows, held), lambda k, turn, at: (0, 0))
    scalar = pl.BlockSpec(memory_space=pltpu.SMEM)
    if last is None:
        more_specs, more, scratch = [], (), []
        out_shape, out_spec = (2 * rows, held), whole
    else:
        part = pl.BlockSpec((2 * rows, held), lambda k, turn, at: (0, column))
        more_specs, more = [scalar, part, whole], (spans, *others)
        scratch = [pltpu.VMEM((2 * rows, held), jnp.float32)]
        out_shape = (spans.shape[1], held)
        out_spec = pl.BlockSpec(out_shape, lambda k, turn, at: (0, 0))
    out, turn_next = pl.pallas_call(
        functools.partial(proj_kernel, len(pieces), last),
        out_shape=(
            jax.ShapeDtypeStruct(out_shape, jnp.float32),
            jax.ShapeDtypeStruct((1,), jnp.int32),
        ),
        grid_spec=pltpu.PrefetchScalarGridSpec(
            num_scalar_prefetch=2,
            grid=(steps,),
            in_specs=[
                pl.BlockSpec((rows, block), lambda k, turn, at: (at[1], at[0] * steps + k)),
                pl.BlockSpec((rows, block), lambda k, turn, at: (at[2], at[0] * steps + k)),
            ]
            + [pl.BlockSpec((p.shape[0], block), lambda k, turn, at: (0, k)) for p in pieces]
            + more_specs,
            out_specs=(out_spec, scalar),
            scratch_shapes=scratch,
        ),
        compiler_params=pltpu.CompilerParams(vmem_limit_bytes=VMEM_LIMIT),
        cost_estimate=LITTLE,
    )(turn, jnp.concatenate([first, own_row, other_row]), own, other, *pieces, *more)
    return turn_next, out


def spans_of(slot_ids, lengths):
    widths = bucket_lengths(slot_ids)
    starts = jnp.cumsum(widths) - widths
    return jnp.stack([starts, starts + lengths]).astype(jnp.int32)


def relay(hidden_acts, output_grads, query_left, query_right, bucket_ids, seq_lengths):
    count = lax.axis_size("dp")
    me, group = lax.axis_index("dp"), lax.axis_index("groups")
    local, ranks = query_left.shape[:2]
    left = query_left.reshape(local * ranks, -1)
    half = left.shape[1] // 2
    send = functools.partial(flip, count=count)

    acts_there = send(hidden_acts, CORE)
    spans_here = spans_of(bucket_ids, seq_lengths)
    spans = jnp.concatenate([spans_here, send(spans_here, CORE)], axis=1)

    a, b, c = {}, {}, {}
    a["own"] = lax.dynamic_slice_in_dim(left, group * half, half, 1)
    b["own"] = query_right.reshape(local * ranks, -1)

    def near(piece):
        return send(piece, NEAR)

    def lines(piece, pairs):
        pairs = [(i * 4 + rest, j * 4 + rest) for i, j in pairs for rest in range(4)]
        return lax.ppermute(piece, "dp", pairs)

    def middle(piece):
        return lines(piece, [(1, 2), (2, 1)])

    def ends(piece):
        return lines(piece, [(0, 3), (3, 0)])

    def over_x(piece):
        return send(piece, COLUMN)

    mine = jnp.reshape(group, (1,)).astype(jnp.int32)
    zero = jnp.zeros((1,), jnp.int32)
    acts = ((hidden_acts, zero), (acts_there, zero))
    groups = (("own", "x", "n", "f"), ("xn", "xf", "o", "xo"))
    tokens_here = hidden_acts.shape[0]
    steps = 4

    def times_c(turn, k, *score):
        return proj(turn, acts, tokens_here, [c[i] for i in groups[k]], 1 - mine, steps, *score)

    def times_b(turn, k, *score):
        return proj(turn, grads, tokens_here, [b[i] for i in groups[k]], zero, steps, *score)

    inside = ((me // 4) % 3 != 0).reshape(1).astype(jnp.int32)

    def pause(turn):
        return after(turn, [])[0]

    grads_there = send(output_grads, CORE)
    grads = ((output_grads, zero), (grads_there, zero))

    core = (me & CORE).reshape(1).astype(jnp.int32)
    copies = (1 - mine, left, b["own"])
    turn, made, (a["own"],) = prepare(zero, core, *copies, None, [a["own"]])
    a["x"] = over_x(a["own"])
    a["n"] = near(a["own"])
    a_mid = middle(a["own"])
    turn, (c["own"], b_one, b_two), _ = prepare(turn, 1 - core, *copies, made, [])

    turn, (a["x"], a["n"], a_mid, b_one, a["own"]) = after(
        turn, [a["x"], a["n"], a_mid, b_one, a["own"]], [acts_there]
    )
    a_end = ends(a["own"])
    b["x"] = over_x(b_one)
    c["x"] = swap_groups(a["x"])
    turn = pause(turn)

    turn, (a["f"], b["x"], c["x"], b_one) = after(
        turn, [a_end, b["x"], c["x"], b_one], [grads_there], (inside, a_mid)
    )
    a["o"] = near(a["f"])
    a["xn"] = over_x(a["n"])
    c["n"] = swap_groups(a["n"])
    b_mid = middle(b_one)
    turn = pause(turn)

    turn, (a["xn"], c["n"], a["o"], b_mid, b_two) = after(turn, [a["xn"], c["n"], a["o"], b_mid, b_two])
    a["xf"] = over_x(a["f"])
    c["f"] = swap_groups(a["f"])
    b_end = ends(b_two)
    turn = pause(turn)

    turn, (b["f"], a["xf"], c["f"], a["o"], b_two) = after(
        turn, [b_end, a["xf"], c["f"], a["o"], b_two], (), (inside, b_mid)
    )
    a["xo"] = over_x(a["o"])
    c["o"] = swap_groups(a["o"])
    b["o"] = near(b["f"])
    turn, c_first = times_c(turn, 0)

    turn, (a["xo"], c["o"], b["o"], a["xn"], b_two) = after(
        turn, [a["xo"], c["o"], b["o"], a["xn"], b_two]
    )
    b["xf"] = over_x(b["f"])
    c["xn"] = swap_groups(a["xn"])
    b["n"] = near(b_two)
    turn, a_all = proj(turn, acts, tokens_here, [a[i] for i in groups[0] + groups[1]], mine, steps)

    split = c["o"].shape[0] // 2
    turn, (b["xf"], c["xn"], b["n"], a["xo"], c["o"], b["x"]) = after(
        turn, [b["xf"], c["xn"], b["n"], a["xo"], c["o"], b["x"]]
    )
    b["xo"] = over_x(b["o"])
    c["xf"] = swap_groups(a["xf"])
    b["xn"] = near(b["x"])
    c["top"] = over_x(c["o"][:split])
    c["low"] = swap_groups(a["xo"][split:])
    turn, score_first = times_b(turn, 0, True, spans, (a_all, c_first), 0)

    turn, (b["xo"], c["xf"], b["xn"]) = after(turn, [b["xo"], c["xf"], b["xn"]])
    turn, b_second = times_b(turn, 1)
    groups = (groups[0], ("xn", "xf", "o", "top", "low"))
    turn, score_second = times_c(turn, 1, False, spans, (a_all, b_second), 1)
    sums = [score_first, score_second]

    slots = bucket_ids.shape[0]
    ours = jnp.concatenate([x[:slots] for x in sums], axis=1)
    others = send(jnp.concatenate([x[slots:] for x in sums], axis=1), CORE)
    codes = (0, COLUMN, NEAR, ACROSS, NEAR | COLUMN, ACROSS | COLUMN, OPPOSITE, OPPOSITE | COLUMN)
    codes = jnp.array(codes, jnp.int32)
    owner = jnp.concatenate([me ^ codes, me ^ CORE ^ codes])
    query = owner[:, None] * local + jnp.arange(local, dtype=jnp.int32)[None, :]
    query = jnp.repeat(query.reshape(-1), ranks)
    placed = query[None, :] == jnp.arange(count * local, dtype=jnp.int32)[:, None]
    return lax.dot_general(
        placed.astype(jnp.float32),
        jnp.concatenate([ours, others], axis=1),
        (((1,), (1,)), ((), ())),
        precision=lax.Precision.HIGHEST,
        preferred_element_type=jnp.float32,
    )


def solution(mesh):
    sizes = mesh.shape
    fits = sizes["dp"] == 16 and sizes["groups"] == 2 and sizes["tensor"] == 1
    return jax.shard_map(
        relay if fits else gather_whole,
        mesh=mesh,
        in_specs=(
            P(("groups", "dp"), "tensor"),
            P(("groups", "dp"), "tensor"),
            P("dp", None, "tensor"),
            P("dp", None, "tensor"),
            P(("groups", "dp")),
            P(("groups", "dp")),
        ),
        out_specs=P("tensor", ("groups", "dp")),
        check_vma=False,
    )
```

```python
import functools

import jax
import jax.numpy as jnp
from jax import lax
from jax.experimental import pallas as pl
from jax.experimental.pallas import tpu as pltpu
from jax.sharding import PartitionSpec as P

BUCKET = 128


def bucket_lengths(slot_ids):
    return BUCKET * jnp.where(
        slot_ids == 0, 1, jnp.where(slot_ids == 1, 2, jnp.where(slot_ids == 2, 4, 0))
    ).astype(jnp.int32)


def slot_matrix(slot_ids, lengths, positions):
    widths = bucket_lengths(slot_ids)
    starts = jnp.cumsum(widths) - widths
    place = jnp.arange(positions, dtype=jnp.int32)[:, None]
    inside = (place >= starts[None, :]) & (place < starts[None, :] + lengths[None, :])
    return inside.astype(jnp.float32)


def project(acts, factors):
    rows = factors.reshape(-1, factors.shape[2])
    return lax.dot_general(acts, rows, (((1,), (1,)), ((), ())), preferred_element_type=jnp.float32)


def gather_whole(hidden_acts, output_grads, query_left, query_right, bucket_ids, seq_lengths):
    tokens_here = hidden_acts.shape[0]
    rank_count = query_left.shape[1]
    left_all, right_all = (
        lax.all_gather(query_left, "dp", axis=0, tiled=True),
        lax.all_gather(query_right, "dp", axis=0, tiled=True),
    )
    left_proj = project(hidden_acts, left_all)
    right_proj = project(output_grads, right_all)
    queries = left_proj.shape[1] // rank_count
    left_terms = left_proj.reshape(tokens_here, queries, rank_count)
    right_terms = right_proj.reshape(tokens_here, queries, rank_count)
    left_terms, right_terms = lax.psum((left_terms, right_terms), "tensor")
    share_size = queries // lax.axis_size("tensor")
    first_query = lax.axis_index("tensor") * share_size
    left_terms = lax.dynamic_slice_in_dim(left_terms, first_query, share_size, 1)
    right_terms = lax.dynamic_slice_in_dim(right_terms, first_query, share_size, 1)
    token_term = jnp.sum(left_terms * right_terms, axis=2)
    slot_mask = slot_matrix(bucket_ids, seq_lengths, tokens_here)
    return jnp.dot(
        token_term.T, slot_mask, precision=lax.Precision.HIGHEST, preferred_element_type=jnp.float32
    )


CORE, COLUMN, NEAR, ACROSS, OPPOSITE = 1, 2, 4, 12, 8
LITTLE = pl.CostEstimate(flops=1, bytes_accessed=1, transcendentals=0)
VMEM_LIMIT = 127 * 512 * 1024


def flip(array, code, count):
    return lax.ppermute(array, "dp", [(i, i ^ code) for i in range(count)])


def swap_groups(array):
    return lax.ppermute(array, "groups", [(0, 1), (1, 0)])


PARTS = 4


def through(held, arrived, gone, source, target):
    rows = source.shape[0] // PARTS
    parts = [pl.ds(i * rows, rows) for i in range(PARTS)]
    come = [pltpu.make_async_copy(source.at[p], held.at[p], arrived.at[i]) for i, p in enumerate(parts)]
    go = [pltpu.make_async_copy(held.at[p], target.at[p], gone.at[i]) for i, p in enumerate(parts)]
    for copy in come:
        copy.start()
    for first, second in zip(come, go):
        first.wait()
        second.start()
    for copy in go:
        copy.wait()


def after_kernel(count, merges, inside_ref, turn_ref, *refs):
    if merges:
        refs, staging = refs[:-3], refs[-3:]
        source, target = refs[0], refs[-1 - count]

        @pl.when(inside_ref[0] == 1)
        def _():
            through(*staging, source, target)

    refs[-1][0] = turn_ref[0]


def after(turn, arrays, inside, merge=None, there=()):
    count = len(arrays)
    scratch = []
    if merge is not None:
        there = (merge, *there)
        scratch = [pltpu.VMEM(merge.shape, merge.dtype)] + [pltpu.SemaphoreType.DMA((PARTS,))] * 2
    hbm = pl.BlockSpec(memory_space=pltpu.HBM)
    scalar = pl.BlockSpec(memory_space=pltpu.SMEM)
    *arrays, turn = pl.pallas_call(
        functools.partial(after_kernel, count, merge is not None),
        out_shape=[jax.ShapeDtypeStruct(x.shape, x.dtype) for x in (*arrays, turn)],
        in_specs=[scalar] * 2 + [hbm] * (len(there) + count),
        out_specs=[hbm] * count + [scalar],
        input_output_aliases={2 + len(there) + i: i for i in range(count)},
        scratch_shapes=scratch,
        compiler_params=pltpu.CompilerParams(vmem_limit_bytes=VMEM_LIMIT),
        cost_estimate=LITTLE,
    )(inside, turn, *there, *arrays)
    return turn, arrays


def prepare_kernel(works_ref, turn_ref, first_ref, left_ref, right_ref, *refs):
    half_ref, one_ref, two_ref, next_ref, half_held, right_held, arrived, gone = refs[-8:]
    next_ref[0] = turn_ref[0]
    width = half_ref.shape[1]

    @pl.when(works_ref[0] == 1)
    def _():
        start = pl.multiple_of(first_ref[0] * width, width)
        through(half_held, arrived, gone, left_ref.at[:, pl.ds(start, width)], half_ref)
        for target in (one_ref, two_ref):
            through(right_held, arrived, gone, right_ref, target)


def prepare(turn, works, first, left, right, made, passed):
    rows, width = left.shape[0], left.shape[1] // 2
    shapes = [(rows, width), right.shape, right.shape]
    out_shape = [jax.ShapeDtypeStruct(x, left.dtype) for x in shapes]
    made = () if made is None else made
    given = (*passed, *made)
    hbm = pl.BlockSpec(memory_space=pltpu.HBM)
    scalar = pl.BlockSpec(memory_space=pltpu.SMEM)
    aliases = {5 + i: i for i in range(len(given))}
    outs = pl.pallas_call(
        prepare_kernel,
        out_shape=[jax.ShapeDtypeStruct(x.shape, x.dtype) for x in passed]
        + out_shape
        + [jax.ShapeDtypeStruct(turn.shape, turn.dtype)],
        in_specs=[scalar] * 3 + [hbm] * (2 + len(given)),
        out_specs=[hbm] * (len(passed) + 3) + [scalar],
        input_output_aliases=aliases,
        scratch_shapes=[pltpu.VMEM((rows, width), left.dtype), pltpu.VMEM(right.shape, right.dtype)]
        + [pltpu.SemaphoreType.DMA((PARTS,))] * 2,
        compiler_params=pltpu.CompilerParams(vmem_limit_bytes=VMEM_LIMIT),
        cost_estimate=LITTLE,
    )(works, turn, first, left, right, *given)
    return outs[-1], outs[len(passed) : -1], outs[: len(passed)]


def lines(array, pairs):
    return lax.ppermute(
        array, "dp", [(a * 4 + rest, b * 4 + rest) for a, b in pairs for rest in range(4)]
    )


def score_into(out_ref, spans_ref, terms_of, rows):
    slots = out_ref.shape[0] // 2
    place = lax.broadcasted_iota(jnp.int32, (rows, 1), 0)
    for part in range(2):
        terms = terms_of(slice(part * rows, (part + 1) * rows))
        for j in range(slots):
            k = part * slots + j
            inside = (place >= spans_ref[0, k]) & (place < spans_ref[1, k])
            out_ref[k : k + 1, :] = jnp.sum(jnp.where(inside, terms, 0.0), axis=0, keepdims=True)


def proj_kernel(count, last, turn_ref, at_ref, own_ref, other_ref, *refs):
    del at_ref
    pieces, refs = refs[:count], refs[count:]
    if last is None:
        acc_ref, next_ref = refs
    else:
        spans_ref, left_ref, second_ref, out_ref, next_ref, acc_ref = refs
    step = pl.program_id(0)
    rows = own_ref.shape[0]

    @pl.when(step == 0)
    def _():
        next_ref[0] = turn_ref[0]
        acc_ref[...] = jnp.zeros_like(acc_ref)

    factors = jnp.concatenate([p[...] for p in pieces], axis=0)
    for part, tokens in enumerate((own_ref, other_ref)):
        acc_ref[part * rows : (part + 1) * rows] += lax.dot_general(
            tokens[...], factors, (((1,), (1,)), ((), ())), preferred_element_type=jnp.float32
        )

    if last is not None:

        @pl.when(step == pl.num_programs(0) - 1)
        def _():
            def terms(here):
                if last:
                    return (left_ref[here] + second_ref[here]) * acc_ref[here]
                return (left_ref[here] + acc_ref[here]) * second_ref[here]

            score_into(out_ref, spans_ref, terms, rows)


def proj(turn, tokens, rows, pieces, first, steps, last=None, spans=None, others=()):
    depth = pieces[0].shape[1]
    block = depth // steps
    held = sum(p.shape[0] for p in pieces)
    (own, own_row), (other, other_row) = tokens
    whole = pl.BlockSpec((2 * rows, held), lambda k, turn, at: (0, 0))
    scalar = pl.BlockSpec(memory_space=pltpu.SMEM)
    if last is None:
        more_specs, more, scratch = [], (), []
        out_shape, out_spec = (2 * rows, held), whole
    else:
        more_specs, more = [scalar, whole, whole], (spans, *others)
        scratch = [pltpu.VMEM((2 * rows, held), jnp.float32)]
        out_shape = (spans.shape[1], held)
        out_spec = pl.BlockSpec(out_shape, lambda k, turn, at: (0, 0))
    out, turn_next = pl.pallas_call(
        functools.partial(proj_kernel, len(pieces), last),
        out_shape=(
            jax.ShapeDtypeStruct(out_shape, jnp.float32),
            jax.ShapeDtypeStruct((1,), jnp.int32),
        ),
        grid_spec=pltpu.PrefetchScalarGridSpec(
            num_scalar_prefetch=2,
            grid=(steps,),
            in_specs=[
                pl.BlockSpec((rows, block), lambda k, turn, at: (at[1], at[0] * steps + k)),
                pl.BlockSpec((rows, block), lambda k, turn, at: (at[2], at[0] * steps + k)),
            ]
            + [pl.BlockSpec((p.shape[0], block), lambda k, turn, at: (0, k)) for p in pieces]
            + more_specs,
            out_specs=(out_spec, scalar),
            scratch_shapes=scratch,
        ),
        compiler_params=pltpu.CompilerParams(vmem_limit_bytes=VMEM_LIMIT),
        cost_estimate=LITTLE,
    )(turn, jnp.concatenate([first, own_row, other_row]), own, other, *pieces, *more)
    return turn_next, out


def spans_of(slot_ids, lengths):
    widths = bucket_lengths(slot_ids)
    starts = jnp.cumsum(widths) - widths
    return jnp.stack([starts, starts + lengths]).astype(jnp.int32)


def relay(hidden_acts, output_grads, query_left, query_right, bucket_ids, seq_lengths):
    count = lax.axis_size("dp")
    me, group = lax.axis_index("dp"), lax.axis_index("groups")
    z = me // 4
    local, ranks = query_left.shape[:2]
    left = query_left.reshape(local * ranks, -1)
    half = left.shape[1] // 2
    send = functools.partial(flip, count=count)

    acts_there = send(hidden_acts, CORE)
    spans_here = spans_of(bucket_ids, seq_lengths)
    spans = jnp.concatenate([spans_here, send(spans_here, CORE)], axis=1)

    a, b, c = {}, {}, {}
    a["own"] = lax.dynamic_slice_in_dim(left, group * half, half, 1)
    b["own"] = query_right.reshape(local * ranks, -1)
    at_end = (z == 0) | (z == 3)

    def near(piece):
        return send(piece, NEAR)

    def middle(piece):
        return lines(piece, [(1, 2), (2, 1)])

    def outward(piece):
        return lines(piece, [(1, 0), (2, 3)])

    def across(piece):
        return send(piece, ACROSS)

    def over_x(piece):
        return send(piece, COLUMN)

    inside = (~at_end).reshape(1).astype(jnp.int32)
    mine = jnp.reshape(group, (1,)).astype(jnp.int32)
    zero = jnp.zeros((1,), jnp.int32)
    acts = ((hidden_acts, zero), (acts_there, zero))
    groups = (("own", "x", "n", "f"), ("xo", "o", "xn", "xf"))
    tokens_here = hidden_acts.shape[0]
    steps = 4

    def times_a(turn, k):
        return proj(turn, acts, tokens_here, [a[i] for i in groups[k]], mine, steps)

    def times_c(turn, k, *score):
        return proj(turn, acts, tokens_here, [c[i] for i in groups[k]], 1 - mine, steps, *score)

    def times_b(turn, k, *score):
        return proj(turn, grads, tokens_here, [b[i] for i in groups[k]], zero, steps, *score)

    def pause(turn):
        return after(turn, [], inside)[0]

    grads_there = send(output_grads, CORE)
    grads = ((output_grads, zero), (grads_there, zero))

    core = (me & CORE).reshape(1).astype(jnp.int32)
    copies = (1 - mine, left, b["own"])
    turn, made, (a["own"],) = prepare(zero, core, *copies, None, [a["own"]])
    a_mid = middle(a["own"])
    a["n"] = near(a["own"])
    a["x"] = over_x(a["own"])
    turn, (c["own"], b_one, b_two), _ = prepare(turn, 1 - core, *copies, made, [])

    turn, (a_mid, a["n"], a["x"]) = after(turn, [a_mid, a["n"], a["x"]], inside, None, [acts_there])
    a_out = outward(a_mid)
    a_in = middle(a["n"])
    b["x"] = over_x(b_one)
    c["x"] = swap_groups(a["x"])
    turn = pause(turn)

    turn, (a_out, b["x"], a_in, c["x"]) = after(turn, [a_out, b["x"], a_in, c["x"]], inside, None, [grads_there])
    a_last = outward(a_in)
    a["xn"] = over_x(a["n"])
    c["n"] = swap_groups(a["n"])
    b["f"] = across(b_one)
    turn, (a["o"],) = after(turn, [a_out], inside, a_in)
    a["xo"] = over_x(a["o"])
    turn = pause(turn)

    turn, (a["f"], a["xn"], c["n"], b_two) = after(turn, [a_last, a["xn"], c["n"], b_two], inside, a_mid)
    b["n"] = near(b_two)
    a["xf"] = over_x(a["f"])
    c["f"] = swap_groups(a["f"])
    turn, a_first = times_a(turn, 0)

    turn, (b["n"], a["xo"], c["f"], a["o"], a["xn"]) = after(
        turn, [b["n"], a["xo"], c["f"], a["o"], a["xn"]], inside
    )
    c["o"] = swap_groups(a["o"])
    c["xn"] = swap_groups(a["xn"])
    turn, c_first = times_c(turn, 0)

    turn, (b["f"], a["xf"], c["o"], a["xo"]) = after(turn, [b["f"], a["xf"], c["o"], a["xo"]], inside)
    b["o"] = near(b["f"])
    b["xf"] = over_x(b["f"])
    c["xo"] = swap_groups(a["xo"])
    turn, score_first = times_b(turn, 0, True, spans, (a_first, c_first))

    split = c["f"].shape[0] // 2
    turn, (b["o"], b["xf"], c["xn"], b_over, a["xf"], c["f"]) = after(
        turn, [b["o"], b["xf"], c["xn"], b["x"], a["xf"], c["f"]], inside
    )
    b["xo"] = over_x(b["o"])
    b["xn"] = near(b_over)
    c["top"] = over_x(c["f"][:split])
    c["low"] = swap_groups(a["xf"][split:])
    turn, a_second = times_a(turn, 1)

    turn, (b["xo"], c["xo"], b["xn"]) = after(turn, [b["xo"], c["xo"], b["xn"]], inside)
    turn, b_second = times_b(turn, 1)
    groups = (groups[0], ("xo", "o", "xn", "top", "low"))
    turn, score_second = times_c(turn, 1, False, spans, (a_second, b_second))
    sums = [score_first, score_second]

    slots = bucket_ids.shape[0]
    ours = jnp.concatenate([x[:slots] for x in sums], axis=1)
    others = send(jnp.concatenate([x[slots:] for x in sums], axis=1), CORE)
    codes = (0, COLUMN, NEAR, ACROSS, OPPOSITE | COLUMN, OPPOSITE, NEAR | COLUMN, ACROSS | COLUMN)
    codes = jnp.array(codes, jnp.int32)
    owner = jnp.concatenate([me ^ codes, me ^ CORE ^ codes])
    query = owner[:, None] * local + jnp.arange(local, dtype=jnp.int32)[None, :]
    query = jnp.repeat(query.reshape(-1), ranks)
    placed = query[None, :] == jnp.arange(count * local, dtype=jnp.int32)[:, None]
    return lax.dot_general(
        placed.astype(jnp.float32),
        jnp.concatenate([ours, others], axis=1),
        (((1,), (1,)), ((), ())),
        precision=lax.Precision.HIGHEST,
        preferred_element_type=jnp.float32,
    )


def solution(mesh):
    sizes = mesh.shape
    fits = sizes["dp"] == 16 and sizes["groups"] == 2 and sizes["tensor"] == 1
    return jax.shard_map(
        relay if fits else gather_whole,
        mesh=mesh,
        in_specs=(
            P(("groups", "dp"), "tensor"),
            P(("groups", "dp"), "tensor"),
            P("dp", None, "tensor"),
            P("dp", None, "tensor"),
            P(("groups", "dp")),
            P(("groups", "dp")),
        ),
        out_specs=P("tensor", ("groups", "dp")),
        check_vma=False,
    )
```

```python
import functools

import jax
import jax.numpy as jnp
from jax import lax
from jax.experimental import pallas as pl
from jax.experimental.pallas import tpu as pltpu
from jax.sharding import PartitionSpec as P

BUCKET = 128


def bucket_lengths(slot_ids):
    return BUCKET * jnp.where(
        slot_ids == 0, 1, jnp.where(slot_ids == 1, 2, jnp.where(slot_ids == 2, 4, 0))
    ).astype(jnp.int32)


def slot_matrix(slot_ids, lengths, positions):
    widths = bucket_lengths(slot_ids)
    starts = jnp.cumsum(widths) - widths
    place = jnp.arange(positions, dtype=jnp.int32)[:, None]
    inside = (place >= starts[None, :]) & (place < starts[None, :] + lengths[None, :])
    return inside.astype(jnp.float32)


def project(acts, factors):
    rows = factors.reshape(-1, factors.shape[2])
    return lax.dot_general(acts, rows, (((1,), (1,)), ((), ())), preferred_element_type=jnp.float32)


def gather_whole(hidden_acts, output_grads, query_left, query_right, bucket_ids, seq_lengths):
    tokens_here = hidden_acts.shape[0]
    rank_count = query_left.shape[1]
    left_all, right_all = (
        lax.all_gather(query_left, "dp", axis=0, tiled=True),
        lax.all_gather(query_right, "dp", axis=0, tiled=True),
    )
    left_proj = project(hidden_acts, left_all)
    right_proj = project(output_grads, right_all)
    queries = left_proj.shape[1] // rank_count
    left_terms = left_proj.reshape(tokens_here, queries, rank_count)
    right_terms = right_proj.reshape(tokens_here, queries, rank_count)
    left_terms, right_terms = lax.psum((left_terms, right_terms), "tensor")
    share_size = queries // lax.axis_size("tensor")
    first_query = lax.axis_index("tensor") * share_size
    left_terms = lax.dynamic_slice_in_dim(left_terms, first_query, share_size, 1)
    right_terms = lax.dynamic_slice_in_dim(right_terms, first_query, share_size, 1)
    token_term = jnp.sum(left_terms * right_terms, axis=2)
    slot_mask = slot_matrix(bucket_ids, seq_lengths, tokens_here)
    return jnp.dot(
        token_term.T, slot_mask, precision=lax.Precision.HIGHEST, preferred_element_type=jnp.float32
    )


CORE, COLUMN, NEAR, ACROSS, OPPOSITE = 1, 2, 4, 12, 8
LITTLE = pl.CostEstimate(flops=1, bytes_accessed=1, transcendentals=0)
VMEM_LIMIT = 255 * 256 * 1024


def flip(array, code, count):
    return lax.ppermute(array, "dp", [(i, i ^ code) for i in range(count)])


def swap_groups(array):
    return lax.ppermute(array, "groups", [(0, 1), (1, 0)])


PARTS = 4


def through(held, arrived, gone, source, target):
    rows = source.shape[0] // PARTS
    parts = [pl.ds(i * rows, rows) for i in range(PARTS)]
    come = [pltpu.make_async_copy(source.at[p], held.at[p], arrived.at[i]) for i, p in enumerate(parts)]
    go = [pltpu.make_async_copy(held.at[p], target.at[p], gone.at[i]) for i, p in enumerate(parts)]
    for copy in come:
        copy.start()
    for first, second in zip(come, go):
        first.wait()
        second.start()
    for copy in go:
        copy.wait()


def after_kernel(count, merges, inside_ref, turn_ref, *refs):
    if merges:
        refs, staging = refs[:-3], refs[-3:]
        source, target = refs[0], refs[-1 - count]

        @pl.when(inside_ref[0] == 1)
        def _():
            through(*staging, source, target)

    refs[-1][0] = turn_ref[0]


def after(turn, arrays, inside, merge=None, there=()):
    count = len(arrays)
    scratch = []
    if merge is not None:
        there = (merge, *there)
        scratch = [pltpu.VMEM(merge.shape, merge.dtype)] + [pltpu.SemaphoreType.DMA((PARTS,))] * 2
    hbm = pl.BlockSpec(memory_space=pltpu.HBM)
    scalar = pl.BlockSpec(memory_space=pltpu.SMEM)
    *arrays, turn = pl.pallas_call(
        functools.partial(after_kernel, count, merge is not None),
        out_shape=[jax.ShapeDtypeStruct(x.shape, x.dtype) for x in (*arrays, turn)],
        in_specs=[scalar] * 2 + [hbm] * (len(there) + count),
        out_specs=[hbm] * count + [scalar],
        input_output_aliases={2 + len(there) + i: i for i in range(count)},
        scratch_shapes=scratch,
        compiler_params=pltpu.CompilerParams(vmem_limit_bytes=VMEM_LIMIT),
        cost_estimate=LITTLE,
    )(inside, turn, *there, *arrays)
    return turn, arrays


def prepare_kernel(works_ref, turn_ref, first_ref, left_ref, right_ref, *refs):
    half_ref, one_ref, two_ref, next_ref, half_held, right_held, arrived, gone = refs[-8:]
    next_ref[0] = turn_ref[0]
    width = half_ref.shape[1]

    @pl.when(works_ref[0] == 1)
    def _():
        start = pl.multiple_of(first_ref[0] * width, width)
        through(half_held, arrived, gone, left_ref.at[:, pl.ds(start, width)], half_ref)
        for target in (one_ref, two_ref):
            through(right_held, arrived, gone, right_ref, target)


def prepare(turn, works, first, left, right, made, passed):
    rows, width = left.shape[0], left.shape[1] // 2
    shapes = [(rows, width), right.shape, right.shape]
    out_shape = [jax.ShapeDtypeStruct(x, left.dtype) for x in shapes]
    made = () if made is None else made
    given = (*passed, *made)
    hbm = pl.BlockSpec(memory_space=pltpu.HBM)
    scalar = pl.BlockSpec(memory_space=pltpu.SMEM)
    aliases = {5 + i: i for i in range(len(given))}
    outs = pl.pallas_call(
        prepare_kernel,
        out_shape=[jax.ShapeDtypeStruct(x.shape, x.dtype) for x in passed]
        + out_shape
        + [jax.ShapeDtypeStruct(turn.shape, turn.dtype)],
        in_specs=[scalar] * 3 + [hbm] * (2 + len(given)),
        out_specs=[hbm] * (len(passed) + 3) + [scalar],
        input_output_aliases=aliases,
        scratch_shapes=[pltpu.VMEM((rows, width), left.dtype), pltpu.VMEM(right.shape, right.dtype)]
        + [pltpu.SemaphoreType.DMA((PARTS,))] * 2,
        compiler_params=pltpu.CompilerParams(vmem_limit_bytes=VMEM_LIMIT),
        cost_estimate=LITTLE,
    )(works, turn, first, left, right, *given)
    return outs[-1], outs[len(passed) : -1], outs[: len(passed)]


def lines(array, pairs):
    return lax.ppermute(
        array, "dp", [(a * 4 + rest, b * 4 + rest) for a, b in pairs for rest in range(4)]
    )


def score_into(out_ref, spans_ref, terms_of, rows):
    slots = out_ref.shape[0] // 2
    place = lax.broadcasted_iota(jnp.int32, (rows, 1), 0)
    for part in range(2):
        terms = terms_of(slice(part * rows, (part + 1) * rows))
        for j in range(slots):
            k = part * slots + j
            inside = (place >= spans_ref[0, k]) & (place < spans_ref[1, k])
            out_ref[k : k + 1, :] = jnp.sum(jnp.where(inside, terms, 0.0), axis=0, keepdims=True)


def proj_kernel(count, last, turn_ref, at_ref, own_ref, other_ref, *refs):
    del at_ref
    pieces, refs = refs[:count], refs[count:]
    if last is None:
        acc_ref, next_ref = refs
    else:
        spans_ref, left_ref, second_ref, out_ref, next_ref, acc_ref = refs
    step = pl.program_id(0)
    rows = own_ref.shape[0]

    @pl.when(step == 0)
    def _():
        next_ref[0] = turn_ref[0]
        acc_ref[...] = jnp.zeros_like(acc_ref)

    factors = jnp.concatenate([p[...] for p in pieces], axis=0)
    for part, tokens in enumerate((own_ref, other_ref)):
        acc_ref[part * rows : (part + 1) * rows] += lax.dot_general(
            tokens[...], factors, (((1,), (1,)), ((), ())), preferred_element_type=jnp.float32
        )

    if last is not None:

        @pl.when(step == pl.num_programs(0) - 1)
        def _():
            def terms(here):
                if last:
                    return (left_ref[here] + second_ref[here]) * acc_ref[here]
                return (left_ref[here] + acc_ref[here]) * second_ref[here]

            score_into(out_ref, spans_ref, terms, rows)


def proj(turn, tokens, rows, pieces, first, steps, last=None, spans=None, others=()):
    depth = pieces[0].shape[1]
    block = depth // steps
    held = sum(p.shape[0] for p in pieces)
    (own, own_row), (other, other_row) = tokens
    whole = pl.BlockSpec((2 * rows, held), lambda k, turn, at: (0, 0))
    scalar = pl.BlockSpec(memory_space=pltpu.SMEM)
    if last is None:
        more_specs, more, scratch = [], (), []
        out_shape, out_spec = (2 * rows, held), whole
    else:
        more_specs, more = [scalar, whole, whole], (spans, *others)
        scratch = [pltpu.VMEM((2 * rows, held), jnp.float32)]
        out_shape = (spans.shape[1], held)
        out_spec = pl.BlockSpec(out_shape, lambda k, turn, at: (0, 0))
    out, turn_next = pl.pallas_call(
        functools.partial(proj_kernel, len(pieces), last),
        out_shape=(
            jax.ShapeDtypeStruct(out_shape, jnp.float32),
            jax.ShapeDtypeStruct((1,), jnp.int32),
        ),
        grid_spec=pltpu.PrefetchScalarGridSpec(
            num_scalar_prefetch=2,
            grid=(steps,),
            in_specs=[
                pl.BlockSpec((rows, block), lambda k, turn, at: (at[1], at[0] * steps + k)),
                pl.BlockSpec((rows, block), lambda k, turn, at: (at[2], at[0] * steps + k)),
            ]
            + [pl.BlockSpec((p.shape[0], block), lambda k, turn, at: (0, k)) for p in pieces]
            + more_specs,
            out_specs=(out_spec, scalar),
            scratch_shapes=scratch,
        ),
        compiler_params=pltpu.CompilerParams(vmem_limit_bytes=VMEM_LIMIT),
        cost_estimate=LITTLE,
    )(turn, jnp.concatenate([first, own_row, other_row]), own, other, *pieces, *more)
    return turn_next, out


def spans_of(slot_ids, lengths):
    widths = bucket_lengths(slot_ids)
    starts = jnp.cumsum(widths) - widths
    return jnp.stack([starts, starts + lengths]).astype(jnp.int32)


def relay(hidden_acts, output_grads, query_left, query_right, bucket_ids, seq_lengths):
    count = lax.axis_size("dp")
    me, group = lax.axis_index("dp"), lax.axis_index("groups")
    z = me // 4
    local, ranks = query_left.shape[:2]
    left = query_left.reshape(local * ranks, -1)
    half = left.shape[1] // 2
    send = functools.partial(flip, count=count)

    acts_there = send(hidden_acts, CORE)
    spans_here = spans_of(bucket_ids, seq_lengths)
    spans = jnp.concatenate([spans_here, send(spans_here, CORE)], axis=1)

    a, b, c = {}, {}, {}
    a["own"] = lax.dynamic_slice_in_dim(left, group * half, half, 1)
    b["own"] = query_right.reshape(local * ranks, -1)
    at_end = (z == 0) | (z == 3)

    def near(piece):
        return send(piece, NEAR)

    def middle(piece):
        return lines(piece, [(1, 2), (2, 1)])

    def ends(piece):
        return lines(piece, [(0, 3), (3, 0)])

    def across(piece):
        return send(piece, ACROSS)

    def over_x(piece):
        return send(piece, COLUMN)

    inside = (~at_end).reshape(1).astype(jnp.int32)
    mine = jnp.reshape(group, (1,)).astype(jnp.int32)
    zero = jnp.zeros((1,), jnp.int32)
    acts = ((hidden_acts, zero), (acts_there, zero))
    groups = (("own", "x", "n", "f"), ("xn", "xf", "o", "xo"))
    tokens_here = hidden_acts.shape[0]
    steps = 4

    def times_a(turn, k):
        return proj(turn, acts, tokens_here, [a[i] for i in groups[k]], mine, steps)

    def times_c(turn, k, *score):
        return proj(turn, acts, tokens_here, [c[i] for i in groups[k]], 1 - mine, steps, *score)

    def times_b(turn, k, *score):
        return proj(turn, grads, tokens_here, [b[i] for i in groups[k]], zero, steps, *score)

    def pause(turn):
        return after(turn, [], inside)[0]

    codes = (0, COLUMN, NEAR, ACROSS, NEAR | COLUMN, ACROSS | COLUMN, OPPOSITE, OPPOSITE | COLUMN)
    codes = jnp.array(codes, jnp.int32)
    owner = jnp.concatenate([me ^ codes, me ^ CORE ^ codes])
    query = owner[:, None] * local + jnp.arange(local, dtype=jnp.int32)[None, :]
    query = jnp.repeat(query.reshape(-1), ranks)
    placed = query[None, :] == jnp.arange(count * local, dtype=jnp.int32)[:, None]
    placed = placed.astype(jnp.float32)

    grads_there = send(output_grads, CORE)
    grads = ((output_grads, zero), (grads_there, zero))

    core = (me & CORE).reshape(1).astype(jnp.int32)
    copies = (1 - mine, left, b["own"])
    turn, made, (a["own"],) = prepare(zero, core, *copies, None, [a["own"]])
    a["x"] = over_x(a["own"])
    a["n"] = near(a["own"])
    a_mid = middle(a["own"])
    turn, (c["own"], b_one, b_two), _ = prepare(turn, 1 - core, *copies, made, [])

    turn, (a["x"], a["n"], a_mid, a["own"]) = after(
        turn, [a["x"], a["n"], a_mid, a["own"]], inside, None, [acts_there]
    )
    a_end = ends(a["own"])
    b["x"] = over_x(b_one)
    c["x"] = swap_groups(a["x"])
    turn = pause(turn)

    turn, (a["f"], b["x"], c["x"]) = after(turn, [a_end, b["x"], c["x"]], inside, a_mid, [grads_there])
    a["o"] = near(a["f"])
    a["xn"] = over_x(a["n"])
    c["n"] = swap_groups(a["n"])
    b["f"] = across(b_one)
    turn = pause(turn)

    turn, (a["o"], a["xn"], c["n"], b_two) = after(turn, [a["o"], a["xn"], c["n"], b_two], inside)
    b["n"] = near(b_two)
    a["xf"] = over_x(a["f"])
    c["f"] = swap_groups(a["f"])
    turn, a_first = times_a(turn, 0)

    turn, (b["n"], a["xf"], c["f"], a["o"], a["xn"]) = after(
        turn, [b["n"], a["xf"], c["f"], a["o"], a["xn"]], inside
    )
    a["xo"] = over_x(a["o"])
    c["o"] = swap_groups(a["o"])
    c["xn"] = swap_groups(a["xn"])
    turn, c_first = times_c(turn, 0)

    turn, (b["f"], a["xo"], c["o"], a["xf"]) = after(turn, [b["f"], a["xo"], c["o"], a["xf"]], inside)
    b["o"] = near(b["f"])
    b["xf"] = over_x(b["f"])
    c["xf"] = swap_groups(a["xf"])
    turn, score_first = times_b(turn, 0, True, spans, (a_first, c_first))

    split = c["o"].shape[0] // 2
    turn, (b["o"], b["xf"], c["xn"], b_over, a["xo"], c["o"], placed) = after(
        turn, [b["o"], b["xf"], c["xn"], b["x"], a["xo"], c["o"], placed], inside
    )
    b["xo"] = over_x(b["o"])
    b["xn"] = near(b_over)
    c["top"] = over_x(c["o"][:split])
    c["low"] = swap_groups(a["xo"][split:])
    turn, a_second = times_a(turn, 1)

    turn, (b["xo"], c["xf"], b["xn"]) = after(turn, [b["xo"], c["xf"], b["xn"]], inside)
    turn, b_second = times_b(turn, 1)
    groups = (groups[0], ("xn", "xf", "o", "top", "low"))
    turn, score_second = times_c(turn, 1, False, spans, (a_second, b_second))
    sums = [score_first, score_second]

    slots = bucket_ids.shape[0]
    others = [send(x, CORE) for x in sums]
    held = [x[:slots] for x in sums] + [x[slots:] for x in others]
    return lax.dot_general(
        placed,
        jnp.concatenate(held, axis=1),
        (((1,), (1,)), ((), ())),
        precision=lax.Precision.HIGHEST,
        preferred_element_type=jnp.float32,
    )


def solution(mesh):
    sizes = mesh.shape
    fits = sizes["dp"] == 16 and sizes["groups"] == 2 and sizes["tensor"] == 1
    return jax.shard_map(
        relay if fits else gather_whole,
        mesh=mesh,
        in_specs=(
            P(("groups", "dp"), "tensor"),
            P(("groups", "dp"), "tensor"),
            P("dp", None, "tensor"),
            P("dp", None, "tensor"),
            P(("groups", "dp")),
            P(("groups", "dp")),
        ),
        out_specs=P("tensor", ("groups", "dp")),
        check_vma=False,
    )
```

```python
import functools

import jax
import jax.numpy as jnp
from jax import lax
from jax.experimental import pallas as pl
from jax.experimental.pallas import tpu as pltpu
from jax.sharding import PartitionSpec as P

BUCKET = 128


def bucket_lengths(slot_ids):
    return BUCKET * jnp.where(
        slot_ids == 0, 1, jnp.where(slot_ids == 1, 2, jnp.where(slot_ids == 2, 4, 0))
    ).astype(jnp.int32)


def slot_matrix(slot_ids, lengths, positions):
    widths = bucket_lengths(slot_ids)
    starts = jnp.cumsum(widths) - widths
    place = jnp.arange(positions, dtype=jnp.int32)[:, None]
    inside = (place >= starts[None, :]) & (place < starts[None, :] + lengths[None, :])
    return inside.astype(jnp.float32)


def project(acts, factors):
    rows = factors.reshape(-1, factors.shape[2])
    return lax.dot_general(acts, rows, (((1,), (1,)), ((), ())), preferred_element_type=jnp.float32)


def gather_whole(hidden_acts, output_grads, query_left, query_right, bucket_ids, seq_lengths):
    tokens_here = hidden_acts.shape[0]
    rank_count = query_left.shape[1]
    left_all, right_all = (
        lax.all_gather(query_left, "dp", axis=0, tiled=True),
        lax.all_gather(query_right, "dp", axis=0, tiled=True),
    )
    left_proj = project(hidden_acts, left_all)
    right_proj = project(output_grads, right_all)
    queries = left_proj.shape[1] // rank_count
    left_terms = left_proj.reshape(tokens_here, queries, rank_count)
    right_terms = right_proj.reshape(tokens_here, queries, rank_count)
    left_terms, right_terms = lax.psum((left_terms, right_terms), "tensor")
    share_size = queries // lax.axis_size("tensor")
    first_query = lax.axis_index("tensor") * share_size
    left_terms = lax.dynamic_slice_in_dim(left_terms, first_query, share_size, 1)
    right_terms = lax.dynamic_slice_in_dim(right_terms, first_query, share_size, 1)
    token_term = jnp.sum(left_terms * right_terms, axis=2)
    slot_mask = slot_matrix(bucket_ids, seq_lengths, tokens_here)
    return jnp.dot(
        token_term.T, slot_mask, precision=lax.Precision.HIGHEST, preferred_element_type=jnp.float32
    )


CORE, COLUMN, NEAR, ACROSS, OPPOSITE = 1, 2, 4, 12, 8
LITTLE = pl.CostEstimate(flops=1, bytes_accessed=1, transcendentals=0)
VMEM_LIMIT = 255 * 256 * 1024


def flip(array, code, count):
    return lax.ppermute(array, "dp", [(i, i ^ code) for i in range(count)])


def swap_groups(array):
    return lax.ppermute(array, "groups", [(0, 1), (1, 0)])


PARTS = 4


def through(held, arrived, gone, source, target):
    rows = source.shape[0] // PARTS
    parts = [pl.ds(i * rows, rows) for i in range(PARTS)]
    come = [pltpu.make_async_copy(source.at[p], held.at[p], arrived.at[i]) for i, p in enumerate(parts)]
    go = [pltpu.make_async_copy(held.at[p], target.at[p], gone.at[i]) for i, p in enumerate(parts)]
    for copy in come:
        copy.start()
    for first, second in zip(come, go):
        first.wait()
        second.start()
    for copy in go:
        copy.wait()


def after_kernel(count, merges, inside_ref, turn_ref, *refs):
    if merges:
        refs, staging = refs[:-3], refs[-3:]
        source, target = refs[0], refs[-1 - count]

        @pl.when(inside_ref[0] == 1)
        def _():
            through(*staging, source, target)

    refs[-1][0] = turn_ref[0]


def after(turn, arrays, inside, merge=None, there=()):
    count = len(arrays)
    scratch = []
    if merge is not None:
        there = (merge, *there)
        scratch = [pltpu.VMEM(merge.shape, merge.dtype)] + [pltpu.SemaphoreType.DMA((PARTS,))] * 2
    hbm = pl.BlockSpec(memory_space=pltpu.HBM)
    scalar = pl.BlockSpec(memory_space=pltpu.SMEM)
    *arrays, turn = pl.pallas_call(
        functools.partial(after_kernel, count, merge is not None),
        out_shape=[jax.ShapeDtypeStruct(x.shape, x.dtype) for x in (*arrays, turn)],
        in_specs=[scalar] * 2 + [hbm] * (len(there) + count),
        out_specs=[hbm] * count + [scalar],
        input_output_aliases={2 + len(there) + i: i for i in range(count)},
        scratch_shapes=scratch,
        compiler_params=pltpu.CompilerParams(vmem_limit_bytes=VMEM_LIMIT),
        cost_estimate=LITTLE,
    )(inside, turn, *there, *arrays)
    return turn, arrays


def prepare_kernel(works_ref, turn_ref, first_ref, left_ref, right_ref, *refs):
    half_ref, one_ref, two_ref, next_ref, half_held, right_held, arrived, gone = refs[-8:]
    next_ref[0] = turn_ref[0]
    width = half_ref.shape[1]

    @pl.when(works_ref[0] == 1)
    def _():
        start = pl.multiple_of(first_ref[0] * width, width)
        through(half_held, arrived, gone, left_ref.at[:, pl.ds(start, width)], half_ref)
        for target in (one_ref, two_ref):
            through(right_held, arrived, gone, right_ref, target)


def prepare(turn, works, first, left, right, made, passed):
    rows, width = left.shape[0], left.shape[1] // 2
    shapes = [(rows, width), right.shape, right.shape]
    out_shape = [jax.ShapeDtypeStruct(x, left.dtype) for x in shapes]
    made = () if made is None else made
    given = (*passed, *made)
    hbm = pl.BlockSpec(memory_space=pltpu.HBM)
    scalar = pl.BlockSpec(memory_space=pltpu.SMEM)
    aliases = {5 + i: i for i in range(len(given))}
    outs = pl.pallas_call(
        prepare_kernel,
        out_shape=[jax.ShapeDtypeStruct(x.shape, x.dtype) for x in passed]
        + out_shape
        + [jax.ShapeDtypeStruct(turn.shape, turn.dtype)],
        in_specs=[scalar] * 3 + [hbm] * (2 + len(given)),
        out_specs=[hbm] * (len(passed) + 3) + [scalar],
        input_output_aliases=aliases,
        scratch_shapes=[pltpu.VMEM((rows, width), left.dtype), pltpu.VMEM(right.shape, right.dtype)]
        + [pltpu.SemaphoreType.DMA((PARTS,))] * 2,
        compiler_params=pltpu.CompilerParams(vmem_limit_bytes=VMEM_LIMIT),
        cost_estimate=LITTLE,
    )(works, turn, first, left, right, *given)
    return outs[-1], outs[len(passed) : -1], outs[: len(passed)]


def lines(array, pairs):
    return lax.ppermute(
        array, "dp", [(a * 4 + rest, b * 4 + rest) for a, b in pairs for rest in range(4)]
    )


def score_into(out_ref, spans_ref, terms_of, rows):
    slots = out_ref.shape[0] // 2
    place = lax.broadcasted_iota(jnp.int32, (rows, 1), 0)
    for part in range(2):
        terms = terms_of(slice(part * rows, (part + 1) * rows))
        for j in range(slots):
            k = part * slots + j
            inside = (place >= spans_ref[0, k]) & (place < spans_ref[1, k])
            out_ref[k : k + 1, :] = jnp.sum(jnp.where(inside, terms, 0.0), axis=0, keepdims=True)


def proj_kernel(count, last, turn_ref, at_ref, own_ref, other_ref, *refs):
    del at_ref
    pieces, refs = refs[:count], refs[count:]
    if last is None:
        acc_ref, next_ref = refs
    else:
        spans_ref, left_ref, second_ref, out_ref, next_ref, acc_ref = refs
    step = pl.program_id(0)
    rows = own_ref.shape[0]

    @pl.when(step == 0)
    def _():
        next_ref[0] = turn_ref[0]
        acc_ref[...] = jnp.zeros_like(acc_ref)

    factors = jnp.concatenate([p[...] for p in pieces], axis=0)
    for part, tokens in enumerate((own_ref, other_ref)):
        acc_ref[part * rows : (part + 1) * rows] += lax.dot_general(
            tokens[...], factors, (((1,), (1,)), ((), ())), preferred_element_type=jnp.float32
        )

    if last is not None:

        @pl.when(step == pl.num_programs(0) - 1)
        def _():
            def terms(here):
                if last:
                    return (left_ref[here] + second_ref[here]) * acc_ref[here]
                return (left_ref[here] + acc_ref[here]) * second_ref[here]

            score_into(out_ref, spans_ref, terms, rows)


def proj(turn, tokens, rows, pieces, first, steps, last=None, spans=None, others=()):
    depth = pieces[0].shape[1]
    block = depth // steps
    held = sum(p.shape[0] for p in pieces)
    (own, own_row), (other, other_row) = tokens
    whole = pl.BlockSpec((2 * rows, held), lambda k, turn, at: (0, 0))
    scalar = pl.BlockSpec(memory_space=pltpu.SMEM)
    if last is None:
        more_specs, more, scratch = [], (), []
        out_shape, out_spec = (2 * rows, held), whole
    else:
        more_specs, more = [scalar, whole, whole], (spans, *others)
        scratch = [pltpu.VMEM((2 * rows, held), jnp.float32)]
        out_shape = (spans.shape[1], held)
        out_spec = pl.BlockSpec(out_shape, lambda k, turn, at: (0, 0))
    out, turn_next = pl.pallas_call(
        functools.partial(proj_kernel, len(pieces), last),
        out_shape=(
            jax.ShapeDtypeStruct(out_shape, jnp.float32),
            jax.ShapeDtypeStruct((1,), jnp.int32),
        ),
        grid_spec=pltpu.PrefetchScalarGridSpec(
            num_scalar_prefetch=2,
            grid=(steps,),
            in_specs=[
                pl.BlockSpec((rows, block), lambda k, turn, at: (at[1], at[0] * steps + k)),
                pl.BlockSpec((rows, block), lambda k, turn, at: (at[2], at[0] * steps + k)),
            ]
            + [pl.BlockSpec((p.shape[0], block), lambda k, turn, at: (0, k)) for p in pieces]
            + more_specs,
            out_specs=(out_spec, scalar),
            scratch_shapes=scratch,
        ),
        compiler_params=pltpu.CompilerParams(vmem_limit_bytes=VMEM_LIMIT),
        cost_estimate=LITTLE,
    )(turn, jnp.concatenate([first, own_row, other_row]), own, other, *pieces, *more)
    return turn_next, out


def spans_of(slot_ids, lengths):
    widths = bucket_lengths(slot_ids)
    starts = jnp.cumsum(widths) - widths
    return jnp.stack([starts, starts + lengths]).astype(jnp.int32)


def relay(hidden_acts, output_grads, query_left, query_right, bucket_ids, seq_lengths):
    count = lax.axis_size("dp")
    me, group = lax.axis_index("dp"), lax.axis_index("groups")
    z = me // 4
    local, ranks = query_left.shape[:2]
    left = query_left.reshape(local * ranks, -1)
    half = left.shape[1] // 2
    send = functools.partial(flip, count=count)

    acts_there = send(hidden_acts, CORE)
    sizes_there = send(jnp.concatenate([bucket_ids, seq_lengths]), CORE)

    a, b, c = {}, {}, {}
    a["own"] = lax.dynamic_slice_in_dim(left, group * half, half, 1)
    b["own"] = query_right.reshape(local * ranks, -1)
    at_end = (z == 0) | (z == 3)

    def near(piece):
        return send(piece, NEAR)

    def middle(piece):
        return lines(piece, [(1, 2), (2, 1)])

    def ends(piece):
        return lines(piece, [(0, 3), (3, 0)])

    def across(piece):
        return send(piece, ACROSS)

    def over_x(piece):
        return send(piece, COLUMN)

    inside = (~at_end).reshape(1).astype(jnp.int32)
    mine = jnp.reshape(group, (1,)).astype(jnp.int32)
    zero = jnp.zeros((1,), jnp.int32)
    acts = ((hidden_acts, zero), (acts_there, zero))
    groups = (("own", "x", "n", "f"), ("xn", "xf", "o", "xo"))
    tokens_here = hidden_acts.shape[0]
    steps = 4

    def times_a(turn, k):
        return proj(turn, acts, tokens_here, [a[i] for i in groups[k]], mine, steps)

    def times_c(turn, k, *score):
        return proj(turn, acts, tokens_here, [c[i] for i in groups[k]], 1 - mine, steps, *score)

    def times_b(turn, k, *score):
        return proj(turn, grads, tokens_here, [b[i] for i in groups[k]], zero, steps, *score)

    def pause(turn):
        return after(turn, [], inside)[0]

    codes = (0, COLUMN, NEAR, ACROSS, NEAR | COLUMN, ACROSS | COLUMN, OPPOSITE, OPPOSITE | COLUMN)
    codes = jnp.array(codes, jnp.int32)
    owner = jnp.concatenate([me ^ codes, me ^ CORE ^ codes])
    query = owner[:, None] * local + jnp.arange(local, dtype=jnp.int32)[None, :]
    query = jnp.repeat(query.reshape(-1), ranks)
    placed = query[None, :] == jnp.arange(count * local, dtype=jnp.int32)[:, None]
    placed = placed.astype(jnp.float32)

    grads_there = send(output_grads, CORE)
    grads = ((output_grads, zero), (grads_there, zero))

    core = (me & CORE).reshape(1).astype(jnp.int32)
    copies = (1 - mine, left, b["own"])
    turn, made, (a["own"], sizes_there) = prepare(zero, core, *copies, None, [a["own"], sizes_there])
    a["x"] = over_x(a["own"])
    a["n"] = near(a["own"])
    a_mid = middle(a["own"])
    turn, (c["own"], b_one, b_two), _ = prepare(turn, 1 - core, *copies, made, [])
    spans = [spans_of(bucket_ids, seq_lengths), spans_of(*jnp.split(sizes_there, 2))]
    spans = jnp.concatenate(spans, axis=1)

    turn, (a["x"], a["n"], a_mid, a["own"]) = after(
        turn, [a["x"], a["n"], a_mid, a["own"]], inside, None, [acts_there]
    )
    a_end = ends(a["own"])
    b["x"] = over_x(b_one)
    c["x"] = swap_groups(a["x"])
    turn = pause(turn)

    turn, (a["f"], b["x"], c["x"]) = after(turn, [a_end, b["x"], c["x"]], inside, a_mid, [grads_there])
    a["o"] = near(a["f"])
    a["xn"] = over_x(a["n"])
    c["n"] = swap_groups(a["n"])
    b["f"] = across(b_one)
    turn = pause(turn)

    turn, (a["o"], a["xn"], c["n"], b_two) = after(turn, [a["o"], a["xn"], c["n"], b_two], inside)
    b["n"] = near(b_two)
    a["xf"] = over_x(a["f"])
    c["f"] = swap_groups(a["f"])
    turn, a_first = times_a(turn, 0)

    turn, (b["n"], a["xf"], c["f"], a["o"], a["xn"]) = after(
        turn, [b["n"], a["xf"], c["f"], a["o"], a["xn"]], inside
    )
    a["xo"] = over_x(a["o"])
    c["o"] = swap_groups(a["o"])
    c["xn"] = swap_groups(a["xn"])
    turn, c_first = times_c(turn, 0)

    turn, (b["f"], a["xo"], c["o"], a["xf"]) = after(turn, [b["f"], a["xo"], c["o"], a["xf"]], inside)
    b["o"] = near(b["f"])
    b["xf"] = over_x(b["f"])
    c["xf"] = swap_groups(a["xf"])
    turn, score_first = times_b(turn, 0, True, spans, (a_first, c_first))

    split = c["o"].shape[0] // 2
    turn, (b["o"], b["xf"], c["xn"], b_over, a["xo"], c["o"], placed) = after(
        turn, [b["o"], b["xf"], c["xn"], b["x"], a["xo"], c["o"], placed], inside
    )
    b["xo"] = over_x(b["o"])
    b["xn"] = near(b_over)
    c["top"] = over_x(c["o"][:split])
    c["low"] = swap_groups(a["xo"][split:])
    turn, a_second = times_a(turn, 1)

    turn, (b["xo"], c["xf"], b["xn"]) = after(turn, [b["xo"], c["xf"], b["xn"]], inside)
    turn, b_second = times_b(turn, 1)
    groups = (groups[0], ("xn", "xf", "o", "top", "low"))
    turn, score_second = times_c(turn, 1, False, spans, (a_second, b_second))
    sums = [score_first, score_second]

    slots = bucket_ids.shape[0]
    others = [send(x, CORE) for x in sums]
    held = [x[:slots] for x in sums] + [x[slots:] for x in others]
    return lax.dot_general(
        placed,
        jnp.concatenate(held, axis=1),
        (((1,), (1,)), ((), ())),
        precision=lax.Precision.HIGHEST,
        preferred_element_type=jnp.float32,
    )


def solution(mesh):
    sizes = mesh.shape
    fits = sizes["dp"] == 16 and sizes["groups"] == 2 and sizes["tensor"] == 1
    return jax.shard_map(
        relay if fits else gather_whole,
        mesh=mesh,
        in_specs=(
            P(("groups", "dp"), "tensor"),
            P(("groups", "dp"), "tensor"),
            P("dp", None, "tensor"),
            P("dp", None, "tensor"),
            P(("groups", "dp")),
            P(("groups", "dp")),
        ),
        out_specs=P("tensor", ("groups", "dp")),
        check_vma=False,
    )
```

```python
import functools

import jax
import jax.numpy as jnp
from jax import lax
from jax.experimental import pallas as pl
from jax.experimental.pallas import tpu as pltpu
from jax.sharding import PartitionSpec as P

BUCKET = 128


def bucket_lengths(slot_ids):
    return BUCKET * jnp.where(
        slot_ids == 0, 1, jnp.where(slot_ids == 1, 2, jnp.where(slot_ids == 2, 4, 0))
    ).astype(jnp.int32)


def slot_matrix(slot_ids, lengths, positions):
    widths = bucket_lengths(slot_ids)
    starts = jnp.cumsum(widths) - widths
    place = jnp.arange(positions, dtype=jnp.int32)[:, None]
    inside = (place >= starts[None, :]) & (place < starts[None, :] + lengths[None, :])
    return inside.astype(jnp.float32)


def project(acts, factors):
    rows = factors.reshape(-1, factors.shape[2])
    return lax.dot_general(acts, rows, (((1,), (1,)), ((), ())), preferred_element_type=jnp.float32)


def gather_whole(hidden_acts, output_grads, query_left, query_right, bucket_ids, seq_lengths):
    tokens_here = hidden_acts.shape[0]
    rank_count = query_left.shape[1]
    left_all, right_all = (
        lax.all_gather(query_left, "dp", axis=0, tiled=True),
        lax.all_gather(query_right, "dp", axis=0, tiled=True),
    )
    left_proj = project(hidden_acts, left_all)
    right_proj = project(output_grads, right_all)
    queries = left_proj.shape[1] // rank_count
    left_terms = left_proj.reshape(tokens_here, queries, rank_count)
    right_terms = right_proj.reshape(tokens_here, queries, rank_count)
    left_terms, right_terms = lax.psum((left_terms, right_terms), "tensor")
    share_size = queries // lax.axis_size("tensor")
    first_query = lax.axis_index("tensor") * share_size
    left_terms = lax.dynamic_slice_in_dim(left_terms, first_query, share_size, 1)
    right_terms = lax.dynamic_slice_in_dim(right_terms, first_query, share_size, 1)
    token_term = jnp.sum(left_terms * right_terms, axis=2)
    slot_mask = slot_matrix(bucket_ids, seq_lengths, tokens_here)
    return jnp.dot(
        token_term.T, slot_mask, precision=lax.Precision.HIGHEST, preferred_element_type=jnp.float32
    )


CORE, COLUMN, NEAR, ACROSS, OPPOSITE = 1, 2, 4, 12, 8
LITTLE = pl.CostEstimate(flops=1, bytes_accessed=1, transcendentals=0)
VMEM_LIMIT = 255 * 256 * 1024


def flip(array, code, count):
    return lax.ppermute(array, "dp", [(i, i ^ code) for i in range(count)])


def swap_groups(array):
    return lax.ppermute(array, "groups", [(0, 1), (1, 0)])


PARTS = 4


def through(held, arrived, gone, source, target):
    rows = source.shape[0] // PARTS
    parts = [pl.ds(i * rows, rows) for i in range(PARTS)]
    come = [pltpu.make_async_copy(source.at[p], held.at[p], arrived.at[i]) for i, p in enumerate(parts)]
    go = [pltpu.make_async_copy(held.at[p], target.at[p], gone.at[i]) for i, p in enumerate(parts)]
    for copy in come:
        copy.start()
    for first, second in zip(come, go):
        first.wait()
        second.start()
    for copy in go:
        copy.wait()


def after_kernel(count, merges, inside_ref, turn_ref, *refs):
    if merges:
        refs, staging = refs[:-3], refs[-3:]
        source, target = refs[0], refs[-1 - count]

        @pl.when(inside_ref[0] == 1)
        def _():
            through(*staging, source, target)

    refs[-1][0] = turn_ref[0]


def after(turn, arrays, inside, merge=None, there=()):
    count = len(arrays)
    scratch = []
    if merge is not None:
        there = (merge, *there)
        scratch = [pltpu.VMEM(merge.shape, merge.dtype)] + [pltpu.SemaphoreType.DMA((PARTS,))] * 2
    hbm = pl.BlockSpec(memory_space=pltpu.HBM)
    scalar = pl.BlockSpec(memory_space=pltpu.SMEM)
    *arrays, turn = pl.pallas_call(
        functools.partial(after_kernel, count, merge is not None),
        out_shape=[jax.ShapeDtypeStruct(x.shape, x.dtype) for x in (*arrays, turn)],
        in_specs=[scalar] * 2 + [hbm] * (len(there) + count),
        out_specs=[hbm] * count + [scalar],
        input_output_aliases={2 + len(there) + i: i for i in range(count)},
        scratch_shapes=scratch,
        compiler_params=pltpu.CompilerParams(vmem_limit_bytes=VMEM_LIMIT),
        cost_estimate=LITTLE,
    )(inside, turn, *there, *arrays)
    return turn, arrays


def prepare_kernel(works_ref, turn_ref, first_ref, left_ref, right_ref, *refs):
    half_ref, one_ref, two_ref, next_ref, half_held, right_held, arrived, gone = refs[-8:]
    next_ref[0] = turn_ref[0]
    width = half_ref.shape[1]

    @pl.when(works_ref[0] == 1)
    def _():
        start = pl.multiple_of(first_ref[0] * width, width)
        through(half_held, arrived, gone, left_ref.at[:, pl.ds(start, width)], half_ref)
        for target in (one_ref, two_ref):
            through(right_held, arrived, gone, right_ref, target)


def prepare(turn, works, first, left, right, made, passed):
    rows, width = left.shape[0], left.shape[1] // 2
    shapes = [(rows, width), right.shape, right.shape]
    out_shape = [jax.ShapeDtypeStruct(x, left.dtype) for x in shapes]
    made = () if made is None else made
    given = (*passed, *made)
    hbm = pl.BlockSpec(memory_space=pltpu.HBM)
    scalar = pl.BlockSpec(memory_space=pltpu.SMEM)
    aliases = {5 + i: i for i in range(len(given))}
    outs = pl.pallas_call(
        prepare_kernel,
        out_shape=[jax.ShapeDtypeStruct(x.shape, x.dtype) for x in passed]
        + out_shape
        + [jax.ShapeDtypeStruct(turn.shape, turn.dtype)],
        in_specs=[scalar] * 3 + [hbm] * (2 + len(given)),
        out_specs=[hbm] * (len(passed) + 3) + [scalar],
        input_output_aliases=aliases,
        scratch_shapes=[pltpu.VMEM((rows, width), left.dtype), pltpu.VMEM(right.shape, right.dtype)]
        + [pltpu.SemaphoreType.DMA((PARTS,))] * 2,
        compiler_params=pltpu.CompilerParams(vmem_limit_bytes=VMEM_LIMIT),
        cost_estimate=LITTLE,
    )(works, turn, first, left, right, *given)
    return outs[-1], outs[len(passed) : -1], outs[: len(passed)]


def lines(array, pairs):
    return lax.ppermute(
        array, "dp", [(a * 4 + rest, b * 4 + rest) for a, b in pairs for rest in range(4)]
    )


def score_into(out_ref, spans_ref, terms_of, rows):
    slots = out_ref.shape[0] // 2
    place = lax.broadcasted_iota(jnp.int32, (rows, 1), 0)
    for part in range(2):
        terms = terms_of(slice(part * rows, (part + 1) * rows))
        for j in range(slots):
            k = part * slots + j
            inside = (place >= spans_ref[0, k]) & (place < spans_ref[1, k])
            out_ref[k : k + 1, :] = jnp.sum(jnp.where(inside, terms, 0.0), axis=0, keepdims=True)


def proj_kernel(count, last, turn_ref, at_ref, own_ref, other_ref, *refs):
    del at_ref
    pieces, refs = refs[:count], refs[count:]
    if last is None:
        acc_ref, next_ref = refs
    else:
        spans_ref, left_ref, second_ref, out_ref, next_ref, acc_ref = refs
    step = pl.program_id(0)
    rows = own_ref.shape[0]

    @pl.when(step == 0)
    def _():
        next_ref[0] = turn_ref[0]
        acc_ref[...] = jnp.zeros_like(acc_ref)

    factors = jnp.concatenate([p[...] for p in pieces], axis=0)
    for part, tokens in enumerate((own_ref, other_ref)):
        acc_ref[part * rows : (part + 1) * rows] += lax.dot_general(
            tokens[...], factors, (((1,), (1,)), ((), ())), preferred_element_type=jnp.float32
        )

    if last is not None:

        @pl.when(step == pl.num_programs(0) - 1)
        def _():
            def terms(here):
                if last:
                    return (left_ref[here] + second_ref[here]) * acc_ref[here]
                return (left_ref[here] + acc_ref[here]) * second_ref[here]

            score_into(out_ref, spans_ref, terms, rows)


def proj(turn, tokens, rows, pieces, first, steps, last=None, spans=None, others=()):
    depth = pieces[0].shape[1]
    block = depth // steps
    held = sum(p.shape[0] for p in pieces)
    (own, own_row), (other, other_row) = tokens
    whole = pl.BlockSpec((2 * rows, held), lambda k, turn, at: (0, 0))
    scalar = pl.BlockSpec(memory_space=pltpu.SMEM)
    if last is None:
        more_specs, more, scratch = [], (), []
        out_shape, out_spec = (2 * rows, held), whole
    else:
        more_specs, more = [scalar, whole, whole], (spans, *others)
        scratch = [pltpu.VMEM((2 * rows, held), jnp.float32)]
        out_shape = (spans.shape[1], held)
        out_spec = pl.BlockSpec(out_shape, lambda k, turn, at: (0, 0))
    out, turn_next = pl.pallas_call(
        functools.partial(proj_kernel, len(pieces), last),
        out_shape=(
            jax.ShapeDtypeStruct(out_shape, jnp.float32),
            jax.ShapeDtypeStruct((1,), jnp.int32),
        ),
        grid_spec=pltpu.PrefetchScalarGridSpec(
            num_scalar_prefetch=2,
            grid=(steps,),
            in_specs=[
                pl.BlockSpec((rows, block), lambda k, turn, at: (at[1], at[0] * steps + k)),
                pl.BlockSpec((rows, block), lambda k, turn, at: (at[2], at[0] * steps + k)),
            ]
            + [pl.BlockSpec((p.shape[0], block), lambda k, turn, at: (0, k)) for p in pieces]
            + more_specs,
            out_specs=(out_spec, scalar),
            scratch_shapes=scratch,
        ),
        compiler_params=pltpu.CompilerParams(vmem_limit_bytes=VMEM_LIMIT),
        cost_estimate=LITTLE,
    )(turn, jnp.concatenate([first, own_row, other_row]), own, other, *pieces, *more)
    return turn_next, out


def spans_of(slot_ids, lengths):
    widths = bucket_lengths(slot_ids)
    starts = jnp.cumsum(widths) - widths
    return jnp.stack([starts, starts + lengths]).astype(jnp.int32)


def relay(hidden_acts, output_grads, query_left, query_right, bucket_ids, seq_lengths):
    count = lax.axis_size("dp")
    me, group = lax.axis_index("dp"), lax.axis_index("groups")
    z = me // 4
    local, ranks = query_left.shape[:2]
    left = query_left.reshape(local * ranks, -1)
    half = left.shape[1] // 2
    send = functools.partial(flip, count=count)

    acts_there = send(hidden_acts, CORE)
    spans_here = spans_of(bucket_ids, seq_lengths)
    spans = jnp.concatenate([spans_here, send(spans_here, CORE)], axis=1)

    a, b, c = {}, {}, {}
    a["own"] = lax.dynamic_slice_in_dim(left, group * half, half, 1)
    b["own"] = query_right.reshape(local * ranks, -1)
    at_end = (z == 0) | (z == 3)

    def near(piece):
        return send(piece, NEAR)

    def middle(piece):
        return lines(piece, [(1, 2), (2, 1)])

    def outward(piece):
        return lines(piece, [(1, 0), (2, 3)])

    def across(piece):
        return send(piece, ACROSS)

    def over_x(piece):
        return send(piece, COLUMN)

    inside = (~at_end).reshape(1).astype(jnp.int32)
    mine = jnp.reshape(group, (1,)).astype(jnp.int32)
    zero = jnp.zeros((1,), jnp.int32)
    acts = ((hidden_acts, zero), (acts_there, zero))
    groups = (("own", "x", "n", "f"), ("xo", "o", "xn", "xf"))
    tokens_here = hidden_acts.shape[0]
    steps = 4

    def times_a(turn, k):
        return proj(turn, acts, tokens_here, [a[i] for i in groups[k]], mine, steps)

    def times_c(turn, k, *score):
        return proj(turn, acts, tokens_here, [c[i] for i in groups[k]], 1 - mine, steps, *score)

    def times_b(turn, k, *score):
        return proj(turn, grads, tokens_here, [b[i] for i in groups[k]], zero, steps, *score)

    def pause(turn):
        return after(turn, [], inside)[0]

    grads_there = send(output_grads, CORE)
    grads = ((output_grads, zero), (grads_there, zero))

    core = (me & CORE).reshape(1).astype(jnp.int32)
    copies = (1 - mine, left, b["own"])
    turn, made, (a["own"],) = prepare(zero, core, *copies, None, [a["own"]])
    a["x"] = over_x(a["own"])
    a["n"] = near(a["own"])
    a_mid = middle(a["own"])
    turn, (c["own"], b_one, b_two), _ = prepare(turn, 1 - core, *copies, made, [])

    turn, (a["x"], a["n"], a_mid) = after(turn, [a["x"], a["n"], a_mid], inside, None, [acts_there])
    a_out = outward(a_mid)
    a_in = middle(a["n"])
    b["x"] = over_x(b_one)
    c["x"] = swap_groups(a["x"])
    turn = pause(turn)

    turn, (a_out, b["x"], a_in, c["x"]) = after(turn, [a_out, b["x"], a_in, c["x"]], inside, None, [grads_there])
    a_last = outward(a_in)
    a["xn"] = over_x(a["n"])
    c["n"] = swap_groups(a["n"])
    b["f"] = across(b_one)
    turn, (a["o"],) = after(turn, [a_out], inside, a_in)
    a["xo"] = over_x(a["o"])
    turn = pause(turn)

    turn, (a_last, a["xn"], c["n"], b_two) = after(turn, [a_last, a["xn"], c["n"], b_two], inside)
    turn, (a["f"],) = after(turn, [a_last], inside, a_mid)
    b["n"] = near(b_two)
    a["xf"] = over_x(a["f"])
    c["f"] = swap_groups(a["f"])
    turn, a_first = times_a(turn, 0)

    turn, (b["n"], a["xo"], c["f"], a["o"], a["xn"]) = after(
        turn, [b["n"], a["xo"], c["f"], a["o"], a["xn"]], inside
    )
    c["o"] = swap_groups(a["o"])
    c["xn"] = swap_groups(a["xn"])
    turn, c_first = times_c(turn, 0)

    turn, (b["f"], a["xf"], c["o"], a["xo"]) = after(turn, [b["f"], a["xf"], c["o"], a["xo"]], inside)
    b["o"] = near(b["f"])
    b["xf"] = over_x(b["f"])
    c["xo"] = swap_groups(a["xo"])
    turn, score_first = times_b(turn, 0, True, spans, (a_first, c_first))

    split = c["f"].shape[0] // 2
    turn, (b["o"], b["xf"], c["xn"], b_over, a["xf"], c["f"]) = after(
        turn, [b["o"], b["xf"], c["xn"], b["x"], a["xf"], c["f"]], inside
    )
    b["xo"] = over_x(b["o"])
    b["xn"] = near(b_over)
    c["top"] = over_x(c["f"][:split])
    c["low"] = swap_groups(a["xf"][split:])
    turn, a_second = times_a(turn, 1)

    turn, (b["xo"], c["xo"], b["xn"]) = after(turn, [b["xo"], c["xo"], b["xn"]], inside)
    turn, b_second = times_b(turn, 1)
    groups = (groups[0], ("xo", "o", "xn", "top", "low"))
    turn, score_second = times_c(turn, 1, False, spans, (a_second, b_second))
    sums = [score_first, score_second]

    slots = bucket_ids.shape[0]
    ours = jnp.concatenate([x[:slots] for x in sums], axis=1)
    others = send(jnp.concatenate([x[slots:] for x in sums], axis=1), CORE)
    codes = (0, COLUMN, NEAR, ACROSS, OPPOSITE | COLUMN, OPPOSITE, NEAR | COLUMN, ACROSS | COLUMN)
    codes = jnp.array(codes, jnp.int32)
    owner = jnp.concatenate([me ^ codes, me ^ CORE ^ codes])
    query = owner[:, None] * local + jnp.arange(local, dtype=jnp.int32)[None, :]
    query = jnp.repeat(query.reshape(-1), ranks)
    placed = query[None, :] == jnp.arange(count * local, dtype=jnp.int32)[:, None]
    return lax.dot_general(
        placed.astype(jnp.float32),
        jnp.concatenate([ours, others], axis=1),
        (((1,), (1,)), ((), ())),
        precision=lax.Precision.HIGHEST,
        preferred_element_type=jnp.float32,
    )


def solution(mesh):
    sizes = mesh.shape
    fits = sizes["dp"] == 16 and sizes["groups"] == 2 and sizes["tensor"] == 1
    return jax.shard_map(
        relay if fits else gather_whole,
        mesh=mesh,
        in_specs=(
            P(("groups", "dp"), "tensor"),
            P(("groups", "dp"), "tensor"),
            P("dp", None, "tensor"),
            P("dp", None, "tensor"),
            P(("groups", "dp")),
            P(("groups", "dp")),
        ),
        out_specs=P("tensor", ("groups", "dp")),
        check_vma=False,
    )
```

```python
import functools

import jax
import jax.numpy as jnp
from jax import lax
from jax.experimental import pallas as pl
from jax.experimental.pallas import tpu as pltpu
from jax.sharding import PartitionSpec as P

BUCKET = 128


def bucket_lengths(slot_ids):
    return BUCKET * jnp.where(
        slot_ids == 0, 1, jnp.where(slot_ids == 1, 2, jnp.where(slot_ids == 2, 4, 0))
    ).astype(jnp.int32)


def slot_matrix(slot_ids, lengths, positions):
    widths = bucket_lengths(slot_ids)
    starts = jnp.cumsum(widths) - widths
    place = jnp.arange(positions, dtype=jnp.int32)[:, None]
    inside = (place >= starts[None, :]) & (place < starts[None, :] + lengths[None, :])
    return inside.astype(jnp.float32)


def project(acts, factors):
    rows = factors.reshape(-1, factors.shape[2])
    return lax.dot_general(acts, rows, (((1,), (1,)), ((), ())), preferred_element_type=jnp.float32)


def gather_whole(hidden_acts, output_grads, query_left, query_right, bucket_ids, seq_lengths):
    tokens_here = hidden_acts.shape[0]
    rank_count = query_left.shape[1]
    left_all, right_all = (
        lax.all_gather(query_left, "dp", axis=0, tiled=True),
        lax.all_gather(query_right, "dp", axis=0, tiled=True),
    )
    left_proj = project(hidden_acts, left_all)
    right_proj = project(output_grads, right_all)
    queries = left_proj.shape[1] // rank_count
    left_terms = left_proj.reshape(tokens_here, queries, rank_count)
    right_terms = right_proj.reshape(tokens_here, queries, rank_count)
    left_terms, right_terms = lax.psum((left_terms, right_terms), "tensor")
    share_size = queries // lax.axis_size("tensor")
    first_query = lax.axis_index("tensor") * share_size
    left_terms = lax.dynamic_slice_in_dim(left_terms, first_query, share_size, 1)
    right_terms = lax.dynamic_slice_in_dim(right_terms, first_query, share_size, 1)
    token_term = jnp.sum(left_terms * right_terms, axis=2)
    slot_mask = slot_matrix(bucket_ids, seq_lengths, tokens_here)
    return jnp.dot(
        token_term.T, slot_mask, precision=lax.Precision.HIGHEST, preferred_element_type=jnp.float32
    )


CORE, COLUMN, NEAR, ACROSS, OPPOSITE = 1, 2, 4, 12, 8
LITTLE = pl.CostEstimate(flops=1, bytes_accessed=1, transcendentals=0)
VMEM_LIMIT = 255 * 256 * 1024


def flip(array, code, count):
    return lax.ppermute(array, "dp", [(i, i ^ code) for i in range(count)])


def swap_groups(array):
    return lax.ppermute(array, "groups", [(0, 1), (1, 0)])


PARTS = 4


def through(held, arrived, gone, source, target):
    rows = source.shape[0] // PARTS
    parts = [pl.ds(i * rows, rows) for i in range(PARTS)]
    come = [pltpu.make_async_copy(source.at[p], held.at[p], arrived.at[i]) for i, p in enumerate(parts)]
    go = [pltpu.make_async_copy(held.at[p], target.at[p], gone.at[i]) for i, p in enumerate(parts)]
    for copy in come:
        copy.start()
    for first, second in zip(come, go):
        first.wait()
        second.start()
    for copy in go:
        copy.wait()


def after_kernel(count, merges, inside_ref, turn_ref, *refs):
    if merges:
        refs, staging = refs[:-3], refs[-3:]
        source, target = refs[0], refs[-1 - count]

        @pl.when(inside_ref[0] == 1)
        def _():
            through(*staging, source, target)

    refs[-1][0] = turn_ref[0]


def after(turn, arrays, inside, merge=None, there=()):
    count = len(arrays)
    scratch = []
    if merge is not None:
        there = (merge, *there)
        scratch = [pltpu.VMEM(merge.shape, merge.dtype)] + [pltpu.SemaphoreType.DMA((PARTS,))] * 2
    hbm = pl.BlockSpec(memory_space=pltpu.HBM)
    scalar = pl.BlockSpec(memory_space=pltpu.SMEM)
    *arrays, turn = pl.pallas_call(
        functools.partial(after_kernel, count, merge is not None),
        out_shape=[jax.ShapeDtypeStruct(x.shape, x.dtype) for x in (*arrays, turn)],
        in_specs=[scalar] * 2 + [hbm] * (len(there) + count),
        out_specs=[hbm] * count + [scalar],
        input_output_aliases={2 + len(there) + i: i for i in range(count)},
        scratch_shapes=scratch,
        compiler_params=pltpu.CompilerParams(vmem_limit_bytes=VMEM_LIMIT),
        cost_estimate=LITTLE,
    )(inside, turn, *there, *arrays)
    return turn, arrays


def prepare_kernel(works_ref, turn_ref, first_ref, left_ref, right_ref, *refs):
    half_ref, one_ref, two_ref, next_ref, half_held, right_held, arrived, gone = refs[-8:]
    next_ref[0] = turn_ref[0]
    width = half_ref.shape[1]

    @pl.when(works_ref[0] == 1)
    def _():
        start = pl.multiple_of(first_ref[0] * width, width)
        through(half_held, arrived, gone, left_ref.at[:, pl.ds(start, width)], half_ref)
        for target in (one_ref, two_ref):
            through(right_held, arrived, gone, right_ref, target)


def prepare(turn, works, first, left, right, made, passed):
    rows, width = left.shape[0], left.shape[1] // 2
    shapes = [(rows, width), right.shape, right.shape]
    out_shape = [jax.ShapeDtypeStruct(x, left.dtype) for x in shapes]
    made = () if made is None else made
    given = (*passed, *made)
    hbm = pl.BlockSpec(memory_space=pltpu.HBM)
    scalar = pl.BlockSpec(memory_space=pltpu.SMEM)
    aliases = {5 + i: i for i in range(len(given))}
    outs = pl.pallas_call(
        prepare_kernel,
        out_shape=[jax.ShapeDtypeStruct(x.shape, x.dtype) for x in passed]
        + out_shape
        + [jax.ShapeDtypeStruct(turn.shape, turn.dtype)],
        in_specs=[scalar] * 3 + [hbm] * (2 + len(given)),
        out_specs=[hbm] * (len(passed) + 3) + [scalar],
        input_output_aliases=aliases,
        scratch_shapes=[pltpu.VMEM((rows, width), left.dtype), pltpu.VMEM(right.shape, right.dtype)]
        + [pltpu.SemaphoreType.DMA((PARTS,))] * 2,
        compiler_params=pltpu.CompilerParams(vmem_limit_bytes=VMEM_LIMIT),
        cost_estimate=LITTLE,
    )(works, turn, first, left, right, *given)
    return outs[-1], outs[len(passed) : -1], outs[: len(passed)]


def lines(array, pairs):
    return lax.ppermute(
        array, "dp", [(a * 4 + rest, b * 4 + rest) for a, b in pairs for rest in range(4)]
    )


def score_into(out_ref, spans_ref, terms_of, rows):
    slots = out_ref.shape[0] // 2
    place = lax.broadcasted_iota(jnp.int32, (rows, 1), 0)
    for part in range(2):
        terms = terms_of(slice(part * rows, (part + 1) * rows))
        for j in range(slots):
            k = part * slots + j
            inside = (place >= spans_ref[0, k]) & (place < spans_ref[1, k])
            out_ref[k : k + 1, :] = jnp.sum(jnp.where(inside, terms, 0.0), axis=0, keepdims=True)


def proj_kernel(count, last, turn_ref, at_ref, own_ref, other_ref, *refs):
    del at_ref
    pieces, refs = refs[:count], refs[count:]
    if last is None:
        acc_ref, next_ref = refs
    else:
        spans_ref, left_ref, second_ref, out_ref, next_ref, acc_ref = refs
    step = pl.program_id(0)
    rows = own_ref.shape[0]

    @pl.when(step == 0)
    def _():
        next_ref[0] = turn_ref[0]
        acc_ref[...] = jnp.zeros_like(acc_ref)

    factors = jnp.concatenate([p[...] for p in pieces], axis=0)
    for part, tokens in enumerate((own_ref, other_ref)):
        acc_ref[part * rows : (part + 1) * rows] += lax.dot_general(
            tokens[...], factors, (((1,), (1,)), ((), ())), preferred_element_type=jnp.float32
        )

    if last is not None:

        @pl.when(step == pl.num_programs(0) - 1)
        def _():
            def terms(here):
                if last:
                    return (left_ref[here] + second_ref[here]) * acc_ref[here]
                return (left_ref[here] + acc_ref[here]) * second_ref[here]

            score_into(out_ref, spans_ref, terms, rows)


def proj(turn, tokens, rows, pieces, first, steps, last=None, spans=None, others=()):
    depth = pieces[0].shape[1]
    block = depth // steps
    held = sum(p.shape[0] for p in pieces)
    (own, own_row), (other, other_row) = tokens
    whole = pl.BlockSpec((2 * rows, held), lambda k, turn, at: (0, 0))
    scalar = pl.BlockSpec(memory_space=pltpu.SMEM)
    if last is None:
        more_specs, more, scratch = [], (), []
        out_shape, out_spec = (2 * rows, held), whole
    else:
        more_specs, more = [scalar, whole, whole], (spans, *others)
        scratch = [pltpu.VMEM((2 * rows, held), jnp.float32)]
        out_shape = (spans.shape[1], held)
        out_spec = pl.BlockSpec(out_shape, lambda k, turn, at: (0, 0))
    out, turn_next = pl.pallas_call(
        functools.partial(proj_kernel, len(pieces), last),
        out_shape=(
            jax.ShapeDtypeStruct(out_shape, jnp.float32),
            jax.ShapeDtypeStruct((1,), jnp.int32),
        ),
        grid_spec=pltpu.PrefetchScalarGridSpec(
            num_scalar_prefetch=2,
            grid=(steps,),
            in_specs=[
                pl.BlockSpec((rows, block), lambda k, turn, at: (at[1], at[0] * steps + k)),
                pl.BlockSpec((rows, block), lambda k, turn, at: (at[2], at[0] * steps + k)),
            ]
            + [pl.BlockSpec((p.shape[0], block), lambda k, turn, at: (0, k)) for p in pieces]
            + more_specs,
            out_specs=(out_spec, scalar),
            scratch_shapes=scratch,
        ),
        compiler_params=pltpu.CompilerParams(vmem_limit_bytes=VMEM_LIMIT),
        cost_estimate=LITTLE,
    )(turn, jnp.concatenate([first, own_row, other_row]), own, other, *pieces, *more)
    return turn_next, out


def spans_of(slot_ids, lengths):
    widths = bucket_lengths(slot_ids)
    starts = jnp.cumsum(widths) - widths
    return jnp.stack([starts, starts + lengths]).astype(jnp.int32)


def relay(hidden_acts, output_grads, query_left, query_right, bucket_ids, seq_lengths):
    count = lax.axis_size("dp")
    me, group = lax.axis_index("dp"), lax.axis_index("groups")
    z = me // 4
    local, ranks = query_left.shape[:2]
    left = query_left.reshape(local * ranks, -1)
    half = left.shape[1] // 2
    send = functools.partial(flip, count=count)

    acts_there = send(hidden_acts, CORE)
    spans_here = spans_of(bucket_ids, seq_lengths)
    spans = jnp.concatenate([spans_here, send(spans_here, CORE)], axis=1)

    a, b, c = {}, {}, {}
    a["own"] = lax.dynamic_slice_in_dim(left, group * half, half, 1)
    b["own"] = query_right.reshape(local * ranks, -1)
    at_end = (z == 0) | (z == 3)

    def near(piece):
        return send(piece, NEAR)

    def middle(piece):
        return lines(piece, [(1, 2), (2, 1)])

    def outward(piece):
        return lines(piece, [(1, 0), (2, 3)])

    def across(piece):
        return send(piece, ACROSS)

    def over_x(piece):
        return send(piece, COLUMN)

    inside = (~at_end).reshape(1).astype(jnp.int32)
    mine = jnp.reshape(group, (1,)).astype(jnp.int32)
    zero = jnp.zeros((1,), jnp.int32)
    acts = ((hidden_acts, zero), (acts_there, zero))
    groups = (("own", "x", "n", "f"), ("xo", "o", "xn", "xf"))
    tokens_here = hidden_acts.shape[0]
    steps = 4

    def times_a(turn, k):
        return proj(turn, acts, tokens_here, [a[i] for i in groups[k]], mine, steps)

    def times_c(turn, k, *score):
        return proj(turn, acts, tokens_here, [c[i] for i in groups[k]], 1 - mine, steps, *score)

    def times_b(turn, k, *score):
        return proj(turn, grads, tokens_here, [b[i] for i in groups[k]], zero, steps, *score)

    def pause(turn):
        return after(turn, [], inside)[0]

    grads_there = send(output_grads, CORE)
    grads = ((output_grads, zero), (grads_there, zero))

    copies = (1 - mine, left, b["own"])
    a["x"] = over_x(a["own"])
    a["n"] = near(a["own"])
    a_mid = middle(a["own"])
    turn, (c["own"], b_one, b_two), _ = prepare(zero, zero + 1, *copies, None, [])

    turn, (a["x"], a["n"], a_mid) = after(turn, [a["x"], a["n"], a_mid], inside, None, [acts_there])
    a_out = outward(a_mid)
    a_in = middle(a["n"])
    b["x"] = over_x(b_one)
    c["x"] = swap_groups(a["x"])
    turn = pause(turn)

    turn, (a_out, b["x"], a_in, c["x"]) = after(turn, [a_out, b["x"], a_in, c["x"]], inside, None, [grads_there])
    a_last = outward(a_in)
    a["xn"] = over_x(a["n"])
    c["n"] = swap_groups(a["n"])
    b["f"] = across(b_one)
    turn, (a["o"],) = after(turn, [a_out], inside, a_in)
    a["xo"] = over_x(a["o"])
    turn = pause(turn)

    turn, (a_last, a["xn"], c["n"], b_two) = after(turn, [a_last, a["xn"], c["n"], b_two], inside)
    turn, (a["f"],) = after(turn, [a_last], inside, a_mid)
    b["n"] = near(b_two)
    a["xf"] = over_x(a["f"])
    c["f"] = swap_groups(a["f"])
    turn, a_first = times_a(turn, 0)

    turn, (b["n"], a["xo"], c["f"], a["o"], a["xn"]) = after(
        turn, [b["n"], a["xo"], c["f"], a["o"], a["xn"]], inside
    )
    c["o"] = swap_groups(a["o"])
    c["xn"] = swap_groups(a["xn"])
    turn, c_first = times_c(turn, 0)

    turn, (b["f"], a["xf"], c["o"], a["xo"]) = after(turn, [b["f"], a["xf"], c["o"], a["xo"]], inside)
    b["o"] = near(b["f"])
    b["xf"] = over_x(b["f"])
    c["xo"] = swap_groups(a["xo"])
    turn, score_first = times_b(turn, 0, True, spans, (a_first, c_first))

    split = c["f"].shape[0] // 2
    turn, (b["o"], b["xf"], c["xn"], b_over, a["xf"], c["f"]) = after(
        turn, [b["o"], b["xf"], c["xn"], b["x"], a["xf"], c["f"]], inside
    )
    b["xo"] = over_x(b["o"])
    b["xn"] = near(b_over)
    c["top"] = over_x(c["f"][:split])
    c["low"] = swap_groups(a["xf"][split:])
    turn, a_second = times_a(turn, 1)

    turn, (b["xo"], c["xo"], b["xn"]) = after(turn, [b["xo"], c["xo"], b["xn"]], inside)
    turn, b_second = times_b(turn, 1)
    groups = (groups[0], ("xo", "o", "xn", "top", "low"))
    turn, score_second = times_c(turn, 1, False, spans, (a_second, b_second))
    sums = [score_first, score_second]

    slots = bucket_ids.shape[0]
    ours = jnp.concatenate([x[:slots] for x in sums], axis=1)
    others = send(jnp.concatenate([x[slots:] for x in sums], axis=1), CORE)
    codes = (0, COLUMN, NEAR, ACROSS, OPPOSITE | COLUMN, OPPOSITE, NEAR | COLUMN, ACROSS | COLUMN)
    codes = jnp.array(codes, jnp.int32)
    owner = jnp.concatenate([me ^ codes, me ^ CORE ^ codes])
    query = owner[:, None] * local + jnp.arange(local, dtype=jnp.int32)[None, :]
    query = jnp.repeat(query.reshape(-1), ranks)
    placed = query[None, :] == jnp.arange(count * local, dtype=jnp.int32)[:, None]
    return lax.dot_general(
        placed.astype(jnp.float32),
        jnp.concatenate([ours, others], axis=1),
        (((1,), (1,)), ((), ())),
        precision=lax.Precision.HIGHEST,
        preferred_element_type=jnp.float32,
    )


def solution(mesh):
    sizes = mesh.shape
    fits = sizes["dp"] == 16 and sizes["groups"] == 2 and sizes["tensor"] == 1
    return jax.shard_map(
        relay if fits else gather_whole,
        mesh=mesh,
        in_specs=(
            P(("groups", "dp"), "tensor"),
            P(("groups", "dp"), "tensor"),
            P("dp", None, "tensor"),
            P("dp", None, "tensor"),
            P(("groups", "dp")),
            P(("groups", "dp")),
        ),
        out_specs=P("tensor", ("groups", "dp")),
        check_vma=False,
    )
```

```python
import functools

import jax
import jax.numpy as jnp
from jax import lax
from jax.experimental import pallas as pl
from jax.experimental.pallas import tpu as pltpu
from jax.sharding import PartitionSpec as P

BUCKET = 128


def bucket_lengths(slot_ids):
    return BUCKET * jnp.where(
        slot_ids == 0, 1, jnp.where(slot_ids == 1, 2, jnp.where(slot_ids == 2, 4, 0))
    ).astype(jnp.int32)


def slot_matrix(slot_ids, lengths, positions):
    widths = bucket_lengths(slot_ids)
    starts = jnp.cumsum(widths) - widths
    place = jnp.arange(positions, dtype=jnp.int32)[:, None]
    inside = (place >= starts[None, :]) & (place < starts[None, :] + lengths[None, :])
    return inside.astype(jnp.float32)


def project(acts, factors):
    rows = factors.reshape(-1, factors.shape[2])
    return lax.dot_general(acts, rows, (((1,), (1,)), ((), ())), preferred_element_type=jnp.float32)


def gather_whole(hidden_acts, output_grads, query_left, query_right, bucket_ids, seq_lengths):
    tokens_here = hidden_acts.shape[0]
    rank_count = query_left.shape[1]
    left_all, right_all = (
        lax.all_gather(query_left, "dp", axis=0, tiled=True),
        lax.all_gather(query_right, "dp", axis=0, tiled=True),
    )
    left_proj = project(hidden_acts, left_all)
    right_proj = project(output_grads, right_all)
    queries = left_proj.shape[1] // rank_count
    left_terms = left_proj.reshape(tokens_here, queries, rank_count)
    right_terms = right_proj.reshape(tokens_here, queries, rank_count)
    left_terms, right_terms = lax.psum((left_terms, right_terms), "tensor")
    share_size = queries // lax.axis_size("tensor")
    first_query = lax.axis_index("tensor") * share_size
    left_terms = lax.dynamic_slice_in_dim(left_terms, first_query, share_size, 1)
    right_terms = lax.dynamic_slice_in_dim(right_terms, first_query, share_size, 1)
    token_term = jnp.sum(left_terms * right_terms, axis=2)
    slot_mask = slot_matrix(bucket_ids, seq_lengths, tokens_here)
    return jnp.dot(
        token_term.T, slot_mask, precision=lax.Precision.HIGHEST, preferred_element_type=jnp.float32
    )


CORE, COLUMN, NEAR, ACROSS, OPPOSITE = 1, 2, 4, 12, 8
LITTLE = pl.CostEstimate(flops=1, bytes_accessed=1, transcendentals=0)
VMEM_LIMIT = 255 * 256 * 1024


def flip(array, code, count):
    return lax.ppermute(array, "dp", [(i, i ^ code) for i in range(count)])


def swap_groups(array):
    return lax.ppermute(array, "groups", [(0, 1), (1, 0)])


PARTS = 4


def through(held, arrived, gone, source, target):
    rows = source.shape[0] // PARTS
    parts = [pl.ds(i * rows, rows) for i in range(PARTS)]
    come = [pltpu.make_async_copy(source.at[p], held.at[p], arrived.at[i]) for i, p in enumerate(parts)]
    go = [pltpu.make_async_copy(held.at[p], target.at[p], gone.at[i]) for i, p in enumerate(parts)]
    for copy in come:
        copy.start()
    for first, second in zip(come, go):
        first.wait()
        second.start()
    for copy in go:
        copy.wait()


def after_kernel(count, merges, inside_ref, turn_ref, *refs):
    if merges:
        refs, staging = refs[:-3], refs[-3:]
        source, target = refs[0], refs[-1 - count]

        @pl.when(inside_ref[0] == 1)
        def _():
            through(*staging, source, target)

    refs[-1][0] = turn_ref[0]


def after(turn, arrays, inside, merge=None, there=()):
    count = len(arrays)
    scratch = []
    if merge is not None:
        there = (merge, *there)
        scratch = [pltpu.VMEM(merge.shape, merge.dtype)] + [pltpu.SemaphoreType.DMA((PARTS,))] * 2
    hbm = pl.BlockSpec(memory_space=pltpu.HBM)
    scalar = pl.BlockSpec(memory_space=pltpu.SMEM)
    *arrays, turn = pl.pallas_call(
        functools.partial(after_kernel, count, merge is not None),
        out_shape=[jax.ShapeDtypeStruct(x.shape, x.dtype) for x in (*arrays, turn)],
        in_specs=[scalar] * 2 + [hbm] * (len(there) + count),
        out_specs=[hbm] * count + [scalar],
        input_output_aliases={2 + len(there) + i: i for i in range(count)},
        scratch_shapes=scratch,
        compiler_params=pltpu.CompilerParams(vmem_limit_bytes=VMEM_LIMIT),
        cost_estimate=LITTLE,
    )(inside, turn, *there, *arrays)
    return turn, arrays


def prepare_kernel(works_ref, turn_ref, first_ref, left_ref, right_ref, *refs):
    half_ref, one_ref, two_ref, next_ref, half_held, right_held, arrived, gone = refs[-8:]
    next_ref[0] = turn_ref[0]
    width = half_ref.shape[1]

    @pl.when(works_ref[0] == 1)
    def _():
        start = pl.multiple_of(first_ref[0] * width, width)
        through(half_held, arrived, gone, left_ref.at[:, pl.ds(start, width)], half_ref)
        for target in (one_ref, two_ref):
            through(right_held, arrived, gone, right_ref, target)


def prepare(turn, works, first, left, right, made, passed):
    rows, width = left.shape[0], left.shape[1] // 2
    shapes = [(rows, width), right.shape, right.shape]
    out_shape = [jax.ShapeDtypeStruct(x, left.dtype) for x in shapes]
    made = () if made is None else made
    given = (*passed, *made)
    hbm = pl.BlockSpec(memory_space=pltpu.HBM)
    scalar = pl.BlockSpec(memory_space=pltpu.SMEM)
    aliases = {5 + i: i for i in range(len(given))}
    outs = pl.pallas_call(
        prepare_kernel,
        out_shape=[jax.ShapeDtypeStruct(x.shape, x.dtype) for x in passed]
        + out_shape
        + [jax.ShapeDtypeStruct(turn.shape, turn.dtype)],
        in_specs=[scalar] * 3 + [hbm] * (2 + len(given)),
        out_specs=[hbm] * (len(passed) + 3) + [scalar],
        input_output_aliases=aliases,
        scratch_shapes=[pltpu.VMEM((rows, width), left.dtype), pltpu.VMEM(right.shape, right.dtype)]
        + [pltpu.SemaphoreType.DMA((PARTS,))] * 2,
        compiler_params=pltpu.CompilerParams(vmem_limit_bytes=VMEM_LIMIT),
        cost_estimate=LITTLE,
    )(works, turn, first, left, right, *given)
    return outs[-1], outs[len(passed) : -1], outs[: len(passed)]


def lines(array, pairs):
    return lax.ppermute(
        array, "dp", [(a * 4 + rest, b * 4 + rest) for a, b in pairs for rest in range(4)]
    )


def score_into(out_ref, spans_ref, terms_of, rows):
    slots = out_ref.shape[0] // 2
    place = lax.broadcasted_iota(jnp.int32, (rows, 1), 0)
    for part in range(2):
        terms = terms_of(slice(part * rows, (part + 1) * rows))
        for j in range(slots):
            k = part * slots + j
            inside = (place >= spans_ref[0, k]) & (place < spans_ref[1, k])
            out_ref[k : k + 1, :] = jnp.sum(jnp.where(inside, terms, 0.0), axis=0, keepdims=True)


def proj_kernel(count, last, turn_ref, at_ref, own_ref, other_ref, *refs):
    del at_ref
    pieces, refs = refs[:count], refs[count:]
    if last is None:
        acc_ref, next_ref = refs
    else:
        spans_ref, left_ref, second_ref, out_ref, next_ref, acc_ref = refs
    step = pl.program_id(0)
    rows = own_ref.shape[0]

    @pl.when(step == 0)
    def _():
        next_ref[0] = turn_ref[0]
        acc_ref[...] = jnp.zeros_like(acc_ref)

    factors = jnp.concatenate([p[...] for p in pieces], axis=0)
    for part, tokens in enumerate((own_ref, other_ref)):
        acc_ref[part * rows : (part + 1) * rows] += lax.dot_general(
            tokens[...], factors, (((1,), (1,)), ((), ())), preferred_element_type=jnp.float32
        )

    if last is not None:

        @pl.when(step == pl.num_programs(0) - 1)
        def _():
            def terms(here):
                if last:
                    return (left_ref[here] + second_ref[here]) * acc_ref[here]
                return (left_ref[here] + acc_ref[here]) * second_ref[here]

            score_into(out_ref, spans_ref, terms, rows)


def proj(turn, tokens, rows, pieces, first, steps, last=None, spans=None, others=()):
    depth = pieces[0].shape[1]
    block = depth // steps
    held = sum(p.shape[0] for p in pieces)
    (own, own_row), (other, other_row) = tokens
    whole = pl.BlockSpec((2 * rows, held), lambda k, turn, at: (0, 0))
    scalar = pl.BlockSpec(memory_space=pltpu.SMEM)
    if last is None:
        more_specs, more, scratch = [], (), []
        out_shape, out_spec = (2 * rows, held), whole
    else:
        more_specs, more = [scalar, whole, whole], (spans, *others)
        scratch = [pltpu.VMEM((2 * rows, held), jnp.float32)]
        out_shape = (spans.shape[1], held)
        out_spec = pl.BlockSpec(out_shape, lambda k, turn, at: (0, 0))
    out, turn_next = pl.pallas_call(
        functools.partial(proj_kernel, len(pieces), last),
        out_shape=(
            jax.ShapeDtypeStruct(out_shape, jnp.float32),
            jax.ShapeDtypeStruct((1,), jnp.int32),
        ),
        grid_spec=pltpu.PrefetchScalarGridSpec(
            num_scalar_prefetch=2,
            grid=(steps,),
            in_specs=[
                pl.BlockSpec((rows, block), lambda k, turn, at: (at[1], at[0] * steps + k)),
                pl.BlockSpec((rows, block), lambda k, turn, at: (at[2], at[0] * steps + k)),
            ]
            + [pl.BlockSpec((p.shape[0], block), lambda k, turn, at: (0, k)) for p in pieces]
            + more_specs,
            out_specs=(out_spec, scalar),
            scratch_shapes=scratch,
        ),
        compiler_params=pltpu.CompilerParams(vmem_limit_bytes=VMEM_LIMIT),
        cost_estimate=LITTLE,
    )(turn, jnp.concatenate([first, own_row, other_row]), own, other, *pieces, *more)
    return turn_next, out


def spans_of(slot_ids, lengths):
    widths = bucket_lengths(slot_ids)
    starts = jnp.cumsum(widths) - widths
    return jnp.stack([starts, starts + lengths]).astype(jnp.int32)


def relay(hidden_acts, output_grads, query_left, query_right, bucket_ids, seq_lengths):
    count = lax.axis_size("dp")
    me, group = lax.axis_index("dp"), lax.axis_index("groups")
    z = me // 4
    local, ranks = query_left.shape[:2]
    left = query_left.reshape(local * ranks, -1)
    half = left.shape[1] // 2
    send = functools.partial(flip, count=count)

    acts_there = send(hidden_acts, CORE)
    spans_here = spans_of(bucket_ids, seq_lengths)
    spans = jnp.concatenate([spans_here, send(spans_here, CORE)], axis=1)

    a, b, c = {}, {}, {}
    a["own"] = lax.dynamic_slice_in_dim(left, group * half, half, 1)
    b["own"] = query_right.reshape(local * ranks, -1)
    at_end = (z == 0) | (z == 3)

    def near(piece):
        return send(piece, NEAR)

    def middle(piece):
        return lines(piece, [(1, 2), (2, 1)])

    def ends(piece):
        return lines(piece, [(0, 3), (3, 0)])

    def across(piece):
        return send(piece, ACROSS)

    def over_x(piece):
        return send(piece, COLUMN)

    inside = (~at_end).reshape(1).astype(jnp.int32)
    mine = jnp.reshape(group, (1,)).astype(jnp.int32)
    zero = jnp.zeros((1,), jnp.int32)
    acts = ((hidden_acts, zero), (acts_there, zero))
    groups = (("own", "x", "n", "f"), ("xn", "xf", "o", "xo"))
    tokens_here = hidden_acts.shape[0]
    steps = 4

    def times_a(turn, k):
        return proj(turn, acts, tokens_here, [a[i] for i in groups[k]], mine, steps)

    def times_c(turn, k, *score):
        return proj(turn, acts, tokens_here, [c[i] for i in groups[k]], 1 - mine, steps, *score)

    def times_b(turn, k, *score):
        return proj(turn, grads, tokens_here, [b[i] for i in groups[k]], zero, steps, *score)

    def pause(turn):
        return after(turn, [], inside)[0]

    codes = (0, COLUMN, NEAR, ACROSS, NEAR | COLUMN, ACROSS | COLUMN, OPPOSITE, OPPOSITE | COLUMN)
    codes = jnp.array(codes, jnp.int32)
    owner = jnp.concatenate([me ^ codes, me ^ CORE ^ codes])
    query = owner[:, None] * local + jnp.arange(local, dtype=jnp.int32)[None, :]
    query = jnp.repeat(query.reshape(-1), ranks)
    placed = query[None, :] == jnp.arange(count * local, dtype=jnp.int32)[:, None]
    placed = placed.astype(jnp.float32)

    grads_there = send(output_grads, CORE)
    grads = ((output_grads, zero), (grads_there, zero))

    copies = (1 - mine, left, b["own"])
    a["x"] = over_x(a["own"])
    a["n"] = near(a["own"])
    a_mid = middle(a["own"])
    turn, (c["own"], b_one, b_two), _ = prepare(zero, zero + 1, *copies, None, [])

    turn, (a["x"], a["n"], a_mid, a["own"]) = after(
        turn, [a["x"], a["n"], a_mid, a["own"]], inside, None, [acts_there]
    )
    a_end = ends(a["own"])
    b["x"] = over_x(b_one)
    c["x"] = swap_groups(a["x"])
    turn = pause(turn)

    turn, (a["f"], b["x"], c["x"]) = after(turn, [a_end, b["x"], c["x"]], inside, a_mid, [grads_there])
    a["o"] = near(a["f"])
    a["xn"] = over_x(a["n"])
    c["n"] = swap_groups(a["n"])
    b["f"] = across(b_one)
    turn = pause(turn)

    turn, (a["o"], a["xn"], c["n"], b_two) = after(turn, [a["o"], a["xn"], c["n"], b_two], inside)
    b["n"] = near(b_two)
    a["xf"] = over_x(a["f"])
    c["f"] = swap_groups(a["f"])
    turn, a_first = times_a(turn, 0)

    turn, (b["n"], a["xf"], c["f"], a["o"], a["xn"]) = after(
        turn, [b["n"], a["xf"], c["f"], a["o"], a["xn"]], inside
    )
    a["xo"] = over_x(a["o"])
    c["o"] = swap_groups(a["o"])
    c["xn"] = swap_groups(a["xn"])
    turn, c_first = times_c(turn, 0)

    turn, (b["f"], a["xo"], c["o"], a["xf"]) = after(turn, [b["f"], a["xo"], c["o"], a["xf"]], inside)
    b["o"] = near(b["f"])
    b["xf"] = over_x(b["f"])
    c["xf"] = swap_groups(a["xf"])
    turn, score_first = times_b(turn, 0, True, spans, (a_first, c_first))

    split = c["o"].shape[0] // 2
    turn, (b["o"], b["xf"], c["xn"], b_over, a["xo"], c["o"], placed) = after(
        turn, [b["o"], b["xf"], c["xn"], b["x"], a["xo"], c["o"], placed], inside
    )
    b["xo"] = over_x(b["o"])
    b["xn"] = near(b_over)
    c["top"] = over_x(c["o"][:split])
    c["low"] = swap_groups(a["xo"][split:])
    turn, a_second = times_a(turn, 1)

    turn, (b["xo"], c["xf"], b["xn"]) = after(turn, [b["xo"], c["xf"], b["xn"]], inside)
    turn, b_second = times_b(turn, 1)
    groups = (groups[0], ("xn", "xf", "o", "top", "low"))
    turn, score_second = times_c(turn, 1, False, spans, (a_second, b_second))
    sums = [score_first, score_second]

    slots = bucket_ids.shape[0]
    others = [send(x, CORE) for x in sums]
    held = [x[:slots] for x in sums] + [x[slots:] for x in others]
    return lax.dot_general(
        placed,
        jnp.concatenate(held, axis=1),
        (((1,), (1,)), ((), ())),
        precision=lax.Precision.HIGHEST,
        preferred_element_type=jnp.float32,
    )


def solution(mesh):
    sizes = mesh.shape
    fits = sizes["dp"] == 16 and sizes["groups"] == 2 and sizes["tensor"] == 1
    return jax.shard_map(
        relay if fits else gather_whole,
        mesh=mesh,
        in_specs=(
            P(("groups", "dp"), "tensor"),
            P(("groups", "dp"), "tensor"),
            P("dp", None, "tensor"),
            P("dp", None, "tensor"),
            P(("groups", "dp")),
            P(("groups", "dp")),
        ),
        out_specs=P("tensor", ("groups", "dp")),
        check_vma=False,
    )
```

```python
import functools

import jax
import jax.numpy as jnp
from jax import lax
from jax.experimental import pallas as pl
from jax.experimental.pallas import tpu as pltpu
from jax.sharding import PartitionSpec as P

BUCKET = 128


def bucket_lengths(slot_ids):
    return BUCKET * jnp.where(
        slot_ids == 0, 1, jnp.where(slot_ids == 1, 2, jnp.where(slot_ids == 2, 4, 0))
    ).astype(jnp.int32)


def slot_matrix(slot_ids, lengths, positions):
    widths = bucket_lengths(slot_ids)
    starts = jnp.cumsum(widths) - widths
    place = jnp.arange(positions, dtype=jnp.int32)[:, None]
    inside = (place >= starts[None, :]) & (place < starts[None, :] + lengths[None, :])
    return inside.astype(jnp.float32)


def project(acts, factors):
    rows = factors.reshape(-1, factors.shape[2])
    return lax.dot_general(acts, rows, (((1,), (1,)), ((), ())), preferred_element_type=jnp.float32)


def gather_whole(hidden_acts, output_grads, query_left, query_right, bucket_ids, seq_lengths):
    tokens_here = hidden_acts.shape[0]
    rank_count = query_left.shape[1]
    left_all, right_all = (
        lax.all_gather(query_left, "dp", axis=0, tiled=True),
        lax.all_gather(query_right, "dp", axis=0, tiled=True),
    )
    left_proj = project(hidden_acts, left_all)
    right_proj = project(output_grads, right_all)
    queries = left_proj.shape[1] // rank_count
    left_terms = left_proj.reshape(tokens_here, queries, rank_count)
    right_terms = right_proj.reshape(tokens_here, queries, rank_count)
    left_terms, right_terms = lax.psum((left_terms, right_terms), "tensor")
    share_size = queries // lax.axis_size("tensor")
    first_query = lax.axis_index("tensor") * share_size
    left_terms = lax.dynamic_slice_in_dim(left_terms, first_query, share_size, 1)
    right_terms = lax.dynamic_slice_in_dim(right_terms, first_query, share_size, 1)
    token_term = jnp.sum(left_terms * right_terms, axis=2)
    slot_mask = slot_matrix(bucket_ids, seq_lengths, tokens_here)
    return jnp.dot(
        token_term.T, slot_mask, precision=lax.Precision.HIGHEST, preferred_element_type=jnp.float32
    )


CORE, COLUMN, NEAR, ACROSS, OPPOSITE = 1, 2, 4, 12, 8
LITTLE = pl.CostEstimate(flops=1, bytes_accessed=1, transcendentals=0)
VMEM_LIMIT = 255 * 256 * 1024


def flip(array, code, count):
    return lax.ppermute(array, "dp", [(i, i ^ code) for i in range(count)])


def swap_groups(array):
    return lax.ppermute(array, "groups", [(0, 1), (1, 0)])


PARTS = 4


def through(held, arrived, gone, source, target):
    rows = source.shape[0] // PARTS
    parts = [pl.ds(i * rows, rows) for i in range(PARTS)]
    come = [pltpu.make_async_copy(source.at[p], held.at[p], arrived.at[i]) for i, p in enumerate(parts)]
    go = [pltpu.make_async_copy(held.at[p], target.at[p], gone.at[i]) for i, p in enumerate(parts)]
    for copy in come:
        copy.start()
    for first, second in zip(come, go):
        first.wait()
        second.start()
    for copy in go:
        copy.wait()


def after_kernel(count, merges, inside_ref, turn_ref, *refs):
    if merges:
        refs, staging = refs[:-3], refs[-3:]
        source, target = refs[0], refs[-2]

        @pl.when(inside_ref[0] == 1)
        def _():
            through(*staging, source, target)

    refs[-1][0] = turn_ref[0]


def after(turn, arrays, inside, merge=None, there=()):
    count = len(arrays)
    scratch = []
    if merge is not None:
        there = (merge, *there)
        scratch = [pltpu.VMEM(merge.shape, merge.dtype)] + [pltpu.SemaphoreType.DMA((PARTS,))] * 2
    hbm = pl.BlockSpec(memory_space=pltpu.HBM)
    scalar = pl.BlockSpec(memory_space=pltpu.SMEM)
    *arrays, turn = pl.pallas_call(
        functools.partial(after_kernel, count, merge is not None),
        out_shape=[jax.ShapeDtypeStruct(x.shape, x.dtype) for x in (*arrays, turn)],
        in_specs=[scalar] * 2 + [hbm] * (len(there) + count),
        out_specs=[hbm] * count + [scalar],
        input_output_aliases={2 + len(there) + i: i for i in range(count)},
        scratch_shapes=scratch,
        compiler_params=pltpu.CompilerParams(vmem_limit_bytes=VMEM_LIMIT),
        cost_estimate=LITTLE,
    )(inside, turn, *there, *arrays)
    return turn, arrays


def prepare_kernel(works_ref, turn_ref, first_ref, left_ref, right_ref, *refs):
    half_ref, one_ref, two_ref, next_ref, half_held, right_held, arrived, gone = refs[-8:]
    next_ref[0] = turn_ref[0]
    width = half_ref.shape[1]

    @pl.when(works_ref[0] == 1)
    def _():
        start = pl.multiple_of(first_ref[0] * width, width)
        through(half_held, arrived, gone, left_ref.at[:, pl.ds(start, width)], half_ref)
        for target in (one_ref, two_ref):
            through(right_held, arrived, gone, right_ref, target)


def prepare(turn, works, first, left, right, made, passed):
    rows, width = left.shape[0], left.shape[1] // 2
    shapes = [(rows, width), right.shape, right.shape]
    out_shape = [jax.ShapeDtypeStruct(x, left.dtype) for x in shapes]
    made = () if made is None else made
    given = (*passed, *made)
    hbm = pl.BlockSpec(memory_space=pltpu.HBM)
    scalar = pl.BlockSpec(memory_space=pltpu.SMEM)
    aliases = {5 + i: i for i in range(len(given))}
    outs = pl.pallas_call(
        prepare_kernel,
        out_shape=[jax.ShapeDtypeStruct(x.shape, x.dtype) for x in passed]
        + out_shape
        + [jax.ShapeDtypeStruct(turn.shape, turn.dtype)],
        in_specs=[scalar] * 3 + [hbm] * (2 + len(given)),
        out_specs=[hbm] * (len(passed) + 3) + [scalar],
        input_output_aliases=aliases,
        scratch_shapes=[pltpu.VMEM((rows, width), left.dtype), pltpu.VMEM(right.shape, right.dtype)]
        + [pltpu.SemaphoreType.DMA((PARTS,))] * 2,
        compiler_params=pltpu.CompilerParams(vmem_limit_bytes=VMEM_LIMIT),
        cost_estimate=LITTLE,
    )(works, turn, first, left, right, *given)
    return outs[-1], outs[len(passed) : -1], outs[: len(passed)]


def lines(array, pairs):
    return lax.ppermute(
        array, "dp", [(a * 4 + rest, b * 4 + rest) for a, b in pairs for rest in range(4)]
    )


def score_into(out_ref, spans_ref, terms_of, rows):
    slots = out_ref.shape[0] // 2
    place = lax.broadcasted_iota(jnp.int32, (rows, 1), 0)
    for part in range(2):
        terms = terms_of(slice(part * rows, (part + 1) * rows))
        for j in range(slots):
            k = part * slots + j
            inside = (place >= spans_ref[0, k]) & (place < spans_ref[1, k])
            out_ref[k : k + 1, :] = jnp.sum(jnp.where(inside, terms, 0.0), axis=0, keepdims=True)


def proj_kernel(count, last, turn_ref, at_ref, own_ref, other_ref, *refs):
    del at_ref
    pieces, refs = refs[:count], refs[count:]
    if last is None:
        acc_ref, next_ref = refs
    else:
        spans_ref, left_ref, second_ref, out_ref, next_ref, acc_ref = refs
    step = pl.program_id(0)
    rows = own_ref.shape[0]

    @pl.when(step == 0)
    def _():
        next_ref[0] = turn_ref[0]
        acc_ref[...] = jnp.zeros_like(acc_ref)

    factors = jnp.concatenate([p[...] for p in pieces], axis=0)
    for part, tokens in enumerate((own_ref, other_ref)):
        acc_ref[part * rows : (part + 1) * rows] += lax.dot_general(
            tokens[...], factors, (((1,), (1,)), ((), ())), preferred_element_type=jnp.float32
        )

    if last is not None:

        @pl.when(step == pl.num_programs(0) - 1)
        def _():
            def terms(here):
                if last:
                    return (left_ref[here] + second_ref[here]) * acc_ref[here]
                return (left_ref[here] + acc_ref[here]) * second_ref[here]

            score_into(out_ref, spans_ref, terms, rows)


def proj(turn, tokens, rows, pieces, first, steps, last=None, spans=None, others=()):
    depth = pieces[0].shape[1]
    block = depth // steps
    held = sum(p.shape[0] for p in pieces)
    (own, own_row), (other, other_row) = tokens
    whole = pl.BlockSpec((2 * rows, held), lambda k, turn, at: (0, 0))
    scalar = pl.BlockSpec(memory_space=pltpu.SMEM)
    if last is None:
        more_specs, more, scratch = [], (), []
        out_shape, out_spec = (2 * rows, held), whole
    else:
        more_specs, more = [scalar, whole, whole], (spans, *others)
        scratch = [pltpu.VMEM((2 * rows, held), jnp.float32)]
        out_shape = (spans.shape[1], held)
        out_spec = pl.BlockSpec(out_shape, lambda k, turn, at: (0, 0))
    out, turn_next = pl.pallas_call(
        functools.partial(proj_kernel, len(pieces), last),
        out_shape=(
            jax.ShapeDtypeStruct(out_shape, jnp.float32),
            jax.ShapeDtypeStruct((1,), jnp.int32),
        ),
        grid_spec=pltpu.PrefetchScalarGridSpec(
            num_scalar_prefetch=2,
            grid=(steps,),
            in_specs=[
                pl.BlockSpec((rows, block), lambda k, turn, at: (at[1], at[0] * steps + k)),
                pl.BlockSpec((rows, block), lambda k, turn, at: (at[2], at[0] * steps + k)),
            ]
            + [pl.BlockSpec((p.shape[0], block), lambda k, turn, at: (0, k)) for p in pieces]
            + more_specs,
            out_specs=(out_spec, scalar),
            scratch_shapes=scratch,
        ),
        compiler_params=pltpu.CompilerParams(vmem_limit_bytes=VMEM_LIMIT),
        cost_estimate=LITTLE,
    )(turn, jnp.concatenate([first, own_row, other_row]), own, other, *pieces, *more)
    return turn_next, out


def spans_of(slot_ids, lengths):
    widths = bucket_lengths(slot_ids)
    starts = jnp.cumsum(widths) - widths
    return jnp.stack([starts, starts + lengths]).astype(jnp.int32)


def relay(hidden_acts, output_grads, query_left, query_right, bucket_ids, seq_lengths):
    count = lax.axis_size("dp")
    me, group = lax.axis_index("dp"), lax.axis_index("groups")
    z = me // 4
    local, ranks = query_left.shape[:2]
    left = query_left.reshape(local * ranks, -1)
    half = left.shape[1] // 2
    send = functools.partial(flip, count=count)

    acts_there = send(hidden_acts, CORE)
    spans_here = spans_of(bucket_ids, seq_lengths)
    spans = jnp.concatenate([spans_here, send(spans_here, CORE)], axis=1)

    a, b, c = {}, {}, {}
    a["own"] = lax.dynamic_slice_in_dim(left, group * half, half, 1)
    b["own"] = query_right.reshape(local * ranks, -1)
    at_end = (z == 0) | (z == 3)

    def near(piece):
        return send(piece, NEAR)

    def middle(piece):
        return lines(piece, [(1, 2), (2, 1)])

    def ends(piece):
        return lines(piece, [(0, 3), (3, 0)])

    def across(piece):
        return send(piece, ACROSS)

    def over_x(piece):
        return send(piece, COLUMN)

    inside = (~at_end).reshape(1).astype(jnp.int32)
    mine = jnp.reshape(group, (1,)).astype(jnp.int32)
    zero = jnp.zeros((1,), jnp.int32)
    acts = ((hidden_acts, zero), (acts_there, zero))
    groups = (("own", "x", "n", "f"), ("xn", "xf", "o", "xo"))
    tokens_here = hidden_acts.shape[0]
    steps = 4

    def times_a(turn, k):
        return proj(turn, acts, tokens_here, [a[i] for i in groups[k]], mine, steps)

    def times_c(turn, k, *score):
        return proj(turn, acts, tokens_here, [c[i] for i in groups[k]], 1 - mine, steps, *score)

    def times_b(turn, k, *score):
        return proj(turn, grads, tokens_here, [b[i] for i in groups[k]], zero, steps, *score)

    def pause(turn):
        return after(turn, [], inside)[0]

    codes = (0, COLUMN, NEAR, ACROSS, NEAR | COLUMN, ACROSS | COLUMN, OPPOSITE, OPPOSITE | COLUMN)
    codes = jnp.array(codes, jnp.int32)
    owner = jnp.concatenate([me ^ codes, me ^ CORE ^ codes])
    query = owner[:, None] * local + jnp.arange(local, dtype=jnp.int32)[None, :]
    query = jnp.repeat(query.reshape(-1), ranks)
    placed = query[None, :] == jnp.arange(count * local, dtype=jnp.int32)[:, None]
    placed = placed.astype(jnp.float32)

    grads_there = send(output_grads, CORE)
    grads = ((output_grads, zero), (grads_there, zero))

    copies = (1 - mine, left, b["own"])
    a["x"] = over_x(a["own"])
    a["n"] = near(a["own"])
    a_mid = middle(a["own"])
    turn, (c["own"], b_one, b_two), _ = prepare(zero, zero + 1, *copies, None, [])

    turn, (a["x"], a["n"], a_mid, a["own"]) = after(
        turn, [a["x"], a["n"], a_mid, a["own"]], inside, None, [acts_there]
    )
    a_end = ends(a["own"])
    b["x"] = over_x(b_one)
    c["x"] = swap_groups(a["x"])
    turn = pause(turn)

    turn, (c["x"], b["x"], a["f"]) = after(turn, [c["x"], b["x"], a_end], inside, a_mid, [grads_there])
    a["o"] = near(a["f"])
    a["xn"] = over_x(a["n"])
    c["n"] = swap_groups(a["n"])
    b["f"] = across(b_one)
    turn = pause(turn)

    turn, (a["o"], a["xn"], c["n"], b_two) = after(turn, [a["o"], a["xn"], c["n"], b_two], inside)
    b["n"] = near(b_two)
    a["xf"] = over_x(a["f"])
    c["f"] = swap_groups(a["f"])
    turn, a_first = times_a(turn, 0)

    turn, (b["n"], a["xf"], c["f"], a["o"], a["xn"]) = after(
        turn, [b["n"], a["xf"], c["f"], a["o"], a["xn"]], inside
    )
    a["xo"] = over_x(a["o"])
    c["o"] = swap_groups(a["o"])
    c["xn"] = swap_groups(a["xn"])
    turn, c_first = times_c(turn, 0)

    turn, (b["f"], a["xo"], c["o"], a["xf"]) = after(turn, [b["f"], a["xo"], c["o"], a["xf"]], inside)
    b["o"] = near(b["f"])
    b["xf"] = over_x(b["f"])
    c["xf"] = swap_groups(a["xf"])
    turn, score_first = times_b(turn, 0, True, spans, (a_first, c_first))

    split = c["o"].shape[0] // 2
    turn, (b["o"], b["xf"], c["xn"], b_over, a["xo"], c["o"], placed) = after(
        turn, [b["o"], b["xf"], c["xn"], b["x"], a["xo"], c["o"], placed], inside
    )
    b["xo"] = over_x(b["o"])
    b["xn"] = near(b_over)
    c["top"] = over_x(c["o"][:split])
    c["low"] = swap_groups(a["xo"][split:])
    turn, a_second = times_a(turn, 1)

    turn, (b["xo"], c["xf"], b["xn"]) = after(turn, [b["xo"], c["xf"], b["xn"]], inside)
    turn, b_second = times_b(turn, 1)
    groups = (groups[0], ("xn", "xf", "o", "top", "low"))
    turn, score_second = times_c(turn, 1, False, spans, (a_second, b_second))
    sums = [score_first, score_second]

    slots = bucket_ids.shape[0]
    others = [send(x, CORE) for x in sums]
    held = [x[:slots] for x in sums] + [x[slots:] for x in others]
    return lax.dot_general(
        placed,
        jnp.concatenate(held, axis=1),
        (((1,), (1,)), ((), ())),
        precision=lax.Precision.HIGHEST,
        preferred_element_type=jnp.float32,
    )


def solution(mesh):
    sizes = mesh.shape
    fits = sizes["dp"] == 16 and sizes["groups"] == 2 and sizes["tensor"] == 1
    return jax.shard_map(
        relay if fits else gather_whole,
        mesh=mesh,
        in_specs=(
            P(("groups", "dp"), "tensor"),
            P(("groups", "dp"), "tensor"),
            P("dp", None, "tensor"),
            P("dp", None, "tensor"),
            P(("groups", "dp")),
            P(("groups", "dp")),
        ),
        out_specs=P("tensor", ("groups", "dp")),
        check_vma=False,
    )
```

```python
import functools

import jax
import jax.numpy as jnp
from jax import lax
from jax.experimental import pallas as pl
from jax.experimental.pallas import tpu as pltpu
from jax.sharding import PartitionSpec as P

BUCKET = 128


def bucket_lengths(slot_ids):
    return BUCKET * jnp.where(
        slot_ids == 0, 1, jnp.where(slot_ids == 1, 2, jnp.where(slot_ids == 2, 4, 0))
    ).astype(jnp.int32)


def slot_matrix(slot_ids, lengths, positions):
    widths = bucket_lengths(slot_ids)
    starts = jnp.cumsum(widths) - widths
    place = jnp.arange(positions, dtype=jnp.int32)[:, None]
    inside = (place >= starts[None, :]) & (place < starts[None, :] + lengths[None, :])
    return inside.astype(jnp.float32)


def project(acts, factors):
    rows = factors.reshape(-1, factors.shape[2])
    return lax.dot_general(acts, rows, (((1,), (1,)), ((), ())), preferred_element_type=jnp.float32)


def gather_whole(hidden_acts, output_grads, query_left, query_right, bucket_ids, seq_lengths):
    tokens_here = hidden_acts.shape[0]
    rank_count = query_left.shape[1]
    left_all, right_all = (
        lax.all_gather(query_left, "dp", axis=0, tiled=True),
        lax.all_gather(query_right, "dp", axis=0, tiled=True),
    )
    left_proj = project(hidden_acts, left_all)
    right_proj = project(output_grads, right_all)
    queries = left_proj.shape[1] // rank_count
    left_terms = left_proj.reshape(tokens_here, queries, rank_count)
    right_terms = right_proj.reshape(tokens_here, queries, rank_count)
    left_terms, right_terms = lax.psum((left_terms, right_terms), "tensor")
    share_size = queries // lax.axis_size("tensor")
    first_query = lax.axis_index("tensor") * share_size
    left_terms = lax.dynamic_slice_in_dim(left_terms, first_query, share_size, 1)
    right_terms = lax.dynamic_slice_in_dim(right_terms, first_query, share_size, 1)
    token_term = jnp.sum(left_terms * right_terms, axis=2)
    slot_mask = slot_matrix(bucket_ids, seq_lengths, tokens_here)
    return jnp.dot(
        token_term.T, slot_mask, precision=lax.Precision.HIGHEST, preferred_element_type=jnp.float32
    )


CORE, COLUMN, NEAR, ACROSS, OPPOSITE = 1, 2, 4, 12, 8
LITTLE = pl.CostEstimate(flops=1, bytes_accessed=1, transcendentals=0)
VMEM_LIMIT = 255 * 256 * 1024


def flip(array, code, count):
    return lax.ppermute(array, "dp", [(i, i ^ code) for i in range(count)])


def swap_groups(array):
    return lax.ppermute(array, "groups", [(0, 1), (1, 0)])


PARTS = 4


def through(held, arrived, gone, source, target):
    rows = source.shape[0] // PARTS
    parts = [pl.ds(i * rows, rows) for i in range(PARTS)]
    come = [pltpu.make_async_copy(source.at[p], held.at[p], arrived.at[i]) for i, p in enumerate(parts)]
    go = [pltpu.make_async_copy(held.at[p], target.at[p], gone.at[i]) for i, p in enumerate(parts)]
    for copy in come:
        copy.start()
    for first, second in zip(come, go):
        first.wait()
        second.start()
    for copy in go:
        copy.wait()


def after_kernel(count, merges, inside_ref, turn_ref, *refs):
    if merges:
        refs, staging = refs[:-3], refs[-3:]
        source, target = refs[0], refs[-1 - count]

        @pl.when(inside_ref[0] == 1)
        def _():
            through(*staging, source, target)

    refs[-1][0] = turn_ref[0]


def after(turn, arrays, inside, merge=None, there=()):
    count = len(arrays)
    scratch = []
    if merge is not None:
        there = (merge, *there)
        scratch = [pltpu.VMEM(merge.shape, merge.dtype)] + [pltpu.SemaphoreType.DMA((PARTS,))] * 2
    hbm = pl.BlockSpec(memory_space=pltpu.HBM)
    scalar = pl.BlockSpec(memory_space=pltpu.SMEM)
    *arrays, turn = pl.pallas_call(
        functools.partial(after_kernel, count, merge is not None),
        out_shape=[jax.ShapeDtypeStruct(x.shape, x.dtype) for x in (*arrays, turn)],
        in_specs=[scalar] * 2 + [hbm] * (len(there) + count),
        out_specs=[hbm] * count + [scalar],
        input_output_aliases={2 + len(there) + i: i for i in range(count)},
        scratch_shapes=scratch,
        compiler_params=pltpu.CompilerParams(vmem_limit_bytes=VMEM_LIMIT),
        cost_estimate=LITTLE,
    )(inside, turn, *there, *arrays)
    return turn, arrays


def prepare_kernel(works_ref, turn_ref, first_ref, left_ref, right_ref, *refs):
    half_ref, one_ref, two_ref, next_ref, half_held, right_held, arrived, gone = refs[-8:]
    next_ref[0] = turn_ref[0]
    width = half_ref.shape[1]

    @pl.when(works_ref[0] == 1)
    def _():
        start = pl.multiple_of(first_ref[0] * width, width)
        through(half_held, arrived, gone, left_ref.at[:, pl.ds(start, width)], half_ref)
        for target in (one_ref, two_ref):
            through(right_held, arrived, gone, right_ref, target)


def prepare(turn, works, first, left, right, made, passed):
    rows, width = left.shape[0], left.shape[1] // 2
    shapes = [(rows, width), right.shape, right.shape]
    out_shape = [jax.ShapeDtypeStruct(x, left.dtype) for x in shapes]
    made = () if made is None else made
    given = (*passed, *made)
    hbm = pl.BlockSpec(memory_space=pltpu.HBM)
    scalar = pl.BlockSpec(memory_space=pltpu.SMEM)
    aliases = {5 + i: i for i in range(len(given))}
    outs = pl.pallas_call(
        prepare_kernel,
        out_shape=[jax.ShapeDtypeStruct(x.shape, x.dtype) for x in passed]
        + out_shape
        + [jax.ShapeDtypeStruct(turn.shape, turn.dtype)],
        in_specs=[scalar] * 3 + [hbm] * (2 + len(given)),
        out_specs=[hbm] * (len(passed) + 3) + [scalar],
        input_output_aliases=aliases,
        scratch_shapes=[pltpu.VMEM((rows, width), left.dtype), pltpu.VMEM(right.shape, right.dtype)]
        + [pltpu.SemaphoreType.DMA((PARTS,))] * 2,
        compiler_params=pltpu.CompilerParams(vmem_limit_bytes=VMEM_LIMIT),
        cost_estimate=LITTLE,
    )(works, turn, first, left, right, *given)
    return outs[-1], outs[len(passed) : -1], outs[: len(passed)]


def lines(array, pairs):
    return lax.ppermute(
        array, "dp", [(a * 4 + rest, b * 4 + rest) for a, b in pairs for rest in range(4)]
    )


def score_into(out_ref, spans_ref, terms_of, rows):
    slots = out_ref.shape[0] // 2
    place = lax.broadcasted_iota(jnp.int32, (rows, 1), 0)
    for part in range(2):
        terms = terms_of(slice(part * rows, (part + 1) * rows))
        for j in range(slots):
            k = part * slots + j
            inside = (place >= spans_ref[0, k]) & (place < spans_ref[1, k])
            out_ref[k : k + 1, :] = jnp.sum(jnp.where(inside, terms, 0.0), axis=0, keepdims=True)


def proj_kernel(count, last, turn_ref, at_ref, own_ref, other_ref, *refs):
    del at_ref
    pieces, refs = refs[:count], refs[count:]
    if last is None:
        acc_ref, next_ref = refs
    else:
        spans_ref, left_ref, second_ref, out_ref, next_ref, acc_ref = refs
    step = pl.program_id(0)
    rows = own_ref.shape[0]

    @pl.when(step == 0)
    def _():
        next_ref[0] = turn_ref[0]
        acc_ref[...] = jnp.zeros_like(acc_ref)

    factors = jnp.concatenate([p[...] for p in pieces], axis=0)
    for part, tokens in enumerate((own_ref, other_ref)):
        acc_ref[part * rows : (part + 1) * rows] += lax.dot_general(
            tokens[...], factors, (((1,), (1,)), ((), ())), preferred_element_type=jnp.float32
        )

    if last is not None:

        @pl.when(step == pl.num_programs(0) - 1)
        def _():
            def terms(here):
                if last:
                    return (left_ref[here] + second_ref[here]) * acc_ref[here]
                return (left_ref[here] + acc_ref[here]) * second_ref[here]

            score_into(out_ref, spans_ref, terms, rows)


def proj(turn, tokens, rows, pieces, first, steps, last=None, spans=None, others=()):
    depth = pieces[0].shape[1]
    block = depth // steps
    held = sum(p.shape[0] for p in pieces)
    (own, own_row), (other, other_row) = tokens
    whole = pl.BlockSpec((2 * rows, held), lambda k, turn, at: (0, 0))
    scalar = pl.BlockSpec(memory_space=pltpu.SMEM)
    if last is None:
        more_specs, more, scratch = [], (), []
        out_shape, out_spec = (2 * rows, held), whole
    else:
        more_specs, more = [scalar, whole, whole], (spans, *others)
        scratch = [pltpu.VMEM((2 * rows, held), jnp.float32)]
        out_shape = (spans.shape[1], held)
        out_spec = pl.BlockSpec(out_shape, lambda k, turn, at: (0, 0))
    out, turn_next = pl.pallas_call(
        functools.partial(proj_kernel, len(pieces), last),
        out_shape=(
            jax.ShapeDtypeStruct(out_shape, jnp.float32),
            jax.ShapeDtypeStruct((1,), jnp.int32),
        ),
        grid_spec=pltpu.PrefetchScalarGridSpec(
            num_scalar_prefetch=2,
            grid=(steps,),
            in_specs=[
                pl.BlockSpec((rows, block), lambda k, turn, at: (at[1], at[0] * steps + k)),
                pl.BlockSpec((rows, block), lambda k, turn, at: (at[2], at[0] * steps + k)),
            ]
            + [pl.BlockSpec((p.shape[0], block), lambda k, turn, at: (0, k)) for p in pieces]
            + more_specs,
            out_specs=(out_spec, scalar),
            scratch_shapes=scratch,
        ),
        compiler_params=pltpu.CompilerParams(vmem_limit_bytes=VMEM_LIMIT),
        cost_estimate=LITTLE,
    )(turn, jnp.concatenate([first, own_row, other_row]), own, other, *pieces, *more)
    return turn_next, out


def spans_of(slot_ids, lengths):
    widths = bucket_lengths(slot_ids)
    starts = jnp.cumsum(widths) - widths
    return jnp.stack([starts, starts + lengths]).astype(jnp.int32)


def relay(hidden_acts, output_grads, query_left, query_right, bucket_ids, seq_lengths):
    count = lax.axis_size("dp")
    me, group = lax.axis_index("dp"), lax.axis_index("groups")
    z = me // 4
    local, ranks = query_left.shape[:2]
    left = query_left.reshape(local * ranks, -1)
    half = left.shape[1] // 2
    send = functools.partial(flip, count=count)

    acts_there = send(hidden_acts, CORE)
    spans_here = spans_of(bucket_ids, seq_lengths)
    spans = jnp.concatenate([spans_here, send(spans_here, CORE)], axis=1)

    a, b, c = {}, {}, {}
    a["own"] = lax.dynamic_slice_in_dim(left, group * half, half, 1)
    b["own"] = query_right.reshape(local * ranks, -1)
    at_end = (z == 0) | (z == 3)

    def near(piece):
        return send(piece, NEAR)

    def middle(piece):
        return lines(piece, [(1, 2), (2, 1)])

    def ends(piece):
        return lines(piece, [(0, 3), (3, 0)])

    def across(piece):
        return send(piece, ACROSS)

    def over_x(piece):
        return send(piece, COLUMN)

    inside = (~at_end).reshape(1).astype(jnp.int32)
    mine = jnp.reshape(group, (1,)).astype(jnp.int32)
    zero = jnp.zeros((1,), jnp.int32)
    acts = ((hidden_acts, zero), (acts_there, zero))
    groups = (("own", "x", "n", "f"), ("xn", "xf", "o", "xo"))
    tokens_here = hidden_acts.shape[0]
    steps = 4

    def times_a(turn, k):
        return proj(turn, acts, tokens_here, [a[i] for i in groups[k]], mine, steps)

    def times_c(turn, k, *score):
        return proj(turn, acts, tokens_here, [c[i] for i in groups[k]], 1 - mine, steps, *score)

    def times_b(turn, k, *score):
        return proj(turn, grads, tokens_here, [b[i] for i in groups[k]], zero, steps, *score)

    def pause(turn):
        return after(turn, [], inside)[0]

    codes = (0, COLUMN, NEAR, ACROSS, NEAR | COLUMN, ACROSS | COLUMN, OPPOSITE, OPPOSITE | COLUMN)
    codes = jnp.array(codes, jnp.int32)
    owner = jnp.concatenate([me ^ codes, me ^ CORE ^ codes])
    query = owner[:, None] * local + jnp.arange(local, dtype=jnp.int32)[None, :]
    query = jnp.repeat(query.reshape(-1), ranks)
    placed = query[None, :] == jnp.arange(count * local, dtype=jnp.int32)[:, None]
    placed = placed.astype(jnp.float32)

    grads_there = send(output_grads, CORE)
    grads = ((output_grads, zero), (grads_there, zero))

    copies = (1 - mine, left, b["own"])
    a["x"] = over_x(a["own"])
    a["n"] = near(a["own"])
    a_mid = middle(a["own"])
    turn, (c["own"], b_one, b_two), _ = prepare(zero, zero + 1, *copies, None, [])

    turn, (a["x"], a["n"], a_mid, a["own"]) = after(
        turn, [a["x"], a["n"], a_mid, a["own"]], inside, None, [acts_there]
    )
    a_end = ends(a["own"])
    b["x"] = over_x(b_one)
    c["x"] = swap_groups(a["x"])
    turn = pause(turn)

    turn, (a["f"], b["x"], c["x"]) = after(turn, [a_end, b["x"], c["x"]], inside, a_mid, [grads_there])
    a["o"] = near(a["f"])
    a["xn"] = over_x(a["n"])
    c["n"] = swap_groups(a["n"])
    b["f"] = across(b_one)
    turn = pause(turn)

    turn, (a["o"], a["xn"], c["n"], b_two) = after(turn, [a["o"], a["xn"], c["n"], b_two], inside)
    b["n"] = near(b_two)
    a["xf"] = over_x(a["f"])
    c["f"] = swap_groups(a["f"])
    turn, a_first = times_a(turn, 0)

    turn, (b["n"], a["xf"], c["f"], a["o"], a["xn"]) = after(
        turn, [b["n"], a["xf"], c["f"], a["o"], a["xn"]], inside
    )
    a["xo"] = over_x(a["o"])
    c["o"] = swap_groups(a["o"])
    c["xn"] = swap_groups(a["xn"])
    turn, c_first = times_c(turn, 0)

    turn, (b["f"], a["xo"], c["o"], a["xf"]) = after(turn, [b["f"], a["xo"], c["o"], a["xf"]], inside)
    b["o"] = near(b["f"])
    b["xf"] = over_x(b["f"])
    c["xf"] = swap_groups(a["xf"])
    turn, score_first = times_b(turn, 0, True, spans, (a_first, c_first))

    split = c["o"].shape[0] // 2
    turn, (b["o"], b["xf"], c["xn"], b_over, a["xo"], c["o"], placed) = after(
        turn, [b["o"], b["xf"], c["xn"], b["x"], a["xo"], c["o"], placed], inside
    )
    b["xo"] = over_x(b["o"])
    b["xn"] = near(b_over)
    c["top"] = over_x(c["o"][:split])
    c["low"] = swap_groups(a["xo"][split:])
    turn, a_second = times_a(turn, 1)

    turn, (b["xo"], b["xn"]) = after(turn, [b["xo"], b["xn"]], inside)
    turn, b_second = times_b(turn, 1)
    groups = (groups[0], ("xn", "xf", "o", "top", "low"))
    turn, score_second = times_c(turn, 1, False, spans, (a_second, b_second))
    sums = [score_first, score_second]

    slots = bucket_ids.shape[0]
    others = [send(x, CORE) for x in sums]
    held = [x[:slots] for x in sums] + [x[slots:] for x in others]
    return lax.dot_general(
        placed,
        jnp.concatenate(held, axis=1),
        (((1,), (1,)), ((), ())),
        precision=lax.Precision.HIGHEST,
        preferred_element_type=jnp.float32,
    )


def solution(mesh):
    sizes = mesh.shape
    fits = sizes["dp"] == 16 and sizes["groups"] == 2 and sizes["tensor"] == 1
    return jax.shard_map(
        relay if fits else gather_whole,
        mesh=mesh,
        in_specs=(
            P(("groups", "dp"), "tensor"),
            P(("groups", "dp"), "tensor"),
            P("dp", None, "tensor"),
            P("dp", None, "tensor"),
            P(("groups", "dp")),
            P(("groups", "dp")),
        ),
        out_specs=P("tensor", ("groups", "dp")),
        check_vma=False,
    )
```
